128 devices in a mesh: dp: 8 (over z_lo, y), ep: 16 (over x, z_hi, core).
Axes of the slice: x: 4, y: 4, z: 4 (z_hi: 2, z_lo: 2; z = z_hi * 2 + z_lo), core: 2. Of those that a mesh axis runs over, the one named last changes fastest.
Arguments:
- queries: bfloat16 [512, 36864], P('dp', 'ep'), may hold values from -60 to 60
- cache_latent: bfloat16 [512, 80, 512], P('dp'), may hold values from -6 to 6
- cache_rope: bfloat16 [512, 80, 64], P('dp'), may hold values from -6 to 6
- cache_len: int32 [512], P('dp'), may hold values from 1 to 80, as said below
- move_plan: int32 [512], replicated, may hold values from 0 to 511, as said below
- w_absorb: bfloat16 [64, 512, 128], P('ep'), may hold values from -0.25 to 0.25
- w_out: bfloat16 [8192, 7168], P('ep'), may hold values from -0.0625 to 0.0625
- norm_gain: float32 [7168], replicated, may hold values from 0.1 to 1.9
- router: bfloat16 [7168, 16], replicated, may hold values from -0.0625 to 0.0625
- routes: int32 [512, 8], P('dp'), may hold values from 0 to 15, all different within a row; in each aligned block of 64 rows (0 to 63, 64 to 127, ...) at most 40 rows name the same one
- w_gate: bfloat16 [16, 7168, 2048], P('ep', None, 'dp'), may hold values from -0.0625 to 0.0625
- w_up: bfloat16 [16, 7168, 2048], P('ep', None, 'dp'), may hold values from -0.0625 to 0.0625
- w_down: bfloat16 [16, 2048, 7168], P('ep', 'dp'), may hold values from -0.125 to 0.125
Outputs:
- attended: bfloat16 [512, 7168], P('dp')
- expert_mix: bfloat16 [512, 7168], P(('dp', 'ep'))
The draws below stay inside these ranges and needn't reach their ends.
Inputs may be any that keep to these rules, and one draw needn't show every extreme that they name: `cache_len`: some request has all 80 positions filled and some only one. `move_plan`: A permutation of the slots. The dp ranks fall into two halves of 4 ranks; each rank of one half swaps exactly 2 requests with each rank of the other half; every other request keeps its slot. `routes`: in the 64 rows of one dp rank no expert is named by more than 40 rows, a bound that some block reaches.
All inputs are finite; a program needn't handle non-finite values.
Results may differ from the reference program's by a relative error of at most 0.035.
Values may be sent and summed in bfloat16 or wider, within the bound.
A program may use at most 128 MiB of HBM per device.

```python
import math
import jax
import jax.numpy as jnp
import numpy as np
from jax import lax

D = 7168
FF = 2048
LAT = 512
ROPE = 64
VDIM = 128
TOPK = 8
MIGP = 2
SLOTS = 64
CAP = 80
HEADS = 64
EXPERTS = 16
ROWS_ALL = 512
CAPX = 40
N_DP = 8


def load_layout(key):
    rank_order = jax.random.permutation(jax.random.fold_in(key, 1), N_DP)
    heavy_flag = jnp.zeros((N_DP,), jnp.int32).at[rank_order[:N_DP // 2]].set(1)
    slot_keys = jax.random.split(jax.random.fold_in(key, 2), N_DP)
    slot_order = jax.vmap(lambda sub_key: jax.random.permutation(sub_key, SLOTS))(slot_keys)
    return (rank_order, heavy_flag, slot_order)


def draw_cache_len(key, part):
    rank_order, heavy_flag, slot_order = load_layout(key)
    key = jax.random.fold_in(key, 3)
    long_len = jax.random.randint(jax.random.fold_in(key, 4), (N_DP, SLOTS), CAP // 2, CAP + 1)
    short_len = jax.random.randint(jax.random.fold_in(key, 5), (N_DP, SLOTS), 1, CAP // 4 + 1)
    lengths = jnp.where(heavy_flag[:, None] == 1, long_len, short_len)
    lengths = lengths.at[rank_order[0], 0].set(CAP)
    lengths = lengths.at[rank_order[N_DP - 1], 0].set(1)
    return lengths.reshape(-1).astype(jnp.int32)


def draw_move_plan(key, part):
    rank_order, heavy_flag, slot_order = load_layout(key)
    half_count = N_DP // 2
    shape_three = (half_count, half_count, MIGP)
    heavy_idx = jnp.broadcast_to(jnp.arange(half_count)[:, None, None], shape_three)
    light_idx = jnp.broadcast_to(jnp.arange(half_count)[None, :, None], shape_three)
    mail_idx = jnp.broadcast_to(jnp.arange(MIGP)[None, None, :], shape_three)
    heavy_rank = rank_order[heavy_idx]
    light_rank = rank_order[half_count + light_idx]
    heavy_slot = slot_order[heavy_rank, light_idx * MIGP + mail_idx]
    light_slot = slot_order[light_rank, heavy_idx * MIGP + mail_idx]
    heavy_global = (heavy_rank * SLOTS + heavy_slot).reshape(-1)
    light_global = (light_rank * SLOTS + light_slot).reshape(-1)
    plan_table = jnp.arange(N_DP * SLOTS, dtype=jnp.int32)
    plan_table = plan_table.at[heavy_global].set(light_global)
    plan_table = plan_table.at[light_global].set(heavy_global)
    return plan_table.astype(jnp.int32)


def draw_queries(key, part):
    key = jax.random.fold_in(key, 11)
    shape_two = (N_DP * SLOTS, HEADS * (LAT + ROPE))
    normal_part = jax.random.normal(jax.random.fold_in(key, 14), shape_two, jnp.float32)
    return jnp.clip(normal_part, -6.0, 6.0).astype(jnp.bfloat16)


def steps_of(own_key, dims, shards, least, top_value):
    loudness = 1.0
    for dim, parts in shards:
        heights = jax.random.uniform(jax.random.fold_in(jax.random.fold_in(own_key, 6), dim), (parts,), jnp.float32, least / len(shards), top_value / len(shards))
        loudness = loudness * jnp.repeat(jnp.exp(heights), dims[dim] // parts).reshape((-1,) + (1,) * (len(dims) - 1 - dim))
    return loudness


def assign_block(stream_key, own, number, rows, number_of, top, reach, slope):
    order = jax.random.permutation(stream_key, number_of)
    crowded, usual = shares(number_of, rows * top, reach, slope, True), shares(number_of, rows * top, reach, slope, False)
    places = jnp.arange(number_of)

    def named(sizes, turn):
        used = int((sizes > 0).sum())
        fixed = max(1, used // 4)
        moved = fixed + (places - fixed + turn * (used - fixed)) % max(1, number_of - fixed)
        return jnp.zeros((number_of,), jnp.int32).at[order[jnp.where(places < fixed, places, moved)]].set(jnp.asarray(sizes, jnp.int32))

    sizes = jnp.where(number % 4 == 0, named(crowded, number // 4), named(usual, number - number // 4 - 1))
    mixed = jax.random.permutation(jax.random.fold_in(own, 3), number_of)
    giver, taker = mixed[0:number_of // 2 * 2:2], mixed[1:number_of // 2 * 2:2]
    slack = jnp.minimum(sizes[giver] - 1, reach - sizes[taker]) // 2
    slack = jnp.where((giver == order[0]) | (taker == order[0]) | (sizes[taker] == 0), 0, jnp.maximum(slack, 0))
    moved = jax.random.randint(jax.random.fold_in(own, 4), (number_of // 2,), 0, 1 << 20) % (slack + 1)
    sizes = sizes.at[giver].add(-moved).at[taker].add(moved)
    labels = jnp.searchsorted(jnp.cumsum(sizes), jnp.arange(rows * top), side="right").astype(jnp.int32)
    listing = labels.reshape(top, rows).T
    listing = listing[jax.random.permutation(jax.random.fold_in(own, 1), rows)]
    turn = jax.random.randint(jax.random.fold_in(own, 2), (rows, 1), 0, top)
    return jnp.take_along_axis(listing, (jnp.arange(top)[None, :] + turn) % top, axis=1)


def shares(amount, total, most, lean, full):
    weights = [(1 << 20) // math.isqrt(grade ** lean) + 1 for grade in range(1, amount + 1)]
    largest = most if full else min(most, max(-(-total // amount), total * weights[0] // sum(weights)))
    least = 1 if total - largest >= amount - 1 else 0
    counts, rest = [largest] + [least] * (amount - 1), total - largest - least * (amount - 1)
    while rest > 0:
        movable = [i for i in range(1, amount) if counts[i] < largest] or [i for i in range(1, amount) if counts[i] < most]
        whole, remaining = sum([weights[i] for i in movable]), rest
        for i in movable:
            extra = min(most - counts[i], max(1, remaining * weights[i] // whole), rest)
            counts[i] = counts[i] + extra
            rest = rest - extra
    return np.array(counts)


def normal_values(rng, dims, spread, most, cuts=(), held_as=jnp.bfloat16):
    entries = spread * jax.random.normal(rng, dims, jnp.float32)
    if cuts:
        entries = entries * steps_of(rng, dims, cuts, -0.22, 0.18)
    return jnp.clip(entries, -most, most).astype(held_as)


def setup_inputs(seed: int = 0) -> dict:
    seeds = jax.random.split(jax.random.key(seed), 14)
    queries = draw_queries(jax.random.fold_in(seeds[13], 71), 0)
    cache_latent = normal_values(seeds[1], (ROWS_ALL, CAP, LAT), 1.0, 6.0, ((0, 8),))
    cache_rope = normal_values(seeds[2], (ROWS_ALL, CAP, ROPE), 1.0, 6.0, ((0, 8),))
    cache_len = draw_cache_len(jax.random.fold_in(seeds[13], 71), 0)
    move_plan = draw_move_plan(jax.random.fold_in(seeds[13], 71), 0)
    w_absorb = normal_values(seeds[5], (HEADS, LAT, VDIM), LAT ** -0.5, 0.25, ((0, 16),))
    w_out = normal_values(seeds[6], (HEADS * VDIM, D), (HEADS * VDIM) ** -0.5, 0.0625, ((0, 16),))
    norm_gain = jnp.clip(1.0 + 0.18 * jax.random.normal(seeds[7], (D,), jnp.float32), 0.1, 1.9)
    router = normal_values(seeds[8], (D, EXPERTS), D ** -0.5, 0.0625)
    routes_keys = jax.random.split(jax.random.fold_in(seeds[9], 1), ROWS_ALL // SLOTS)
    routes_turns = jax.random.permutation(jax.random.fold_in(seeds[9], 3), ROWS_ALL // SLOTS)
    routes = jax.vmap(lambda own, number: assign_block(jax.random.fold_in(seeds[9], 2), own, number, SLOTS, EXPERTS, TOPK, CAPX, 0))(routes_keys, routes_turns).reshape((ROWS_ALL, TOPK))
    w_gate = normal_values(seeds[10], (EXPERTS, D, FF), D ** -0.5, 0.0625, ((0, 16), (2, 8)))
    w_up = normal_values(seeds[11], (EXPERTS, D, FF), D ** -0.5, 0.0625, ((0, 16), (2, 8)))
    w_down = normal_values(seeds[12], (EXPERTS, FF, D), FF ** -0.5, 0.125, ((0, 16), (1, 8)))
    return dict(queries=queries, cache_latent=cache_latent, cache_rope=cache_rope, cache_len=cache_len, move_plan=move_plan, w_absorb=w_absorb, w_out=w_out, norm_gain=norm_gain, router=router, routes=routes, w_gate=w_gate, w_up=w_up, w_down=w_down)


epsilon = 1e-06
route_scale = 2.5

def reference(queries, cache_latent, cache_rope, cache_len, move_plan, w_absorb, w_out, norm_gain, router, routes, w_gate, w_up, w_down):
    score_scale = (VDIM + ROPE) ** (-0.5)
    positions = jnp.arange(CAP, dtype=jnp.int32)

    def attend_row(operands):
        query_row, source = operands
        latent = cache_latent[source].astype(jnp.float32)
        rope_keys = cache_rope[source].astype(jnp.float32)
        length = cache_len[source]
        shaped = query_row.reshape(HEADS, LAT + ROPE).astype(jnp.float32)
        scores = jnp.einsum('hl,tl->ht', shaped[:, :LAT], latent) + jnp.einsum('hr,tr->ht', shaped[:, LAT:], rope_keys)
        scores = scores * score_scale
        scores = jnp.where((positions < length)[None, :], scores, -jnp.inf)
        scores = scores - lax.optimization_barrier(jnp.max(scores, axis=1, keepdims=True))
        expsum = jnp.exp(scores)
        weights_soft = (expsum / lax.optimization_barrier(jnp.sum(expsum, axis=1, keepdims=True))).astype(jnp.bfloat16)
        return jnp.einsum('ht,tl->hl', weights_soft.astype(jnp.float32), latent).astype(jnp.bfloat16)
    latent_out = lax.map(attend_row, (queries, move_plan))
    values = jnp.einsum('rhl,hlv->rhv', latent_out.astype(jnp.float32), w_absorb.astype(jnp.float32)).astype(jnp.bfloat16)
    hidden_sum = jnp.dot(values.reshape(ROWS_ALL, HEADS * VDIM), w_out, preferred_element_type=jnp.float32)
    attended = hidden_sum.astype(jnp.bfloat16)
    meansq = lax.optimization_barrier(jnp.mean(hidden_sum * hidden_sum, axis=1, keepdims=True))
    normed = (hidden_sum * lax.rsqrt(meansq + epsilon) * norm_gain).astype(jnp.bfloat16)
    affinity = jax.nn.sigmoid(jnp.dot(normed, router, preferred_element_type=jnp.float32))
    chosen = jnp.take_along_axis(affinity, routes, axis=1)
    route_weight = route_scale * chosen / lax.optimization_barrier(jnp.sum(chosen, axis=1, keepdims=True))

    def add_expert(expert, running):
        gate_act = jnp.dot(normed, w_gate[expert], preferred_element_type=jnp.float32)
        up_act = jnp.dot(normed, w_up[expert], preferred_element_type=jnp.float32)
        hidden = (jax.nn.silu(gate_act) * up_act).astype(jnp.bfloat16)
        outputs = jnp.dot(hidden, w_down[expert], preferred_element_type=jnp.float32)
        coefficient = lax.optimization_barrier(jnp.sum(jnp.where(routes == expert, route_weight, 0.0), axis=1))
        return running + coefficient[:, None] * outputs
    mixture = lax.fori_loop(0, EXPERTS, add_expert, jnp.zeros((ROWS_ALL, D), jnp.float32))
    return (attended, mixture.astype(jnp.bfloat16))
```

```python
import jax
import jax.numpy as jnp
from jax import lax
from jax.experimental import pallas as pl
from jax.experimental.pallas import tpu as pltpu
from jax.sharding import PartitionSpec as P

ROPE = 64
VDIM = 128
MIGP = 2


epsilon = 1e-06
route_scale = 2.5


def move_caches(cache_latent, cache_rope, cache_len, move_plan):
    rank_count = lax.axis_size("dp")
    slot_count = cache_len.shape[0]
    myself = lax.axis_index("dp")
    plan_table = move_plan.reshape(rank_count, slot_count)
    source_rank = plan_table // slot_count
    source_slot = plan_table % slot_count
    others = jnp.arange(rank_count, dtype=jnp.int32)[:, None] != myself
    outgoing = (source_rank == myself) & others
    mailbox = jnp.cumsum(outgoing.astype(jnp.int32), axis=1) - 1
    letters = jnp.arange(MIGP, dtype=jnp.int32)
    chosen = outgoing[:, :, None] & (mailbox[:, :, None] == letters[None, None, :])
    send_slot = jnp.sum(jnp.where(chosen, source_slot[:, :, None], 0), axis=1)
    packed = (
        cache_latent[send_slot],
        cache_rope[send_slot],
        cache_len[send_slot].astype(jnp.bfloat16),
    )
    got_latent, got_rope, got_length = (
        lax.all_to_all(packed[0], "dp", split_axis=0, concat_axis=0, tiled=True),
        lax.all_to_all(packed[1], "dp", split_axis=0, concat_axis=0, tiled=True),
        lax.all_to_all(packed[2], "dp", split_axis=0, concat_axis=0, tiled=True),
    )
    own_rank = lax.dynamic_index_in_dim(source_rank, myself, 0, keepdims=False)
    own_slot = lax.dynamic_index_in_dim(source_slot, myself, 0, keepdims=False)
    incoming = own_rank != myself
    position = jnp.arange(slot_count, dtype=jnp.int32)
    earlier = (own_rank[:, None] == own_rank[None, :]) & (position[None, :] < position[:, None])
    letter = jnp.sum(earlier.astype(jnp.int32), axis=1)
    pool_index = jnp.where(incoming, slot_count + own_rank * MIGP + letter, own_slot)
    latent_pool = jnp.concatenate(
        [cache_latent, got_latent.reshape((-1,) + cache_latent.shape[1:])], 0
    )
    rope_pool = jnp.concatenate([cache_rope, got_rope.reshape((-1,) + cache_rope.shape[1:])], 0)
    length_pool = jnp.concatenate([cache_len, got_length.reshape(-1).astype(jnp.int32)], 0)
    return (latent_pool[pool_index], rope_pool[pool_index], length_pool[pool_index])


def attend(queries, latent, rope_keys, lengths, w_absorb):
    slot_count = latent.shape[0]
    head_count = w_absorb.shape[0]
    latent_width = latent.shape[2]
    score_scale = (VDIM + ROPE) ** (-0.5)
    shaped = queries.reshape(slot_count, head_count, -1)
    scores = jnp.einsum(
        "shl,stl->sht", shaped[:, :, :latent_width], latent, preferred_element_type=jnp.float32
    )
    scores = scores + jnp.einsum(
        "shr,str->sht", shaped[:, :, latent_width:], rope_keys, preferred_element_type=jnp.float32
    )
    scores = scores * score_scale
    positions = jnp.arange(latent.shape[1], dtype=jnp.int32)
    scores = jnp.where(positions[None, None, :] < lengths[:, None, None], scores, -jnp.inf)
    scores = scores - jnp.max(scores, axis=2, keepdims=True)
    expsum = jnp.exp(scores)
    weights_soft = (expsum / jnp.sum(expsum, axis=2, keepdims=True)).astype(jnp.bfloat16)
    latent_out = jnp.einsum(
        "sht,stl->shl", weights_soft, latent, preferred_element_type=jnp.float32
    ).astype(jnp.bfloat16)
    values = jnp.einsum(
        "shl,hlv->shv", latent_out, w_absorb, preferred_element_type=jnp.float32
    ).astype(jnp.bfloat16)
    return values.reshape(slot_count, -1)


MESH = pl.DeviceIdType.MESH
AXES = ("x", "z", "y")
ORDERS = (("y", "z", "x"), ("z", "x", "y"), ("x", "y", "z"))


def coordinates():
    dp, ep = lax.axis_index("dp"), lax.axis_index("ep")
    me = {"x": ep // 4, "z": (ep // 2) % 2 * 2 + dp // 4, "y": dp % 4}
    return me, ep % 2


def device(at, core):
    return ((at["z"] % 2) * 4 + at["y"], at["x"] * 4 + at["z"] // 2 * 2 + core)


def moved(me, axis, offset):
    return {**me, axis: (me[axis] + offset) % 4}


def pick(ref, where, tail=(), axes=AXES):
    return ref.at[tuple(where.get(a, slice(None)) for a in axes) + tuple(tail)]


class Copies:
    def __init__(self, send, recv):
        self.send, self.recv, self.used, self.sent = send, recv, 0, []

    def start(self, src, dst, to):
        copy = pltpu.make_async_remote_copy(
            src_ref=src,
            dst_ref=dst,
            send_sem=self.send.at[self.used],
            recv_sem=self.recv.at[self.used],
            device_id=to,
            device_id_type=MESH,
        )
        copy.start()
        self.used += 1
        self.sent.append(copy)
        return copy

    def finish(self):
        for copy in self.sent:
            copy.wait_send()


def experts_kernel(
    values,
    routes,
    gain,
    w_out,
    router,
    w_gate,
    w_up,
    w_down,
    attended,
    mixed,
    wo,
    wr,
    wg,
    wu,
    wd,
    terms,
    core_terms,
    slab_terms,
    tokens,
    gate_sum,
    up_sum,
    score_sum,
    square_sum,
    act,
    partial,
    core_partial,
    far_parts,
    near_parts,
    sums_two,
    parts_two,
    sums_three,
    parts_three,
    final_half,
    load_sem,
    send_sem,
    recv_sem,
):
    me, core = coordinates()
    other = 1 - core
    sibling = device(me, other)
    copies = Copies(send_sem, recv_sem)
    width = wg.shape[1]
    slots = values.shape[0]
    half = slots // 2
    tiles = width // 128
    wide = (tiles * 5 + 6) // 7 * 128
    piece_rows = ((0, half // 2), (half // 2, half // 2), (0, half))
    piece_cols = ((0, wide), (0, wide), (wide, width - wide))
    unit_cols = partial.shape[-1]
    share = (unit_cols // 128 * 5 + 6) // 14 * 128
    out_cols = ((0, share), (share, share), (2 * share, unit_cols - 2 * share))

    slab_offsets = [(dx, dz) for dx in range(4) for dz in range(2) if (dx, dz) != (0, 0)]

    def slab_chip(dx, dz):
        return {**me, "x": (me["x"] + dx) % 4, "z": (me["z"] + 2 * dz) % 4}

    def slab_index(chip):
        return chip["x"] * 2 + chip["z"] // 2

    order = slab_offsets + [(0, 0)]
    slabs = [slab_index(slab_chip(dx, dz)) for dx, dz in order]

    def columns(slab):
        return pl.ds(pl.multiple_of(slab * width, 128), width)

    loads = []
    for k, slab in enumerate(slabs):
        loads.append(
            pltpu.make_async_copy(w_out.at[:, columns(slab)], wo.at[:, columns(slab)], load_sem.at[k])
        )
    for k, (source, target) in enumerate(((w_gate, wg), (w_up, wu), (router, wr), (w_down, wd))):
        loads.append(pltpu.make_async_copy(source, target, load_sem.at[8 + k]))
    for load in loads:
        load.start()

    peers = [sibling]
    for axis in AXES:
        peers += [device(moved(me, axis, k), core) for k in (1, 2, 3)]
    peers += [device(slab_chip(dx, 1), core) for dx in (1, 2, 3)]
    barrier = pltpu.get_barrier_semaphore()
    for peer in peers:
        pl.semaphore_signal(barrier, inc=1, device_id=peer, device_id_type=MESH)
    pl.semaphore_wait(barrier, len(peers))

    from_sibling = []
    for k, slab in enumerate(slabs):
        loads[k].wait()
        head_terms = jnp.dot(values[...], wo[:, columns(slab)], preferred_element_type=jnp.float32)
        terms[k] = head_terms.astype(jnp.bfloat16).reshape(2, half, width)
        from_sibling.append(copies.start(terms.at[k, other], core_terms.at[k], sibling))
    from_slabs = []
    for k, (dx, dz) in enumerate(order):
        from_sibling[k].wait_recv()
        total = terms[k, core].astype(jnp.float32) + core_terms[k].astype(jnp.float32)
        if k < len(slab_offsets):
            terms[k, core] = total.astype(jnp.bfloat16)
            from_slabs.append(
                copies.start(terms.at[k, core], slab_terms.at[k], device(slab_chip(dx, dz), core))
            )
    for k, copy in enumerate(from_slabs):
        copy.wait_recv()
        total = total + slab_terms[k].astype(jnp.float32)
    own_rows = pl.ds(pl.multiple_of(core * half, 16), half)
    tokens[me["x"], me["z"], me["y"], own_rows, :] = total.astype(jnp.bfloat16)

    def block(p, where):
        first, count = piece_rows[p]
        rows = pl.ds(pl.multiple_of(core * half + first, 16), count)
        return pick(tokens, where, (rows, pl.ds(*piece_cols[p])))

    def spread(p, where, to):
        return copies.start(block(p, where), block(p, where), to)

    to_core = []
    phase_one, phase_two = {}, {}
    for p, (first, second, last) in enumerate(ORDERS):
        phase_one[p] = [spread(p, me, device(moved(me, first, k), core)) for k in (1, 3, 2)]
    for p, (first, second, last) in enumerate(ORDERS):
        for copy in phase_one[p]:
            copy.wait_recv()
        where = {second: me[second], last: me[last]}
        phase_two[p] = [spread(p, where, device(moved(me, second, k), core)) for k in (1, 3, 2)]
    near = {}
    for p, (first, second, last) in enumerate(ORDERS):
        for copy in phase_two[p]:
            copy.wait_recv()
        parts = [{last: me[last], second: pl.ds(0, 2)}, {last: me[last], second: pl.ds(2, 2)}]
        right, left = device(moved(me, last, 1), core), device(moved(me, last, 3), core)
        right_a, left_b = spread(p, parts[0], right), spread(p, parts[1], left)
        right_b, left_a = spread(p, parts[1], right), spread(p, parts[0], left)
        near[p] = (right_a, right_b, left_a, left_b)
        to_core.append(spread(p, {last: me[last]}, sibling))
    far = {}
    for p, (first, second, last) in enumerate(ORDERS):
        right_a, right_b, left_a, left_b = near[p]
        right, left = device(moved(me, last, 1), core), device(moved(me, last, 3), core)
        before, after = (me[last] + 3) % 4, (me[last] + 1) % 4
        right_a.wait_recv()
        forward_a = spread(p, {last: before, second: pl.ds(0, 2)}, right)
        left_b.wait_recv()
        forward_b = spread(p, {last: after, second: pl.ds(2, 2)}, left)
        far[p] = (forward_a, forward_b)
    for p, (first, second, last) in enumerate(ORDERS):
        right_a, right_b, left_a, left_b = near[p]
        before, after = (me[last] + 3) % 4, (me[last] + 1) % 4
        right_b.wait_recv()
        to_core.append(spread(p, {last: before}, sibling))
        left_a.wait_recv()
        to_core.append(spread(p, {last: after}, sibling))
    for p, (first, second, last) in enumerate(ORDERS):
        for copy in far[p]:
            copy.wait_recv()
        to_core.append(spread(p, {last: (me[last] + 2) % 4}, sibling))
    for copy in to_core:
        copy.wait_recv()

    rank_copies = []
    for slab in range(8):
        rank_copies.append(
            pltpu.make_async_copy(
                tokens.at[slab // 2, slab % 2 * 2 + me["z"] % 2, me["y"]],
                attended.at[:, pl.ds(slab * width, width)],
                load_sem.at[12 + slab],
            )
        )
        rank_copies[-1].start()

    for load in loads[8:]:
        load.wait()
    gate_sum[...] = jnp.zeros_like(gate_sum)
    up_sum[...] = jnp.zeros_like(up_sum)
    score_sum[...] = jnp.zeros_like(score_sum)
    square_sum[...] = jnp.zeros_like(square_sum)

    @pl.loop(0, 8)
    def _(slab):
        rows = tokens[slab // 2, pl.ds(slab % 2 * 2, 2)].reshape(8 * slots, width).astype(jnp.float32)
        square_sum[...] += jnp.sum(rows * rows, axis=1, keepdims=True)
        gained = (rows * gain[slab]).astype(jnp.bfloat16)
        gate_sum[...] += jnp.dot(gained, wg[slab], preferred_element_type=jnp.float32)
        up_sum[...] += jnp.dot(gained, wu[slab], preferred_element_type=jnp.float32)
        score_sum[...] += jnp.dot(gained, wr[slab], preferred_element_type=jnp.float32)

    scale = lax.rsqrt(square_sum[...] * (1.0 / (8 * width)) + epsilon)
    scores = score_sum[...] * scale
    affinity = 1.0 / (1.0 + jnp.exp(-scores))
    experts = lax.broadcasted_iota(jnp.int32, scores.shape, 1)
    named = jnp.zeros(scores.shape, jnp.float32)
    for k in range(routes.shape[1]):
        named = named + jnp.where(routes[:, k : k + 1] == experts, 1.0, 0.0)
    chosen = affinity * named
    mine = jnp.sum(jnp.where(experts == lax.axis_index("ep"), chosen, 0.0), axis=1, keepdims=True)
    weight = route_scale * mine / jnp.sum(chosen, axis=1, keepdims=True)
    gate = gate_sum[...] * scale
    hidden = gate / (1.0 + jnp.exp(-gate)) * (up_sum[...] * scale) * weight
    act[...] = hidden.astype(jnp.bfloat16)

    def down(p, column_half):
        first, count = out_cols[p]
        quarters = []
        for quarter in range(2):
            start = pl.multiple_of(column_half * (2 * unit_cols) + quarter * unit_cols + first, 128)
            quarters.append(
                jnp.dot(act[...], wd[:, pl.ds(start, count)], preferred_element_type=jnp.float32)
                .reshape(2, 4, 4, 2, 8, count)
            )
        both = jnp.concatenate(quarters, axis=4).astype(jnp.bfloat16)
        for zl in range(2):
            for y in range(4):
                for zh in range(2):
                    partial[column_half, :, zh * 2 + zl, y, :, pl.ds(first, count)] = both[zl, y, :, zh]

    units = range(3)
    to_core = []
    for p in units:
        down(p, other)
        cols = pl.ds(*out_cols[p])
        to_core.append(
            copies.start(partial.at[other, :, :, :, :, cols], core_partial.at[:, :, :, :, cols], sibling)
        )
    rest = [tuple(a for a in AXES if a != order[2]) for order in ORDERS]
    far, near = {}, {}

    for p, (first, second, last) in enumerate(ORDERS):
        cols = pl.ds(*out_cols[p])
        width_p = out_cols[p][1]
        down(p, core)
        to_core[p].wait_recv()

        @pl.loop(0, 4)
        def _(x):
            partial[core, x, :, :, :, cols] = (
                partial[core, x, :, :, :, cols].astype(jnp.float32)
                + core_partial[x, :, :, :, cols].astype(jnp.float32)
            ).astype(jnp.bfloat16)

        def source(where):
            return pick(partial.at[core], where, (slice(None), cols))

        right, left = device(moved(me, last, 1), core), device(moved(me, last, 3), core)
        before, after, across = (me[last] + 3) % 4, (me[last] + 1) % 4, (me[last] + 2) % 4
        tail = (slice(None), pl.ds(0, width_p))

        def landing(ref, where):
            return pick(ref, where, tail, rest[p])

        a, b = {second: pl.ds(0, 2)}, {second: pl.ds(2, 2)}
        far_a = copies.start(source({last: across, **a}), landing(far_parts.at[p], a), right)
        far_b = copies.start(source({last: across, **b}), landing(far_parts.at[p], b), left)
        right_b = copies.start(source({last: after, **b}), landing(near_parts.at[p, 0], b), right)
        left_a = copies.start(source({last: before, **a}), landing(near_parts.at[p, 1], a), left)
        far[p], near[p] = (far_a, far_b), [right_b, left_a]

    for p, (first, second, last) in enumerate(ORDERS):
        cols = pl.ds(*out_cols[p])
        width_p = out_cols[p][1]
        right, left = device(moved(me, last, 1), core), device(moved(me, last, 3), core)
        before, after = (me[last] + 3) % 4, (me[last] + 1) % 4
        tail = (slice(None), pl.ds(0, width_p))
        for side, (copy, part, at, to) in enumerate(
            ((far[p][0], pl.ds(0, 2), after, right), (far[p][1], pl.ds(2, 2), before, left))
        ):
            copy.wait_recv()
            here = pick(partial.at[core], {last: at, second: part}, (slice(None), cols))
            came = pick(far_parts.at[p], {second: part}, tail, rest[p])
            here[...] = (here[...].astype(jnp.float32) + came[...].astype(jnp.float32)).astype(jnp.bfloat16)
            near[p].append(copies.start(here, pick(near_parts.at[p, side], {second: part}, tail, rest[p]), to))

    phase_two = {}
    for p, (first, second, last) in enumerate(ORDERS):
        cols = pl.ds(*out_cols[p])
        width_p = out_cols[p][1]
        tail = (slice(None), pl.ds(0, width_p))
        for copy in near[p]:
            copy.wait_recv()
        here = pick(partial.at[core], {last: me[last]}, (slice(None), cols))
        total = here[...].astype(jnp.float32)
        for side in range(2):
            total = total + near_parts[p, side, :, :, :, pl.ds(0, width_p)].astype(jnp.float32)
        sums_two[p, :, :, :, pl.ds(0, width_p)] = total.astype(jnp.bfloat16)
        phase_two[p] = []
        for k in (1, 3, 2):
            to = moved(me, second, k)
            phase_two[p].append(
                copies.start(
                    pick(sums_two.at[p], {second: to[second]}, tail, rest[p]),
                    parts_two.at[p, k - 1, :, :, pl.ds(0, width_p)],
                    device(to, core),
                )
            )
    phase_three = {}
    for p, (first, second, last) in enumerate(ORDERS):
        width_p = out_cols[p][1]
        tail = (slice(None), pl.ds(0, width_p))
        for copy in phase_two[p]:
            copy.wait_recv()
        total = pick(sums_two.at[p], {second: me[second]}, tail, rest[p])[...].astype(jnp.float32)
        for k in range(3):
            total = total + parts_two[p, k, :, :, pl.ds(0, width_p)].astype(jnp.float32)
        sums_three[p, :, :, pl.ds(0, width_p)] = total.astype(jnp.bfloat16)
        phase_three[p] = []
        for k in (1, 3, 2):
            to = moved(me, first, k)
            phase_three[p].append(
                copies.start(
                    sums_three.at[p, to[first], :, pl.ds(0, width_p)],
                    parts_three.at[p, k - 1, :, pl.ds(0, width_p)],
                    device(to, core),
                )
            )
    for p, (first, second, last) in enumerate(ORDERS):
        width_p = out_cols[p][1]
        for copy in phase_three[p]:
            copy.wait_recv()
        total = sums_three[p, me[first], :, pl.ds(0, width_p)].astype(jnp.float32)
        for k in range(3):
            total = total + parts_three[p, k, :, pl.ds(0, width_p)].astype(jnp.float32)
        final_half[0, :, pl.ds(*out_cols[p])] = total.astype(jnp.bfloat16)
    last_copy = copies.start(final_half.at[0], final_half.at[1], sibling)
    mixed[core] = final_half[0]
    last_copy.wait_recv()
    mixed[other] = final_half[1]
    for copy in rank_copies:
        copy.wait()
    copies.finish()


def run_experts(values, routes, gain, w_out, router, w_gate, w_up, w_down):
    slots, heads_width = values.shape
    model = w_out.shape[1]
    width = model // 8
    half = slots // 2
    hidden = w_gate.shape[1]
    experts = router.shape[1]
    rows = 8 * slots
    unit_cols = model // 4
    share = (unit_cols // 128 * 5 + 6) // 14 * 128
    bf16, f32 = jnp.bfloat16, jnp.float32
    vmem = pl.BlockSpec(memory_space=pltpu.VMEM)
    hbm = pl.BlockSpec(memory_space=pl.ANY)
    return pl.pallas_call(
        experts_kernel,
        out_shape=(
            jax.ShapeDtypeStruct((slots, model), bf16),
            jax.ShapeDtypeStruct((2, 16, unit_cols), bf16),
        ),
        in_specs=[vmem, vmem, vmem, hbm, hbm, hbm, hbm, hbm],
        out_specs=(hbm, vmem),
        scratch_shapes=[
            pltpu.VMEM((heads_width, model), bf16),
            pltpu.VMEM((8, width, experts), bf16),
            pltpu.VMEM((8, width, hidden), bf16),
            pltpu.VMEM((8, width, hidden), bf16),
            pltpu.VMEM((hidden, model), bf16),
            pltpu.VMEM((8, 2, half, width), bf16),
            pltpu.VMEM((8, half, width), bf16),
            pltpu.VMEM((7, half, width), bf16),
            pltpu.VMEM((4, 4, 4, slots, width), bf16),
            pltpu.VMEM((rows, hidden), f32),
            pltpu.VMEM((rows, hidden), f32),
            pltpu.VMEM((rows, experts), f32),
            pltpu.VMEM((rows, 1), f32),
            pltpu.VMEM((rows, hidden), bf16),
            pltpu.VMEM((2, 4, 4, 4, 16, unit_cols), bf16),
            pltpu.VMEM((4, 4, 4, 16, unit_cols), bf16),
            pltpu.VMEM((3, 4, 4, 16, share), bf16),
            pltpu.VMEM((3, 2, 4, 4, 16, share), bf16),
            pltpu.VMEM((3, 4, 4, 16, share), bf16),
            pltpu.VMEM((3, 3, 4, 16, share), bf16),
            pltpu.VMEM((3, 4, 16, share), bf16),
            pltpu.VMEM((3, 3, 16, share), bf16),
            pltpu.VMEM((2, 16, unit_cols), bf16),
            pltpu.SemaphoreType.DMA((20,)),
            pltpu.SemaphoreType.DMA((112,)),
            pltpu.SemaphoreType.DMA((112,)),
        ],
        compiler_params=pltpu.CompilerParams(
            collective_id=0, has_side_effects=True, vmem_limit_bytes=60 * 1024 * 1024
        ),
        name="experts",
    )(
        values,
        routes,
        gain.reshape(8, 1, width),
        w_out,
        router.reshape(8, width, experts),
        w_gate.reshape(8, width, hidden),
        w_up.reshape(8, width, hidden),
        w_down,
    )


def per_device(
    queries,
    cache_latent,
    cache_rope,
    cache_len,
    move_plan,
    w_absorb,
    w_out,
    norm_gain,
    router,
    routes,
    w_gate,
    w_up,
    w_down,
):
    all_routes = lax.all_gather(routes, "dp", axis=0, tiled=True)
    latent, rope_keys, lengths = move_caches(cache_latent, cache_rope, cache_len, move_plan)
    values = attend(queries, latent, rope_keys, lengths, w_absorb)
    attended, mixed = run_experts(
        values, all_routes, norm_gain, w_out, router, w_gate[0], w_up[0], w_down[0]
    )
    core = lax.axis_index("ep") % 2
    quarters = mixed.reshape(2, 2, 2, 4, mixed.shape[-1])
    own = lax.dynamic_index_in_dim(quarters, core, 2, keepdims=False)
    mixture = own.transpose(2, 0, 1, 3).reshape(4, -1)
    return (attended, mixture)


def solution(mesh):
    in_specs = (
        P("dp", "ep"),
        P("dp", None, None),
        P("dp", None, None),
        P("dp"),
        P(),
        P("ep", None, None),
        P("ep", None),
        P(),
        P(),
        P("dp", None),
        P("ep", None, "dp"),
        P("ep", None, "dp"),
        P("ep", "dp", None),
    )
    out_specs = (P("dp", None), P(("dp", "ep"), None))
    return jax.shard_map(
        per_device, mesh=mesh, in_specs=in_specs, out_specs=out_specs, check_vma=False
    )
```

```python
import jax
import jax.numpy as jnp
from jax import lax
from jax.experimental import pallas as pl
from jax.experimental.pallas import tpu as pltpu
from jax.sharding import PartitionSpec as P

VDIM = 128

epsilon = 1e-06
route_scale = 2.5


MESH = pl.DeviceIdType.MESH
AXES = ("x", "z", "y")
ORDERS = (("y", "z", "x"), ("z", "x", "y"), ("x", "y", "z"))


def coordinates():
    dp, ep = lax.axis_index("dp"), lax.axis_index("ep")
    me = {"x": ep // 4, "z": (ep // 2) % 2 * 2 + dp // 4, "y": dp % 4}
    return me, ep % 2


def device(at, core):
    return ((at["z"] % 2) * 4 + at["y"], at["x"] * 4 + at["z"] // 2 * 2 + core)


def moved(me, axis, offset):
    return {**me, axis: (me[axis] + offset) % 4}


def pick(ref, where, tail=(), axes=AXES):
    return ref.at[tuple(where.get(a, slice(None)) for a in axes) + tuple(tail)]


class Copies:
    def __init__(self, send, recv):
        self.send, self.recv, self.used, self.sent = send, recv, 0, []

    def start(self, src, dst, to):
        copy = pltpu.make_async_remote_copy(
            src_ref=src,
            dst_ref=dst,
            send_sem=self.send.at[self.used],
            recv_sem=self.recv.at[self.used],
            device_id=to,
            device_id_type=MESH,
        )
        copy.start()
        self.used += 1
        self.sent.append(copy)
        return copy

    def finish(self):
        for copy in self.sent:
            copy.wait_send()


def decode_kernel(
    queries,
    plan,
    lengths,
    routes,
    gain,
    cache_latent,
    cache_rope,
    w_absorb,
    w_out,
    router,
    w_gate,
    w_up,
    w_down,
    attended,
    mixed,
    keys,
    rope_keys,
    wa,
    query_latent,
    query_rope,
    query_out,
    query_in,
    marks_out,
    marks,
    latent_out,
    values,
    values_out,
    values_in,
    wo,
    wr,
    wg,
    wu,
    wd,
    terms,
    core_terms,
    slab_terms,
    tokens,
    gate_sum,
    up_sum,
    score_sum,
    square_sum,
    act,
    partial,
    core_partial,
    far_parts,
    near_parts,
    sums_two,
    parts_two,
    sums_three,
    parts_three,
    final_half,
    load_sem,
    send_sem,
    recv_sem,
):
    me, core = coordinates()
    other = 1 - core
    sibling = device(me, other)
    copies = Copies(send_sem, recv_sem)
    width = wg.shape[1]
    slots, heads = queries.shape[0], wa.shape[0]
    latent_width, rope_width = keys.shape[1], rope_keys.shape[1]
    cap = keys.shape[0] // slots
    half = slots // 2
    tiles = width // 128
    wide = (tiles * 5 + 6) // 7 * 128
    piece_rows = ((0, half // 2), (half // 2, half // 2), (0, half))
    piece_cols = ((0, wide), (0, wide), (wide, width - wide))
    unit_cols = partial.shape[-1]
    share = (unit_cols // 128 * 5 + 6) // 14 * 128
    out_cols = ((0, share), (share, share), (2 * share, unit_cols - 2 * share))

    slab_offsets = [(dx, dz) for dx in range(4) for dz in range(2) if (dx, dz) != (0, 0)]

    def slab_chip(dx, dz):
        return {**me, "x": (me["x"] + dx) % 4, "z": (me["z"] + 2 * dz) % 4}

    def slab_index(chip):
        return chip["x"] * 2 + chip["z"] // 2

    order = slab_offsets + [(0, 0)]
    slabs = [slab_index(slab_chip(dx, dz)) for dx, dz in order]

    def columns(slab):
        return pl.ds(pl.multiple_of(slab * width, 128), width)

    loads = []
    group = 16
    group_keys = group * cap
    groups = slots // group
    cache_loads = []
    for g in range(groups):
        rows = pl.ds(g * group_keys, group_keys)
        cache_loads.append(
            (
                pltpu.make_async_copy(cache_latent.at[rows], keys.at[rows], load_sem.at[20 + 2 * g]),
                pltpu.make_async_copy(cache_rope.at[rows], rope_keys.at[rows], load_sem.at[21 + 2 * g]),
            )
        )
        for load in cache_loads[-1]:
            load.start()
    absorb_load = pltpu.make_async_copy(w_absorb, wa, load_sem.at[28])
    absorb_load.start()
    for k, slab in enumerate(slabs):
        loads.append(
            pltpu.make_async_copy(w_out.at[:, columns(slab)], wo.at[:, columns(slab)], load_sem.at[k])
        )
    for k, (source, target) in enumerate(((w_gate, wg), (w_up, wu), (router, wr), (w_down, wd))):
        loads.append(pltpu.make_async_copy(source, target, load_sem.at[8 + k]))
    for load in loads:
        load.start()

    f32, bf16 = jnp.float32, jnp.bfloat16
    my_rank = lax.axis_index("dp")

    def iota(shape, axis):
        return lax.broadcasted_iota(jnp.int32, shape, axis)

    def mark(condition):
        return jnp.where(condition, 1.0, 0.0)

    def dot(a, b):
        return jnp.dot(a, b, preferred_element_type=f32)

    shift = slots.bit_length() - 1
    rank_of, slot_of = plan[...] >> shift, plan[...] & (slots - 1)
    rank_row = iota((8, slots), 0)
    earlier = mark(iota((slots, slots), 0) < iota((slots, slots), 1)).astype(bf16)
    own_rank = jnp.sum(jnp.where(rank_row == my_rank, rank_of, 0).astype(f32), axis=0, keepdims=True)
    leaving = mark((own_rank == rank_row.astype(f32)) & (rank_row != my_rank))
    letter = jnp.sum(leaving * dot(leaving.astype(bf16), earlier), axis=0, keepdims=True)
    away = jnp.sum(leaving, axis=0, keepdims=True)
    key_row = jnp.where(away > 0.5, own_rank * 2.0 + letter, -1.0)
    diagonal = iota((slots, slots), 0) == iota((slots, slots), 1)
    key = jnp.sum(jnp.where(diagonal, key_row, 0.0), axis=1, keepdims=True).astype(jnp.int32)
    stays = key < 0
    length = jnp.sum(jnp.where(diagonal, lengths[...].astype(f32), 0.0), axis=1, keepdims=True).astype(jnp.int32)

    arriving = mark((rank_of == my_rank) & (rank_row != my_rank))
    nth = dot(arriving.astype(bf16), earlier)
    guest_slot = []
    for k in range(2):
        is_kth = (arriving > 0.5) & (jnp.abs(nth - k) < 0.5)
        guest_slot.append(jnp.sum(jnp.where(is_kth, slot_of + 1, 0).astype(f32), axis=1, keepdims=True) - 1.0)

    def letter_places(axis, shape):
        place = iota(shape, axis)
        inner = place & 15
        return place >> 4, inner >> 1, inner & 1, inner < 2 * heads

    for h in range(heads):
        start = h * (latent_width + rope_width)
        query_latent[h] = queries[:, start : start + latent_width]
        query_rope[h] = queries[:, start + latent_width : start + latent_width + rope_width]

    to_rank, to_head, to_letter, used = letter_places(0, (128, slots))
    wanted = jnp.where(used, to_rank * 2 + to_letter, -2).astype(f32)
    chosen = mark(key_row == wanted)
    out_latent = jnp.zeros((128, latent_width), f32)
    out_rope = jnp.zeros((128, rope_width), f32)
    for h in range(heads):
        rows = jnp.where(to_head == h, chosen, 0.0).astype(bf16)
        out_latent = out_latent + dot(rows, query_latent[h])
        out_rope = out_rope + dot(rows, query_rope[h])
    query_out[:, :, 0:latent_width] = out_latent.astype(bf16).reshape(8, 16, latent_width)
    query_out[:, :, latent_width:] = (
        jnp.concatenate([out_rope, jnp.zeros((128, 128 - rope_width), f32)], axis=1)
        .astype(bf16)
        .reshape(8, 16, 128)
    )
    experts = iota((slots, marks.shape[2]), 1)
    named = jnp.zeros(experts.shape, f32)
    for k in range(routes.shape[1]):
        named = named + mark(routes[:, k : k + 1] == experts)
    marks_out[...] = named.astype(bf16)
    marks[my_rank] = named.astype(bf16)
    query_in[my_rank] = jnp.zeros(query_in.shape[1:], bf16)
    values_in[my_rank] = jnp.zeros(values_in.shape[1:], bf16)

    peers = [sibling]
    for axis in AXES:
        peers += [device(moved(me, axis, k), core) for k in (1, 2, 3)]
    peers += [device(slab_chip(dx, 1), core) for dx in (1, 2, 3)]
    rank_offsets = [(dz, dy) for dz in range(2) for dy in range(4) if (dz, dy) != (0, 0)]

    def rank_chip(dz, dy):
        z = me["z"] // 2 * 2 + (me["z"] + dz) % 2
        return {**me, "z": z, "y": (me["y"] + dy) % 4}

    peers += [device(rank_chip(1, dy), core) for dy in (1, 2, 3)]
    barrier = pltpu.get_barrier_semaphore()
    for peer in peers:
        pl.semaphore_signal(barrier, inc=1, device_id=peer, device_id_type=MESH)
    pl.semaphore_wait(barrier, len(peers))

    from_ranks = []
    for dz, dy in rank_offsets:
        chip = rank_chip(dz, dy)
        to = device(chip, core)
        from_ranks.append(copies.start(query_out.at[to[0]], query_in.at[my_rank], to))
    from_marks = []
    for dz, dy in rank_offsets:
        from_marks.append(copies.start(marks_out, marks.at[my_rank], device(rank_chip(dz, dy), core)))

    from_rank, from_head, from_letter, used = letter_places(1, (8, 128))
    guests = jnp.where(from_letter == 0, guest_slot[0], guest_slot[1])
    guests = jnp.where((from_rank == iota((8, 128), 0)) & used, guests + 1.0, 0.0)
    guests = jnp.sum(guests, axis=0, keepdims=True) - 1.0
    _, from_head, _, _ = letter_places(1, (slots, 128))
    is_guest = mark(guests == iota((slots, 128), 0).astype(f32))
    for copy in from_ranks:
        copy.wait_recv()
    came = query_in[...].reshape(128, query_in.shape[2])
    for h in range(heads):
        rows = jnp.where(from_head == h, is_guest, 0.0).astype(bf16)
        guest = dot(rows, came)
        query_latent[h] = jnp.where(stays, query_latent[h].astype(f32), guest[:, :latent_width]).astype(bf16)
        query_rope[h] = jnp.where(
            stays, query_rope[h].astype(f32), guest[:, latent_width : latent_width + rope_width]
        ).astype(bf16)

    score_scale = (VDIM + rope_width) ** -0.5
    rows_shape = (heads * group, group_keys)
    position = iota(rows_shape, 1) - iota(rows_shape, 0) % group * cap
    contract_last = (((1,), (1,)), ((), ()))
    for g in range(groups):
        for load in cache_loads[g]:
            load.wait()
        mine = pl.ds(g * group, group)
        q_latent = query_latent[:, mine, :].reshape(heads * group, latent_width)
        q_rope = query_rope[:, mine, :].reshape(heads * group, rope_width)
        here = pl.ds(g * group_keys, group_keys)
        scores = lax.dot_general(q_latent, keys[here, :], contract_last, preferred_element_type=f32)
        scores = scores + lax.dot_general(q_rope, rope_keys[here, :], contract_last, preferred_element_type=f32)
        limit = jnp.concatenate([length[g * group : (g + 1) * group]] * heads, axis=0)
        seen = (position >= 0) & (position < limit)
        scores = jnp.where(seen, scores * score_scale, -jnp.inf)
        raised = jnp.exp(scores - jnp.max(scores, axis=1, keepdims=True))
        probs = (raised / jnp.sum(raised, axis=1, keepdims=True)).astype(bf16)
        latent_out[:, mine, :] = dot(probs, keys[here, :]).astype(bf16).reshape(heads, group, latent_width)
    absorb_load.wait()
    for h in range(heads):
        values[:, h * VDIM : (h + 1) * VDIM] = dot(latent_out[h], wa[h]).astype(bf16)

    guest_column = jnp.concatenate(guest_slot, axis=0)
    select = mark(guest_column == iota((16, slots), 1).astype(f32)).astype(bf16)
    values_out[...] = dot(select, values[...]).astype(bf16)
    from_ranks = []
    for dz, dy in rank_offsets:
        from_ranks.append(copies.start(values_out, values_in.at[my_rank], device(rank_chip(dz, dy), core)))
    for copy in from_ranks:
        copy.wait_recv()
    place = (key >> 1) * 16 + (key & 1) * 8 + my_rank
    back = mark((iota((slots, 128), 1) == place) & (key >= 0)).astype(bf16)
    returned = dot(back, values_in[...].reshape(128, values_in.shape[2]))
    values[...] = jnp.where(stays, values[...].astype(f32), returned).astype(bf16)

    from_sibling = []
    for k, slab in enumerate(slabs):
        loads[k].wait()
        head_terms = jnp.dot(values[...], wo[:, columns(slab)], preferred_element_type=jnp.float32)
        terms[k] = head_terms.astype(jnp.bfloat16).reshape(2, half, width)
        from_sibling.append(copies.start(terms.at[k, other], core_terms.at[k], sibling))
    from_slabs = []
    for k, (dx, dz) in enumerate(order):
        from_sibling[k].wait_recv()
        total = terms[k, core].astype(jnp.float32) + core_terms[k].astype(jnp.float32)
        if k < len(slab_offsets):
            terms[k, core] = total.astype(jnp.bfloat16)
            from_slabs.append(
                copies.start(terms.at[k, core], slab_terms.at[k], device(slab_chip(dx, dz), core))
            )
    for k, copy in enumerate(from_slabs):
        copy.wait_recv()
        total = total + slab_terms[k].astype(jnp.float32)
    own_rows = pl.ds(pl.multiple_of(core * half, 16), half)
    tokens[me["x"], me["z"], me["y"], own_rows, :] = total.astype(jnp.bfloat16)

    def block(p, where):
        first, count = piece_rows[p]
        rows = pl.ds(pl.multiple_of(core * half + first, 16), count)
        return pick(tokens, where, (rows, pl.ds(*piece_cols[p])))

    def spread(p, where, to):
        return copies.start(block(p, where), block(p, where), to)

    to_core = []
    phase_one, phase_two = {}, {}
    for p, (first, second, last) in enumerate(ORDERS):
        phase_one[p] = [spread(p, me, device(moved(me, first, k), core)) for k in (1, 3, 2)]
    for p, (first, second, last) in enumerate(ORDERS):
        for copy in phase_one[p]:
            copy.wait_recv()
        where = {second: me[second], last: me[last]}
        phase_two[p] = [spread(p, where, device(moved(me, second, k), core)) for k in (1, 3, 2)]
    near = {}
    for p, (first, second, last) in enumerate(ORDERS):
        for copy in phase_two[p]:
            copy.wait_recv()
        parts = [{last: me[last], second: pl.ds(0, 2)}, {last: me[last], second: pl.ds(2, 2)}]
        right, left = device(moved(me, last, 1), core), device(moved(me, last, 3), core)
        right_a, left_b = spread(p, parts[0], right), spread(p, parts[1], left)
        right_b, left_a = spread(p, parts[1], right), spread(p, parts[0], left)
        near[p] = (right_a, right_b, left_a, left_b)
        to_core.append(spread(p, {last: me[last]}, sibling))
    far = {}
    for p, (first, second, last) in enumerate(ORDERS):
        right_a, right_b, left_a, left_b = near[p]
        right, left = device(moved(me, last, 1), core), device(moved(me, last, 3), core)
        before, after = (me[last] + 3) % 4, (me[last] + 1) % 4
        right_a.wait_recv()
        forward_a = spread(p, {last: before, second: pl.ds(0, 2)}, right)
        left_b.wait_recv()
        forward_b = spread(p, {last: after, second: pl.ds(2, 2)}, left)
        far[p] = (forward_a, forward_b)
    for p, (first, second, last) in enumerate(ORDERS):
        right_a, right_b, left_a, left_b = near[p]
        before, after = (me[last] + 3) % 4, (me[last] + 1) % 4
        right_b.wait_recv()
        to_core.append(spread(p, {last: before}, sibling))
        left_a.wait_recv()
        to_core.append(spread(p, {last: after}, sibling))
    for p, (first, second, last) in enumerate(ORDERS):
        for copy in far[p]:
            copy.wait_recv()
        to_core.append(spread(p, {last: (me[last] + 2) % 4}, sibling))
    for copy in to_core:
        copy.wait_recv()

    rank_copies = []
    for slab in range(8):
        rank_copies.append(
            pltpu.make_async_copy(
                tokens.at[slab // 2, slab % 2 * 2 + me["z"] % 2, me["y"]],
                attended.at[:, pl.ds(slab * width, width)],
                load_sem.at[12 + slab],
            )
        )
        rank_copies[-1].start()

    for load in loads[8:]:
        load.wait()
    gate_sum[...] = jnp.zeros_like(gate_sum)
    up_sum[...] = jnp.zeros_like(up_sum)
    score_sum[...] = jnp.zeros_like(score_sum)
    square_sum[...] = jnp.zeros_like(square_sum)

    @pl.loop(0, 8)
    def _(slab):
        rows = tokens[slab // 2, pl.ds(slab % 2 * 2, 2)].reshape(8 * slots, width).astype(jnp.float32)
        square_sum[...] += jnp.sum(rows * rows, axis=1, keepdims=True)
        gained = (rows * gain[slab]).astype(jnp.bfloat16)
        gate_sum[...] += jnp.dot(gained, wg[slab], preferred_element_type=jnp.float32)
        up_sum[...] += jnp.dot(gained, wu[slab], preferred_element_type=jnp.float32)
        score_sum[...] += jnp.dot(gained, wr[slab], preferred_element_type=jnp.float32)

    scale = lax.rsqrt(square_sum[...] * (1.0 / (8 * width)) + epsilon)
    scores = score_sum[...] * scale
    affinity = 1.0 / (1.0 + jnp.exp(-scores))
    experts = lax.broadcasted_iota(jnp.int32, scores.shape, 1)
    for copy in from_marks:
        copy.wait_recv()
    chosen = affinity * marks[...].reshape(scores.shape).astype(f32)
    mine = jnp.sum(jnp.where(experts == lax.axis_index("ep"), chosen, 0.0), axis=1, keepdims=True)
    weight = route_scale * mine / jnp.sum(chosen, axis=1, keepdims=True)
    gate = gate_sum[...] * scale
    hidden = gate / (1.0 + jnp.exp(-gate)) * (up_sum[...] * scale) * weight
    act[...] = hidden.astype(jnp.bfloat16)

    def down(p, column_half):
        first, count = out_cols[p]
        quarters = []
        for quarter in range(2):
            start = pl.multiple_of(column_half * (2 * unit_cols) + quarter * unit_cols + first, 128)
            quarters.append(
                jnp.dot(act[...], wd[:, pl.ds(start, count)], preferred_element_type=jnp.float32)
                .reshape(2, 4, 4, 2, 8, count)
            )
        both = jnp.concatenate(quarters, axis=4).astype(jnp.bfloat16)
        for zl in range(2):
            for y in range(4):
                for zh in range(2):
                    partial[column_half, :, zh * 2 + zl, y, :, pl.ds(first, count)] = both[zl, y, :, zh]

    units = range(3)
    to_core = []
    for p in units:
        down(p, other)
        cols = pl.ds(*out_cols[p])
        to_core.append(
            copies.start(partial.at[other, :, :, :, :, cols], core_partial.at[:, :, :, :, cols], sibling)
        )
    rest = [tuple(a for a in AXES if a != order[2]) for order in ORDERS]
    far, near = {}, {}

    for p, (first, second, last) in enumerate(ORDERS):
        cols = pl.ds(*out_cols[p])
        width_p = out_cols[p][1]
        down(p, core)
        to_core[p].wait_recv()

        @pl.loop(0, 4)
        def _(x):
            partial[core, x, :, :, :, cols] = (
                partial[core, x, :, :, :, cols].astype(jnp.float32)
                + core_partial[x, :, :, :, cols].astype(jnp.float32)
            ).astype(jnp.bfloat16)

        def source(where):
            return pick(partial.at[core], where, (slice(None), cols))

        right, left = device(moved(me, last, 1), core), device(moved(me, last, 3), core)
        before, after, across = (me[last] + 3) % 4, (me[last] + 1) % 4, (me[last] + 2) % 4
        tail = (slice(None), pl.ds(0, width_p))

        def landing(ref, where):
            return pick(ref, where, tail, rest[p])

        a, b = {second: pl.ds(0, 2)}, {second: pl.ds(2, 2)}
        far_a = copies.start(source({last: across, **a}), landing(far_parts.at[p], a), right)
        far_b = copies.start(source({last: across, **b}), landing(far_parts.at[p], b), left)
        right_b = copies.start(source({last: after, **b}), landing(near_parts.at[p, 0], b), right)
        left_a = copies.start(source({last: before, **a}), landing(near_parts.at[p, 1], a), left)
        far[p], near[p] = (far_a, far_b), [right_b, left_a]

    for p, (first, second, last) in enumerate(ORDERS):
        cols = pl.ds(*out_cols[p])
        width_p = out_cols[p][1]
        right, left = device(moved(me, last, 1), core), device(moved(me, last, 3), core)
        before, after = (me[last] + 3) % 4, (me[last] + 1) % 4
        tail = (slice(None), pl.ds(0, width_p))
        for side, (copy, part, at, to) in enumerate(
            ((far[p][0], pl.ds(0, 2), after, right), (far[p][1], pl.ds(2, 2), before, left))
        ):
            copy.wait_recv()
            here = pick(partial.at[core], {last: at, second: part}, (slice(None), cols))
            came = pick(far_parts.at[p], {second: part}, tail, rest[p])
            here[...] = (here[...].astype(jnp.float32) + came[...].astype(jnp.float32)).astype(jnp.bfloat16)
            near[p].append(copies.start(here, pick(near_parts.at[p, side], {second: part}, tail, rest[p]), to))

    phase_two = {}
    for p, (first, second, last) in enumerate(ORDERS):
        cols = pl.ds(*out_cols[p])
        width_p = out_cols[p][1]
        tail = (slice(None), pl.ds(0, width_p))
        for copy in near[p]:
            copy.wait_recv()
        here = pick(partial.at[core], {last: me[last]}, (slice(None), cols))
        total = here[...].astype(jnp.float32)
        for side in range(2):
            total = total + near_parts[p, side, :, :, :, pl.ds(0, width_p)].astype(jnp.float32)
        sums_two[p, :, :, :, pl.ds(0, width_p)] = total.astype(jnp.bfloat16)
        phase_two[p] = []
        for k in (1, 3, 2):
            to = moved(me, second, k)
            phase_two[p].append(
                copies.start(
                    pick(sums_two.at[p], {second: to[second]}, tail, rest[p]),
                    parts_two.at[p, k - 1, :, :, pl.ds(0, width_p)],
                    device(to, core),
                )
            )
    phase_three = {}
    for p, (first, second, last) in enumerate(ORDERS):
        width_p = out_cols[p][1]
        tail = (slice(None), pl.ds(0, width_p))
        for copy in phase_two[p]:
            copy.wait_recv()
        total = pick(sums_two.at[p], {second: me[second]}, tail, rest[p])[...].astype(jnp.float32)
        for k in range(3):
            total = total + parts_two[p, k, :, :, pl.ds(0, width_p)].astype(jnp.float32)
        sums_three[p, :, :, pl.ds(0, width_p)] = total.astype(jnp.bfloat16)
        phase_three[p] = []
        for k in (1, 3, 2):
            to = moved(me, first, k)
            phase_three[p].append(
                copies.start(
                    sums_three.at[p, to[first], :, pl.ds(0, width_p)],
                    parts_three.at[p, k - 1, :, pl.ds(0, width_p)],
                    device(to, core),
                )
            )
    for p, (first, second, last) in enumerate(ORDERS):
        width_p = out_cols[p][1]
        for copy in phase_three[p]:
            copy.wait_recv()
        total = sums_three[p, me[first], :, pl.ds(0, width_p)].astype(jnp.float32)
        for k in range(3):
            total = total + parts_three[p, k, :, pl.ds(0, width_p)].astype(jnp.float32)
        final_half[0, :, pl.ds(*out_cols[p])] = total.astype(jnp.bfloat16)
    last_copy = copies.start(final_half.at[0], final_half.at[1], sibling)
    mixed[core] = final_half[0]
    last_copy.wait_recv()
    mixed[other] = final_half[1]
    for copy in rank_copies:
        copy.wait()
    copies.finish()


def run_decode(
    queries, plan, lengths, routes, gain, cache_latent, cache_rope, w_absorb, w_out, router, w_gate, w_up, w_down
):
    slots = queries.shape[0]
    cap, latent_width = cache_latent.shape[1:]
    rope_width = cache_rope.shape[2]
    heads = w_absorb.shape[0]
    heads_width = w_out.shape[0]
    model = w_out.shape[1]
    width = model // 8
    half = slots // 2
    hidden = w_gate.shape[1]
    experts = router.shape[1]
    rows = 8 * slots
    unit_cols = model // 4
    share = (unit_cols // 128 * 5 + 6) // 14 * 128
    bf16, f32 = jnp.bfloat16, jnp.float32
    vmem = pl.BlockSpec(memory_space=pltpu.VMEM)
    hbm = pl.BlockSpec(memory_space=pl.ANY)
    return pl.pallas_call(
        decode_kernel,
        out_shape=(
            jax.ShapeDtypeStruct((slots, model), bf16),
            jax.ShapeDtypeStruct((2, 16, unit_cols), bf16),
        ),
        in_specs=[vmem] * 5 + [hbm] * 8,
        out_specs=(hbm, vmem),
        scratch_shapes=[
            pltpu.VMEM((slots * cap, latent_width), bf16),
            pltpu.VMEM((slots * cap, rope_width), bf16),
            pltpu.VMEM(w_absorb.shape, bf16),
            pltpu.VMEM((heads, slots, latent_width), bf16),
            pltpu.VMEM((heads, slots, rope_width), bf16),
            pltpu.VMEM((8, 16, latent_width + 128), bf16),
            pltpu.VMEM((8, 16, latent_width + 128), bf16),
            pltpu.VMEM((slots, experts), bf16),
            pltpu.VMEM((8, slots, experts), bf16),
            pltpu.VMEM((heads, slots, latent_width), bf16),
            pltpu.VMEM((slots, heads_width), bf16),
            pltpu.VMEM((16, heads_width), bf16),
            pltpu.VMEM((8, 16, heads_width), bf16),
            pltpu.VMEM((heads_width, model), bf16),
            pltpu.VMEM((8, width, experts), bf16),
            pltpu.VMEM((8, width, hidden), bf16),
            pltpu.VMEM((8, width, hidden), bf16),
            pltpu.VMEM((hidden, model), bf16),
            pltpu.VMEM((8, 2, half, width), bf16),
            pltpu.VMEM((8, half, width), bf16),
            pltpu.VMEM((7, half, width), bf16),
            pltpu.VMEM((4, 4, 4, slots, width), bf16),
            pltpu.VMEM((rows, hidden), f32),
            pltpu.VMEM((rows, hidden), f32),
            pltpu.VMEM((rows, experts), f32),
            pltpu.VMEM((rows, 1), f32),
            pltpu.VMEM((rows, hidden), bf16),
            pltpu.VMEM((2, 4, 4, 4, 16, unit_cols), bf16),
            pltpu.VMEM((4, 4, 4, 16, unit_cols), bf16),
            pltpu.VMEM((3, 4, 4, 16, share), bf16),
            pltpu.VMEM((3, 2, 4, 4, 16, share), bf16),
            pltpu.VMEM((3, 4, 4, 16, share), bf16),
            pltpu.VMEM((3, 3, 4, 16, share), bf16),
            pltpu.VMEM((3, 4, 16, share), bf16),
            pltpu.VMEM((3, 3, 16, share), bf16),
            pltpu.VMEM((2, 16, unit_cols), bf16),
            pltpu.SemaphoreType.DMA((32,)),
            pltpu.SemaphoreType.DMA((128,)),
            pltpu.SemaphoreType.DMA((128,)),
        ],
        compiler_params=pltpu.CompilerParams(
            collective_id=0, has_side_effects=True, vmem_limit_bytes=60 * 1024 * 1024
        ),
        name="decode",
    )(
        queries,
        plan,
        lengths,
        routes,
        gain.reshape(8, 1, width),
        cache_latent.reshape(slots * cap, latent_width),
        cache_rope.reshape(slots * cap, rope_width),
        w_absorb,
        w_out,
        router.reshape(8, width, experts),
        w_gate.reshape(8, width, hidden),
        w_up.reshape(8, width, hidden),
        w_down,
    )


def per_device(
    queries,
    cache_latent,
    cache_rope,
    cache_len,
    move_plan,
    w_absorb,
    w_out,
    norm_gain,
    router,
    routes,
    w_gate,
    w_up,
    w_down,
):
    slots = cache_len.shape[0]
    attended, mixed = run_decode(
        queries,
        move_plan.reshape(-1, slots),
        cache_len.reshape(1, slots),
        routes,
        norm_gain,
        cache_latent,
        cache_rope,
        w_absorb,
        w_out,
        router,
        w_gate[0],
        w_up[0],
        w_down[0],
    )
    core = lax.axis_index("ep") % 2
    quarters = mixed.reshape(2, 2, 2, 4, mixed.shape[-1])
    own = lax.dynamic_index_in_dim(quarters, core, 2, keepdims=False)
    mixture = own.transpose(2, 0, 1, 3).reshape(4, -1)
    return (attended, mixture)


def solution(mesh):
    in_specs = (
        P("dp", "ep"),
        P("dp", None, None),
        P("dp", None, None),
        P("dp"),
        P(),
        P("ep", None, None),
        P("ep", None),
        P(),
        P(),
        P("dp", None),
        P("ep", None, "dp"),
        P("ep", None, "dp"),
        P("ep", "dp", None),
    )
    out_specs = (P("dp", None), P(("dp", "ep"), None))
    return jax.shard_map(
        per_device, mesh=mesh, in_specs=in_specs, out_specs=out_specs, check_vma=False
    )
```

```python
import jax
import jax.numpy as jnp
from jax import lax
from jax.experimental import pallas as pl
from jax.experimental.pallas import tpu as pltpu
from jax.sharding import PartitionSpec as P

VDIM = 128

epsilon = 1e-06
route_scale = 2.5


MESH = pl.DeviceIdType.MESH
AXES = ("x", "z", "y")
ORDERS = (("y", "z", "x"), ("z", "x", "y"), ("x", "y", "z"))


def coordinates():
    dp, ep = lax.axis_index("dp"), lax.axis_index("ep")
    me = {"x": ep // 4, "z": (ep // 2) % 2 * 2 + dp // 4, "y": dp % 4}
    return me, ep % 2


def device(at, core):
    return ((at["z"] % 2) * 4 + at["y"], at["x"] * 4 + at["z"] // 2 * 2 + core)


def moved(me, axis, offset):
    return {**me, axis: (me[axis] + offset) % 4}


def pick(ref, where, tail=(), axes=AXES):
    return ref.at[tuple(where.get(a, slice(None)) for a in axes) + tuple(tail)]


class Copies:
    def __init__(self, send, recv):
        self.send, self.recv, self.used, self.sent = send, recv, 0, []

    def start(self, src, dst, to):
        copy = pltpu.make_async_remote_copy(
            src_ref=src,
            dst_ref=dst,
            send_sem=self.send.at[self.used],
            recv_sem=self.recv.at[self.used],
            device_id=to,
            device_id_type=MESH,
        )
        copy.start()
        self.used += 1
        self.sent.append(copy)
        return copy

    def finish(self):
        for copy in self.sent:
            copy.wait_send()


def decode_kernel(
    queries,
    plan,
    lengths,
    routes,
    gain,
    cache_latent,
    cache_rope,
    w_absorb,
    w_out,
    router,
    w_gate,
    w_up,
    w_down,
    attended,
    mixed,
    keys,
    rope_keys,
    wa,
    query_latent,
    query_rope,
    query_out,
    query_in,
    marks_out,
    marks,
    latent_out,
    values,
    values_out,
    values_in,
    wo,
    wr,
    wg,
    wu,
    wd,
    terms,
    core_terms,
    slab_terms,
    tokens,
    gate_sum,
    up_sum,
    score_sum,
    square_sum,
    act,
    partial,
    core_partial,
    far_parts,
    near_parts,
    sums_two,
    parts_two,
    sums_three,
    parts_three,
    final_half,
    load_sem,
    send_sem,
    recv_sem,
):
    me, core = coordinates()
    other = 1 - core
    sibling = device(me, other)
    copies = Copies(send_sem, recv_sem)
    width = wg.shape[1]
    slots, heads = queries.shape[0], wa.shape[0]
    latent_width, rope_width = keys.shape[1], rope_keys.shape[1]
    cap = keys.shape[0] // slots
    half = slots // 2
    tiles = width // 128
    wide = (tiles * 5 + 6) // 7 * 128
    piece_rows = ((0, half // 2), (half // 2, half // 2), (0, half))
    piece_cols = ((0, wide), (0, wide), (wide, width - wide))
    unit_cols = partial.shape[-1]
    share = (unit_cols // 128 * 5 + 6) // 14 * 128
    out_cols = ((0, share), (share, share), (2 * share, unit_cols - 2 * share))

    slab_offsets = [(dx, dz) for dx in range(4) for dz in range(2) if (dx, dz) != (0, 0)]

    def slab_chip(dx, dz):
        return {**me, "x": (me["x"] + dx) % 4, "z": (me["z"] + 2 * dz) % 4}

    def slab_index(chip):
        return chip["x"] * 2 + chip["z"] // 2

    order = slab_offsets + [(0, 0)]
    slabs = [slab_index(slab_chip(dx, dz)) for dx, dz in order]

    def columns(slab):
        return pl.ds(pl.multiple_of(slab * width, 128), width)

    loads = []
    group = 16
    group_keys = group * cap
    groups = slots // group
    cache_loads = []
    for g in range(groups):
        rows = pl.ds(g * group_keys, group_keys)
        cache_loads.append(
            (
                pltpu.make_async_copy(cache_latent.at[rows], keys.at[rows], load_sem.at[20 + 2 * g]),
                pltpu.make_async_copy(
                    cache_rope.at[pl.ds(g * group, group)], rope_keys.at[pl.ds(g * group, group)], load_sem.at[21 + 2 * g]
                ),
            )
        )
        for load in cache_loads[-1]:
            load.start()
    absorb_load = pltpu.make_async_copy(w_absorb, wa, load_sem.at[28])
    absorb_load.start()
    for k, slab in enumerate(slabs):
        loads.append(
            pltpu.make_async_copy(w_out.at[:, columns(slab)], wo.at[:, columns(slab)], load_sem.at[k])
        )
    for k, (source, target) in enumerate(((w_gate, wg), (w_up, wu), (router, wr), (w_down, wd))):
        loads.append(pltpu.make_async_copy(source, target, load_sem.at[8 + k]))
    for load in loads:
        load.start()

    f32, bf16 = jnp.float32, jnp.bfloat16
    my_rank = lax.axis_index("dp")

    def iota(shape, axis):
        return lax.broadcasted_iota(jnp.int32, shape, axis)

    def mark(condition):
        return jnp.where(condition, 1.0, 0.0)

    def dot(a, b):
        return jnp.dot(a, b, preferred_element_type=f32)

    shift = slots.bit_length() - 1
    sources = jnp.concatenate([plan[:, r * slots : (r + 1) * slots] for r in range(8)], axis=0)
    rank_of, slot_of = sources >> shift, sources & (slots - 1)
    rank_row = iota((8, slots), 0)
    earlier = mark(iota((slots, slots), 0) < iota((slots, slots), 1)).astype(bf16)
    own_rank = jnp.sum(jnp.where(rank_row == my_rank, rank_of, 0).astype(f32), axis=0, keepdims=True)
    leaving = mark((own_rank == rank_row.astype(f32)) & (rank_row != my_rank))
    letter = jnp.sum(leaving * dot(leaving.astype(bf16), earlier), axis=0, keepdims=True)
    away = jnp.sum(leaving, axis=0, keepdims=True)
    key_row = jnp.where(away > 0.5, own_rank * 2.0 + letter, -1.0)
    diagonal = iota((slots, slots), 0) == iota((slots, slots), 1)
    key = jnp.sum(jnp.where(diagonal, key_row, 0.0), axis=1, keepdims=True).astype(jnp.int32)
    stays = key < 0
    length = jnp.sum(jnp.where(diagonal, lengths[...].astype(f32), 0.0), axis=1, keepdims=True).astype(jnp.int32)

    arriving = mark((rank_of == my_rank) & (rank_row != my_rank))
    nth = dot(arriving.astype(bf16), earlier)
    guest_slot = []
    for k in range(2):
        is_kth = (arriving > 0.5) & (jnp.abs(nth - k) < 0.5)
        guest_slot.append(jnp.sum(jnp.where(is_kth, slot_of + 1, 0).astype(f32), axis=1, keepdims=True) - 1.0)

    def letter_places(axis, shape):
        place = iota(shape, axis)
        inner = place & 15
        return place >> 4, inner >> 1, inner & 1, inner < 2 * heads

    for h in range(heads):
        start = h * (latent_width + rope_width)
        query_latent[h] = queries[:, start : start + latent_width]
        query_rope[h] = queries[:, start + latent_width : start + latent_width + rope_width]

    to_rank, to_head, to_letter, used = letter_places(0, (128, slots))
    wanted = jnp.where(used, to_rank * 2 + to_letter, -2).astype(f32)
    chosen = mark(key_row == wanted)
    out_latent = jnp.zeros((128, latent_width), f32)
    out_rope = jnp.zeros((128, rope_width), f32)
    for h in range(heads):
        rows = jnp.where(to_head == h, chosen, 0.0).astype(bf16)
        out_latent = out_latent + dot(rows, query_latent[h])
        out_rope = out_rope + dot(rows, query_rope[h])
    query_out[:, :, 0:latent_width] = out_latent.astype(bf16).reshape(8, 16, latent_width)
    query_out[:, :, latent_width:] = (
        jnp.concatenate([out_rope, jnp.zeros((128, 128 - rope_width), f32)], axis=1)
        .astype(bf16)
        .reshape(8, 16, 128)
    )
    experts = iota((slots, marks.shape[2]), 1)
    named = jnp.zeros(experts.shape, f32)
    for k in range(routes.shape[0]):
        route = jnp.sum(jnp.where(diagonal, routes[k : k + 1, :], 0).astype(f32), axis=1, keepdims=True)
        named = named + mark(route.astype(jnp.int32) == experts)
    marks_out[...] = named.astype(bf16)
    marks[my_rank] = named.astype(bf16)
    query_in[my_rank] = jnp.zeros(query_in.shape[1:], bf16)
    values_in[my_rank] = jnp.zeros(values_in.shape[1:], bf16)

    peers = [sibling]
    for axis in AXES:
        peers += [device(moved(me, axis, k), core) for k in (1, 2, 3)]
    peers += [device(slab_chip(dx, 1), core) for dx in (1, 2, 3)]
    rank_offsets = [(dz, dy) for dz in range(2) for dy in range(4) if (dz, dy) != (0, 0)]

    def rank_chip(dz, dy):
        z = me["z"] // 2 * 2 + (me["z"] + dz) % 2
        return {**me, "z": z, "y": (me["y"] + dy) % 4}

    peers += [device(rank_chip(1, dy), core) for dy in (1, 2, 3)]
    barrier = pltpu.get_barrier_semaphore()
    for peer in peers:
        pl.semaphore_signal(barrier, inc=1, device_id=peer, device_id_type=MESH)
    pl.semaphore_wait(barrier, len(peers))

    from_ranks = []
    for dz, dy in rank_offsets:
        chip = rank_chip(dz, dy)
        to = device(chip, core)
        from_ranks.append(copies.start(query_out.at[to[0]], query_in.at[my_rank], to))
    from_marks = []
    for dz, dy in rank_offsets:
        from_marks.append(copies.start(marks_out, marks.at[my_rank], device(rank_chip(dz, dy), core)))

    from_rank, from_head, from_letter, used = letter_places(1, (8, 128))
    guests = jnp.where(from_letter == 0, guest_slot[0], guest_slot[1])
    guests = jnp.where((from_rank == iota((8, 128), 0)) & used, guests + 1.0, 0.0)
    guests = jnp.sum(guests, axis=0, keepdims=True) - 1.0
    _, from_head, _, _ = letter_places(1, (slots, 128))
    is_guest = mark(guests == iota((slots, 128), 0).astype(f32))
    for copy in from_ranks:
        copy.wait_recv()
    came = query_in[...].reshape(128, query_in.shape[2])
    for h in range(heads):
        rows = jnp.where(from_head == h, is_guest, 0.0).astype(bf16)
        guest = dot(rows, came)
        query_latent[h] = jnp.where(stays, query_latent[h].astype(f32), guest[:, :latent_width]).astype(bf16)
        query_rope[h] = jnp.where(
            stays, query_rope[h].astype(f32), guest[:, latent_width : latent_width + rope_width]
        ).astype(bf16)

    score_scale = (VDIM + rope_width) ** -0.5
    rows_shape = (heads * group, group_keys)
    position = iota(rows_shape, 1) - iota(rows_shape, 0) % group * cap
    contract_last = (((1,), (1,)), ((), ()))
    for g in range(groups):
        for load in cache_loads[g]:
            load.wait()
        mine = pl.ds(g * group, group)
        q_latent = query_latent[:, mine, :].reshape(heads * group, latent_width)
        q_rope = query_rope[:, mine, :].reshape(heads * group, rope_width)
        here = pl.ds(g * group_keys, group_keys)
        scores = lax.dot_general(q_latent, keys[here, :], contract_last, preferred_element_type=f32)
        rotary = jnp.concatenate([rope_keys[g * group + k] for k in range(group)], axis=1)
        scores = scores + dot(q_rope, rotary)
        limit = jnp.concatenate([length[g * group : (g + 1) * group]] * heads, axis=0)
        seen = (position >= 0) & (position < limit)
        scores = jnp.where(seen, scores * score_scale, -jnp.inf)
        raised = jnp.exp(scores - jnp.max(scores, axis=1, keepdims=True))
        probs = (raised / jnp.sum(raised, axis=1, keepdims=True)).astype(bf16)
        latent_out[:, mine, :] = dot(probs, keys[here, :]).astype(bf16).reshape(heads, group, latent_width)
    absorb_load.wait()
    for h in range(heads):
        values[:, h * VDIM : (h + 1) * VDIM] = dot(latent_out[h], wa[h]).astype(bf16)

    guest_column = jnp.concatenate(guest_slot, axis=0)
    select = mark(guest_column == iota((16, slots), 1).astype(f32)).astype(bf16)
    values_out[...] = dot(select, values[...]).astype(bf16)
    from_ranks = []
    for dz, dy in rank_offsets:
        from_ranks.append(copies.start(values_out, values_in.at[my_rank], device(rank_chip(dz, dy), core)))
    for copy in from_ranks:
        copy.wait_recv()
    place = (key >> 1) * 16 + (key & 1) * 8 + my_rank
    back = mark((iota((slots, 128), 1) == place) & (key >= 0)).astype(bf16)
    returned = dot(back, values_in[...].reshape(128, values_in.shape[2]))
    values[...] = jnp.where(stays, values[...].astype(f32), returned).astype(bf16)

    from_sibling = []
    for k, slab in enumerate(slabs):
        loads[k].wait()
        head_terms = jnp.dot(values[...], wo[:, columns(slab)], preferred_element_type=jnp.float32)
        terms[k] = head_terms.astype(jnp.bfloat16).reshape(2, half, width)
        from_sibling.append(copies.start(terms.at[k, other], core_terms.at[k], sibling))
    from_slabs = []
    for k, (dx, dz) in enumerate(order):
        from_sibling[k].wait_recv()
        total = terms[k, core].astype(jnp.float32) + core_terms[k].astype(jnp.float32)
        if k < len(slab_offsets):
            terms[k, core] = total.astype(jnp.bfloat16)
            from_slabs.append(
                copies.start(terms.at[k, core], slab_terms.at[k], device(slab_chip(dx, dz), core))
            )
    for k, copy in enumerate(from_slabs):
        copy.wait_recv()
        total = total + slab_terms[k].astype(jnp.float32)
    own_rows = pl.ds(pl.multiple_of(core * half, 16), half)
    tokens[me["x"], me["z"], me["y"], own_rows, :] = total.astype(jnp.bfloat16)

    def block(p, where):
        first, count = piece_rows[p]
        rows = pl.ds(pl.multiple_of(core * half + first, 16), count)
        return pick(tokens, where, (rows, pl.ds(*piece_cols[p])))

    def spread(p, where, to):
        return copies.start(block(p, where), block(p, where), to)

    to_core = []
    phase_one, phase_two = {}, {}
    for p, (first, second, last) in enumerate(ORDERS):
        phase_one[p] = [spread(p, me, device(moved(me, first, k), core)) for k in (1, 3, 2)]
    for p, (first, second, last) in enumerate(ORDERS):
        for copy in phase_one[p]:
            copy.wait_recv()
        where = {second: me[second], last: me[last]}
        phase_two[p] = [spread(p, where, device(moved(me, second, k), core)) for k in (1, 3, 2)]
    near = {}
    for p, (first, second, last) in enumerate(ORDERS):
        for copy in phase_two[p]:
            copy.wait_recv()
        parts = [{last: me[last], second: pl.ds(0, 2)}, {last: me[last], second: pl.ds(2, 2)}]
        right, left = device(moved(me, last, 1), core), device(moved(me, last, 3), core)
        right_a, left_b = spread(p, parts[0], right), spread(p, parts[1], left)
        right_b, left_a = spread(p, parts[1], right), spread(p, parts[0], left)
        near[p] = (right_a, right_b, left_a, left_b)
        to_core.append(spread(p, {last: me[last]}, sibling))
    far = {}
    for p, (first, second, last) in enumerate(ORDERS):
        right_a, right_b, left_a, left_b = near[p]
        right, left = device(moved(me, last, 1), core), device(moved(me, last, 3), core)
        before, after = (me[last] + 3) % 4, (me[last] + 1) % 4
        right_a.wait_recv()
        forward_a = spread(p, {last: before, second: pl.ds(0, 2)}, right)
        left_b.wait_recv()
        forward_b = spread(p, {last: after, second: pl.ds(2, 2)}, left)
        far[p] = (forward_a, forward_b)
    for p, (first, second, last) in enumerate(ORDERS):
        right_a, right_b, left_a, left_b = near[p]
        before, after = (me[last] + 3) % 4, (me[last] + 1) % 4
        right_b.wait_recv()
        to_core.append(spread(p, {last: before}, sibling))
        left_a.wait_recv()
        to_core.append(spread(p, {last: after}, sibling))
    for p, (first, second, last) in enumerate(ORDERS):
        for copy in far[p]:
            copy.wait_recv()
        to_core.append(spread(p, {last: (me[last] + 2) % 4}, sibling))
    for copy in to_core:
        copy.wait_recv()

    rank_copies = []
    for slab in range(8):
        rank_copies.append(
            pltpu.make_async_copy(
                tokens.at[slab // 2, slab % 2 * 2 + me["z"] % 2, me["y"]],
                attended.at[:, pl.ds(slab * width, width)],
                load_sem.at[12 + slab],
            )
        )
        rank_copies[-1].start()

    for load in loads[8:]:
        load.wait()
    gate_sum[...] = jnp.zeros_like(gate_sum)
    up_sum[...] = jnp.zeros_like(up_sum)
    score_sum[...] = jnp.zeros_like(score_sum)
    square_sum[...] = jnp.zeros_like(square_sum)

    @pl.loop(0, 8)
    def _(slab):
        rows = tokens[slab // 2, pl.ds(slab % 2 * 2, 2)].reshape(8 * slots, width).astype(jnp.float32)
        square_sum[...] += jnp.sum(rows * rows, axis=1, keepdims=True)
        gained = (rows * gain[slab]).astype(jnp.bfloat16)
        gate_sum[...] += jnp.dot(gained, wg[slab], preferred_element_type=jnp.float32)
        up_sum[...] += jnp.dot(gained, wu[slab], preferred_element_type=jnp.float32)
        score_sum[...] += lax.dot_general(
            gained,
            wr[:, pl.ds(pl.multiple_of(slab * width, 128), width)],
            contract_last,
            preferred_element_type=f32,
        )

    scale = lax.rsqrt(square_sum[...] * (1.0 / (8 * width)) + epsilon)
    scores = score_sum[...] * scale
    affinity = 1.0 / (1.0 + jnp.exp(-scores))
    experts = lax.broadcasted_iota(jnp.int32, scores.shape, 1)
    for copy in from_marks:
        copy.wait_recv()
    chosen = affinity * marks[...].reshape(scores.shape).astype(f32)
    mine = jnp.sum(jnp.where(experts == lax.axis_index("ep"), chosen, 0.0), axis=1, keepdims=True)
    weight = route_scale * mine / jnp.sum(chosen, axis=1, keepdims=True)
    gate = gate_sum[...] * scale
    hidden = gate / (1.0 + jnp.exp(-gate)) * (up_sum[...] * scale) * weight
    act[...] = hidden.astype(jnp.bfloat16)

    def down(p, column_half):
        first, count = out_cols[p]
        quarters = []
        for quarter in range(2):
            start = pl.multiple_of(column_half * (2 * unit_cols) + quarter * unit_cols + first, 128)
            quarters.append(
                jnp.dot(act[...], wd[:, pl.ds(start, count)], preferred_element_type=jnp.float32)
                .reshape(2, 4, 4, 2, 8, count)
            )
        both = jnp.concatenate(quarters, axis=4).astype(jnp.bfloat16)
        for zl in range(2):
            for y in range(4):
                for zh in range(2):
                    partial[column_half, :, zh * 2 + zl, y, :, pl.ds(first, count)] = both[zl, y, :, zh]

    units = range(3)
    to_core = []
    for p in units:
        down(p, other)
        cols = pl.ds(*out_cols[p])
        to_core.append(
            copies.start(partial.at[other, :, :, :, :, cols], core_partial.at[:, :, :, :, cols], sibling)
        )
    rest = [tuple(a for a in AXES if a != order[2]) for order in ORDERS]
    far, near = {}, {}

    for p, (first, second, last) in enumerate(ORDERS):
        cols = pl.ds(*out_cols[p])
        width_p = out_cols[p][1]
        down(p, core)
        to_core[p].wait_recv()

        @pl.loop(0, 4)
        def _(x):
            partial[core, x, :, :, :, cols] = (
                partial[core, x, :, :, :, cols].astype(jnp.float32)
                + core_partial[x, :, :, :, cols].astype(jnp.float32)
            ).astype(jnp.bfloat16)

        def source(where):
            return pick(partial.at[core], where, (slice(None), cols))

        right, left = device(moved(me, last, 1), core), device(moved(me, last, 3), core)
        before, after, across = (me[last] + 3) % 4, (me[last] + 1) % 4, (me[last] + 2) % 4
        tail = (slice(None), pl.ds(0, width_p))

        def landing(ref, where):
            return pick(ref, where, tail, rest[p])

        a, b = {second: pl.ds(0, 2)}, {second: pl.ds(2, 2)}
        far_a = copies.start(source({last: across, **a}), landing(far_parts.at[p], a), right)
        far_b = copies.start(source({last: across, **b}), landing(far_parts.at[p], b), left)
        right_b = copies.start(source({last: after, **b}), landing(near_parts.at[p, 0], b), right)
        left_a = copies.start(source({last: before, **a}), landing(near_parts.at[p, 1], a), left)
        far[p], near[p] = (far_a, far_b), [right_b, left_a]

    for p, (first, second, last) in enumerate(ORDERS):
        cols = pl.ds(*out_cols[p])
        width_p = out_cols[p][1]
        right, left = device(moved(me, last, 1), core), device(moved(me, last, 3), core)
        before, after = (me[last] + 3) % 4, (me[last] + 1) % 4
        tail = (slice(None), pl.ds(0, width_p))
        for side, (copy, part, at, to) in enumerate(
            ((far[p][0], pl.ds(0, 2), after, right), (far[p][1], pl.ds(2, 2), before, left))
        ):
            copy.wait_recv()
            here = pick(partial.at[core], {last: at, second: part}, (slice(None), cols))
            came = pick(far_parts.at[p], {second: part}, tail, rest[p])
            here[...] = (here[...].astype(jnp.float32) + came[...].astype(jnp.float32)).astype(jnp.bfloat16)
            near[p].append(copies.start(here, pick(near_parts.at[p, side], {second: part}, tail, rest[p]), to))

    phase_two = {}
    for p, (first, second, last) in enumerate(ORDERS):
        cols = pl.ds(*out_cols[p])
        width_p = out_cols[p][1]
        tail = (slice(None), pl.ds(0, width_p))
        for copy in near[p]:
            copy.wait_recv()
        here = pick(partial.at[core], {last: me[last]}, (slice(None), cols))
        total = here[...].astype(jnp.float32)
        for side in range(2):
            total = total + near_parts[p, side, :, :, :, pl.ds(0, width_p)].astype(jnp.float32)
        sums_two[p, :, :, :, pl.ds(0, width_p)] = total.astype(jnp.bfloat16)
        phase_two[p] = []
        for k in (1, 3, 2):
            to = moved(me, second, k)
            phase_two[p].append(
                copies.start(
                    pick(sums_two.at[p], {second: to[second]}, tail, rest[p]),
                    parts_two.at[p, k - 1, :, :, pl.ds(0, width_p)],
                    device(to, core),
                )
            )
    phase_three = {}
    for p, (first, second, last) in enumerate(ORDERS):
        width_p = out_cols[p][1]
        tail = (slice(None), pl.ds(0, width_p))
        for copy in phase_two[p]:
            copy.wait_recv()
        total = pick(sums_two.at[p], {second: me[second]}, tail, rest[p])[...].astype(jnp.float32)
        for k in range(3):
            total = total + parts_two[p, k, :, :, pl.ds(0, width_p)].astype(jnp.float32)
        sums_three[p, :, :, pl.ds(0, width_p)] = total.astype(jnp.bfloat16)
        phase_three[p] = []
        for k in (1, 3, 2):
            to = moved(me, first, k)
            phase_three[p].append(
                copies.start(
                    sums_three.at[p, to[first], :, pl.ds(0, width_p)],
                    parts_three.at[p, k - 1, :, pl.ds(0, width_p)],
                    device(to, core),
                )
            )
    for p, (first, second, last) in enumerate(ORDERS):
        width_p = out_cols[p][1]
        for copy in phase_three[p]:
            copy.wait_recv()
        total = sums_three[p, me[first], :, pl.ds(0, width_p)].astype(jnp.float32)
        for k in range(3):
            total = total + parts_three[p, k, :, pl.ds(0, width_p)].astype(jnp.float32)
        final_half[0, :, pl.ds(*out_cols[p])] = total.astype(jnp.bfloat16)
    last_copy = copies.start(final_half.at[0], final_half.at[1], sibling)
    last_copy.wait_recv()
    for side, column_half in enumerate((core, other)):
        both = final_half[side].astype(f32)
        for quarter in range(2):
            eight = both[quarter * 8 : quarter * 8 + 8]
            own = jnp.where(core == 0, eight[0:4], eight[4:8])
            start = pl.multiple_of(column_half * (2 * unit_cols) + quarter * unit_cols, 128)
            mixed[:, pl.ds(start, unit_cols)] = own.astype(bf16)
    for copy in rank_copies:
        copy.wait()
    copies.finish()


def run_decode(
    queries, plan, lengths, routes, gain, cache_latent, cache_rope, w_absorb, w_out, router, w_gate, w_up, w_down
):
    slots = queries.shape[0]
    cap, latent_width = cache_latent.shape[1:]
    rope_width = cache_rope.shape[2]
    heads = w_absorb.shape[0]
    heads_width = w_out.shape[0]
    model = w_out.shape[1]
    width = model // 8
    half = slots // 2
    hidden = w_gate.shape[1]
    experts = router.shape[1]
    rows = 8 * slots
    unit_cols = model // 4
    share = (unit_cols // 128 * 5 + 6) // 14 * 128
    bf16, f32 = jnp.bfloat16, jnp.float32
    vmem = pl.BlockSpec(memory_space=pltpu.VMEM)
    hbm = pl.BlockSpec(memory_space=pl.ANY)
    return pl.pallas_call(
        decode_kernel,
        out_shape=(
            jax.ShapeDtypeStruct((slots, model), bf16),
            jax.ShapeDtypeStruct((4, model), bf16),
        ),
        in_specs=[vmem] * 5 + [hbm] * 8,
        out_specs=(hbm, vmem),
        scratch_shapes=[
            pltpu.VMEM((slots * cap, latent_width), bf16),
            pltpu.VMEM((slots, rope_width, cap), bf16),
            pltpu.VMEM(w_absorb.shape, bf16),
            pltpu.VMEM((heads, slots, latent_width), bf16),
            pltpu.VMEM((heads, slots, rope_width), bf16),
            pltpu.VMEM((8, 16, latent_width + 128), bf16),
            pltpu.VMEM((8, 16, latent_width + 128), bf16),
            pltpu.VMEM((slots, experts), bf16),
            pltpu.VMEM((8, slots, experts), bf16),
            pltpu.VMEM((heads, slots, latent_width), bf16),
            pltpu.VMEM((slots, heads_width), bf16),
            pltpu.VMEM((16, heads_width), bf16),
            pltpu.VMEM((8, 16, heads_width), bf16),
            pltpu.VMEM((heads_width, model), bf16),
            pltpu.VMEM((experts, model), bf16),
            pltpu.VMEM((8, width, hidden), bf16),
            pltpu.VMEM((8, width, hidden), bf16),
            pltpu.VMEM((hidden, model), bf16),
            pltpu.VMEM((8, 2, half, width), bf16),
            pltpu.VMEM((8, half, width), bf16),
            pltpu.VMEM((7, half, width), bf16),
            pltpu.VMEM((4, 4, 4, slots, width), bf16),
            pltpu.VMEM((rows, hidden), f32),
            pltpu.VMEM((rows, hidden), f32),
            pltpu.VMEM((rows, experts), f32),
            pltpu.VMEM((rows, 1), f32),
            pltpu.VMEM((rows, hidden), bf16),
            pltpu.VMEM((2, 4, 4, 4, 16, unit_cols), bf16),
            pltpu.VMEM((4, 4, 4, 16, unit_cols), bf16),
            pltpu.VMEM((3, 4, 4, 16, share), bf16),
            pltpu.VMEM((3, 2, 4, 4, 16, share), bf16),
            pltpu.VMEM((3, 4, 4, 16, share), bf16),
            pltpu.VMEM((3, 3, 4, 16, share), bf16),
            pltpu.VMEM((3, 4, 16, share), bf16),
            pltpu.VMEM((3, 3, 16, share), bf16),
            pltpu.VMEM((2, 16, unit_cols), bf16),
            pltpu.SemaphoreType.DMA((32,)),
            pltpu.SemaphoreType.DMA((128,)),
            pltpu.SemaphoreType.DMA((128,)),
        ],
        compiler_params=pltpu.CompilerParams(
            collective_id=0, has_side_effects=True, vmem_limit_bytes=60 * 1024 * 1024
        ),
        name="decode",
    )(
        queries,
        plan,
        lengths,
        routes.T,
        gain.reshape(8, 1, width),
        cache_latent.reshape(slots * cap, latent_width),
        cache_rope.transpose(0, 2, 1),
        w_absorb,
        w_out,
        router.T,
        w_gate.reshape(8, width, hidden),
        w_up.reshape(8, width, hidden),
        w_down,
    )


def copy_kernel(source, small_source, target, small_target, held, small_held, sems):
    parts = held.shape[0]
    width = source.shape[1] // parts
    small_in = pltpu.make_async_copy(small_source, small_held, sems.at[2 * parts])
    small_in.start()
    copies_in, copies_out = [], []
    for k in range(parts):
        columns = pl.ds(k * width, width)
        copies_in.append(pltpu.make_async_copy(source.at[:, columns], held.at[k], sems.at[k]))
        copies_out.append(pltpu.make_async_copy(held.at[k], target.at[:, columns], sems.at[parts + k]))
        copies_in[-1].start()
    small_in.wait()
    small_out = pltpu.make_async_copy(small_held, small_target, sems.at[2 * parts + 1])
    small_out.start()
    for copy_in, copy_out in zip(copies_in, copies_out):
        copy_in.wait()
        copy_out.start()
    for copy in copies_out:
        copy.wait()
    small_out.wait()


def write_out(attended, mixed):
    hbm = pl.BlockSpec(memory_space=pl.ANY)
    parts = 4
    return pl.pallas_call(
        copy_kernel,
        out_shape=(
            jax.ShapeDtypeStruct(attended.shape, attended.dtype),
            jax.ShapeDtypeStruct(mixed.shape, mixed.dtype),
        ),
        in_specs=[hbm, hbm],
        out_specs=(hbm, hbm),
        scratch_shapes=[
            pltpu.VMEM((parts, attended.shape[0], attended.shape[1] // parts), attended.dtype),
            pltpu.VMEM(mixed.shape, mixed.dtype),
            pltpu.SemaphoreType.DMA((2 * parts + 2,)),
        ],
        compiler_params=pltpu.CompilerParams(vmem_limit_bytes=60 * 1024 * 1024),
        name="write_out",
    )(attended, mixed)


def per_device(
    queries,
    cache_latent,
    cache_rope,
    cache_len,
    move_plan,
    w_absorb,
    w_out,
    norm_gain,
    router,
    routes,
    w_gate,
    w_up,
    w_down,
):
    slots = cache_len.shape[0]
    attended, mixed = run_decode(
        queries,
        move_plan.reshape(1, -1),
        cache_len.reshape(1, slots),
        routes,
        norm_gain,
        cache_latent,
        cache_rope,
        w_absorb,
        w_out,
        router,
        w_gate[0],
        w_up[0],
        w_down[0],
    )
    return write_out(attended, mixed)


def solution(mesh):
    in_specs = (
        P("dp", "ep"),
        P("dp", None, None),
        P("dp", None, None),
        P("dp"),
        P(),
        P("ep", None, None),
        P("ep", None),
        P(),
        P(),
        P("dp", None),
        P("ep", None, "dp"),
        P("ep", None, "dp"),
        P("ep", "dp", None),
    )
    out_specs = (P("dp", None), P(("dp", "ep"), None))
    return jax.shard_map(
        per_device, mesh=mesh, in_specs=in_specs, out_specs=out_specs, check_vma=False
    )
```

```python
import jax
import jax.numpy as jnp
from jax import lax
from jax.experimental import pallas as pl
from jax.experimental.pallas import tpu as pltpu
from jax.sharding import PartitionSpec as P

VDIM = 128

epsilon = 1e-06
route_scale = 2.5


MESH = pl.DeviceIdType.MESH
AXES = ("x", "z", "y")
ORDERS = (("y", "z", "x"), ("z", "x", "y"), ("x", "y", "z"))


def coordinates():
    dp, ep = lax.axis_index("dp"), lax.axis_index("ep")
    me = {"x": ep // 4, "z": (ep // 2) % 2 * 2 + dp // 4, "y": dp % 4}
    return me, ep % 2


def device(at, core):
    return ((at["z"] % 2) * 4 + at["y"], at["x"] * 4 + at["z"] // 2 * 2 + core)


def moved(me, axis, offset):
    return {**me, axis: (me[axis] + offset) % 4}


def pick(ref, where, tail=(), axes=AXES):
    return ref.at[tuple(where.get(a, slice(None)) for a in axes) + tuple(tail)]


class Copies:
    def __init__(self, send, recv):
        self.send, self.recv, self.used, self.sent = send, recv, 0, []

    def start(self, src, dst, to):
        copy = pltpu.make_async_remote_copy(
            src_ref=src,
            dst_ref=dst,
            send_sem=self.send.at[self.used],
            recv_sem=self.recv.at[self.used],
            device_id=to,
            device_id_type=MESH,
        )
        copy.start()
        self.used += 1
        self.sent.append(copy)
        return copy

    def finish(self):
        for copy in self.sent:
            copy.wait_send()


def decode_kernel(
    plan,
    lengths,
    routes,
    queries_in,
    gain_in,
    cache_latent,
    cache_rope,
    w_absorb,
    w_out,
    router,
    w_gate,
    w_up,
    w_down,
    attended,
    mixed,
    queries,
    gain,
    keys,
    rope_keys,
    rotary,
    wa,
    query_latent,
    query_rope,
    query_out,
    query_in,
    marks_out,
    marks,
    latent_out,
    values,
    values_out,
    values_in,
    wo,
    wr,
    wg,
    wu,
    wd,
    terms,
    core_terms,
    slab_terms,
    tokens,
    act,
    partial,
    core_partial,
    far_parts,
    near_parts,
    sums_two,
    parts_two,
    sums_three,
    parts_three,
    final_half,
    load_sem,
    send_sem,
    recv_sem,
):
    me, core = coordinates()
    other = 1 - core
    sibling = device(me, other)
    copies = Copies(send_sem, recv_sem)
    width = wg.shape[1] // 2
    slots, heads = queries.shape[0], wa.shape[0]
    latent_width, rope_width = keys.shape[1], rope_keys.shape[1]
    cap = keys.shape[0] // slots
    half = slots // 2
    tiles = width // 128
    wide = (tiles * 5 + 6) // 7 * 128
    piece_rows = ((0, half // 2), (half // 2, half // 2), (0, half))
    piece_cols = ((0, wide), (0, wide), (wide, width - wide))
    unit_cols = partial.shape[-1]
    share = (unit_cols // 128 * 5 + 6) // 14 * 128
    out_cols = ((0, share), (share, share), (2 * share, unit_cols - 2 * share))

    slab_offsets = [(dx, dz) for dx in range(4) for dz in range(2) if (dx, dz) != (0, 0)]

    def slab_chip(dx, dz):
        return {**me, "x": (me["x"] + dx) % 4, "z": (me["z"] + 2 * dz) % 4}

    def slab_index(chip):
        return chip["x"] * 2 + chip["z"] // 2

    order = slab_offsets + [(0, 0)]
    slabs = [slab_index(slab_chip(dx, dz)) for dx, dz in order]

    def columns(slab):
        return pl.ds(pl.multiple_of(slab * width, 128), width)

    peers = [sibling]
    for axis in AXES:
        peers += [device(moved(me, axis, k), core) for k in (1, 2, 3)]
    peers += [device(slab_chip(dx, 1), core) for dx in (1, 2, 3)]
    rank_offsets = [(dz, dy) for dz in range(2) for dy in range(4) if (dz, dy) != (0, 0)]

    def rank_chip(dz, dy):
        z = me["z"] // 2 * 2 + (me["z"] + dz) % 2
        return {**me, "z": z, "y": (me["y"] + dy) % 4}

    peers += [device(rank_chip(1, dy), core) for dy in (1, 2, 3)]
    barrier = pltpu.get_barrier_semaphore()
    for peer in peers:
        pl.semaphore_signal(barrier, inc=1, device_id=peer, device_id_type=MESH)

    query_load = pltpu.make_async_copy(queries_in, queries, load_sem.at[50])
    query_load.start()
    gain_load = pltpu.make_async_copy(gain_in, gain, load_sem.at[51])
    loads = []
    group = 16
    group_keys = group * cap
    groups = slots // group
    cache_loads = []
    for g in range(groups):
        rows = pl.ds(g * group_keys, group_keys)
        cache_loads.append(
            (
                pltpu.make_async_copy(cache_latent.at[rows], keys.at[rows], load_sem.at[20 + 2 * g]),
                pltpu.make_async_copy(
                    cache_rope.at[pl.ds(g * group, group)], rope_keys.at[pl.ds(g * group, group)], load_sem.at[21 + 2 * g]
                ),
            )
        )
        for load in cache_loads[-1]:
            load.start()
    absorb_load = pltpu.make_async_copy(w_absorb, wa, load_sem.at[28])
    absorb_load.start()
    for k, slab in enumerate(slabs):
        loads.append(
            pltpu.make_async_copy(w_out.at[:, columns(slab)], wo.at[:, columns(slab)], load_sem.at[k])
        )
    for k, (source, target) in enumerate(((w_gate, wg), (w_up, wu), (router, wr), (w_down, wd))):
        loads.append(pltpu.make_async_copy(source, target, load_sem.at[8 + k]))
    loads.append(gain_load)
    for load in loads:
        load.start()

    f32, bf16 = jnp.float32, jnp.bfloat16
    my_rank = lax.axis_index("dp")

    def iota(shape, axis):
        return lax.broadcasted_iota(jnp.int32, shape, axis)

    def mark(condition):
        return jnp.where(condition, 1.0, 0.0)

    def dot(a, b):
        return jnp.dot(a, b, preferred_element_type=f32)

    shift = slots.bit_length() - 1
    sources = jnp.concatenate([plan[:, r * slots : (r + 1) * slots] for r in range(8)], axis=0)
    rank_of, slot_of = sources >> shift, sources & (slots - 1)
    rank_row = iota((8, slots), 0)
    earlier = mark(iota((slots, slots), 0) < iota((slots, slots), 1)).astype(bf16)
    own_rank = jnp.sum(jnp.where(rank_row == my_rank, rank_of, 0).astype(f32), axis=0, keepdims=True)
    leaving = mark((own_rank == rank_row.astype(f32)) & (rank_row != my_rank))
    letter = jnp.sum(leaving * dot(leaving.astype(bf16), earlier), axis=0, keepdims=True)
    away = jnp.sum(leaving, axis=0, keepdims=True)
    key_row = jnp.where(away > 0.5, own_rank * 2.0 + letter, -1.0)
    diagonal = iota((slots, slots), 0) == iota((slots, slots), 1)
    key = jnp.sum(jnp.where(diagonal, key_row, 0.0), axis=1, keepdims=True).astype(jnp.int32)
    stays = key < 0
    length = jnp.sum(jnp.where(diagonal, lengths[...].astype(f32), 0.0), axis=1, keepdims=True).astype(jnp.int32)

    arriving = mark((rank_of == my_rank) & (rank_row != my_rank))
    nth = dot(arriving.astype(bf16), earlier)
    guest_slot = []
    for k in range(2):
        is_kth = (arriving > 0.5) & (jnp.abs(nth - k) < 0.5)
        guest_slot.append(jnp.sum(jnp.where(is_kth, slot_of + 1, 0).astype(f32), axis=1, keepdims=True) - 1.0)

    def letter_places(axis, shape):
        place = iota(shape, axis)
        inner = place & 15
        return place >> 4, inner >> 1, inner & 1, inner < 2 * heads

    query_load.wait()
    for h in range(heads):
        start = h * (latent_width + rope_width)
        query_latent[h] = queries[:, start : start + latent_width]
        query_rope[h] = queries[:, start + latent_width : start + latent_width + rope_width]

    to_rank, to_head, to_letter, used = letter_places(0, (128, slots))
    wanted = jnp.where(used, to_rank * 2 + to_letter, -2).astype(f32)
    chosen = mark(key_row == wanted)
    out_latent = jnp.zeros((128, latent_width), f32)
    out_rope = jnp.zeros((128, rope_width), f32)
    for h in range(heads):
        rows = jnp.where(to_head == h, chosen, 0.0).astype(bf16)
        out_latent = out_latent + dot(rows, query_latent[h])
        out_rope = out_rope + dot(rows, query_rope[h])
    query_out[:, :, 0:latent_width] = out_latent.astype(bf16).reshape(8, 16, latent_width)
    query_out[:, :, latent_width:] = (
        jnp.concatenate([out_rope, jnp.zeros((128, 128 - rope_width), f32)], axis=1)
        .astype(bf16)
        .reshape(8, 16, 128)
    )
    experts = iota((slots, marks.shape[3]), 1)
    named = jnp.zeros(experts.shape, f32)
    for k in range(routes.shape[0]):
        route = jnp.sum(jnp.where(diagonal, routes[k : k + 1, :], 0).astype(f32), axis=1, keepdims=True)
        named = named + mark(route.astype(jnp.int32) == experts)
    marks_out[...] = named.astype(bf16).reshape(marks_out.shape)
    marks[my_rank] = marks_out[...]
    query_in[my_rank] = jnp.zeros(query_in.shape[1:], bf16)
    values_in[my_rank] = jnp.zeros(values_in.shape[1:], bf16)

    pl.semaphore_wait(barrier, len(peers))
    from_ranks = []
    for dz, dy in rank_offsets:
        chip = rank_chip(dz, dy)
        to = device(chip, core)
        from_ranks.append(copies.start(query_out.at[to[0]], query_in.at[my_rank], to))
    from_marks = []
    for dz, dy in rank_offsets:
        from_marks.append(copies.start(marks_out, marks.at[my_rank], device(rank_chip(dz, dy), core)))

    from_rank, from_head, from_letter, used = letter_places(1, (8, 128))
    guests = jnp.where(from_letter == 0, guest_slot[0], guest_slot[1])
    guests = jnp.where((from_rank == iota((8, 128), 0)) & used, guests + 1.0, 0.0)
    guests = jnp.sum(guests, axis=0, keepdims=True) - 1.0
    _, from_head, _, _ = letter_places(1, (slots, 128))
    is_guest = mark(guests == iota((slots, 128), 0).astype(f32))
    for g in range(groups):
        for load in cache_loads[g]:
            load.wait()
    for g in range(groups):
        rotary[g] = jnp.concatenate([rope_keys[g * group + k] for k in range(group)], axis=1)
    for copy in from_ranks:
        copy.wait_recv()
    came = query_in[...].reshape(128, query_in.shape[2])
    for h in range(heads):
        rows = jnp.where(from_head == h, is_guest, 0.0).astype(bf16)
        guest = dot(rows, came)
        query_latent[h] = jnp.where(stays, query_latent[h].astype(f32), guest[:, :latent_width]).astype(bf16)
        query_rope[h] = jnp.where(
            stays, query_rope[h].astype(f32), guest[:, latent_width : latent_width + rope_width]
        ).astype(bf16)

    score_scale = (VDIM + rope_width) ** -0.5
    rows_shape = (heads * group, group_keys)
    position = iota(rows_shape, 1) - iota(rows_shape, 0) % group * cap
    contract_last = (((1,), (1,)), ((), ()))
    for g in range(groups):
        mine = pl.ds(g * group, group)
        q_latent = query_latent[:, mine, :].reshape(heads * group, latent_width)
        q_rope = query_rope[:, mine, :].reshape(heads * group, rope_width)
        here = pl.ds(g * group_keys, group_keys)
        scores = lax.dot_general(q_latent, keys[here, :], contract_last, preferred_element_type=f32)
        scores = scores + dot(q_rope, rotary[g])
        limit = jnp.concatenate([length[g * group : (g + 1) * group]] * heads, axis=0)
        seen = (position >= 0) & (position < limit)
        scores = jnp.where(seen, scores * score_scale, -jnp.inf)
        raised = jnp.exp(scores - jnp.max(scores, axis=1, keepdims=True))
        probs = (raised / jnp.sum(raised, axis=1, keepdims=True)).astype(bf16)
        latent_out[:, mine, :] = dot(probs, keys[here, :]).astype(bf16).reshape(heads, group, latent_width)
    absorb_load.wait()
    for h in range(heads):
        values[:, h * VDIM : (h + 1) * VDIM] = dot(latent_out[h], wa[h]).astype(bf16)

    guest_column = jnp.concatenate(guest_slot, axis=0)
    select = mark(guest_column == iota((16, slots), 1).astype(f32)).astype(bf16)
    values_out[...] = dot(select, values[...]).astype(bf16)
    from_ranks = []
    for dz, dy in rank_offsets:
        from_ranks.append(copies.start(values_out, values_in.at[my_rank], device(rank_chip(dz, dy), core)))
    for copy in from_ranks:
        copy.wait_recv()
    place = (key >> 1) * 16 + (key & 1) * 8 + my_rank
    back = mark((iota((slots, 128), 1) == place) & (key >= 0)).astype(bf16)
    returned = dot(back, values_in[...].reshape(128, values_in.shape[2]))
    values[...] = jnp.where(stays, values[...].astype(f32), returned).astype(bf16)

    from_sibling = []
    for load in loads[:8]:
        load.wait()
    for k, slab in enumerate(slabs):
        head_terms = jnp.dot(values[...], wo[:, columns(slab)], preferred_element_type=jnp.float32)
        terms[k] = head_terms.astype(jnp.bfloat16).reshape(2, half, width)
        from_sibling.append(copies.start(terms.at[k, other], core_terms.at[k], sibling))
    from_slabs = []
    for k, (dx, dz) in enumerate(order):
        from_sibling[k].wait_recv()
        total = terms[k, core].astype(jnp.float32) + core_terms[k].astype(jnp.float32)
        if k < len(slab_offsets):
            terms[k, core] = total.astype(jnp.bfloat16)
            from_slabs.append(
                copies.start(terms.at[k, core], slab_terms.at[k], device(slab_chip(dx, dz), core))
            )
    for k, copy in enumerate(from_slabs):
        copy.wait_recv()
        total = total + slab_terms[k].astype(jnp.float32)
    tokens[me["x"], me["z"], me["y"], core] = total.astype(jnp.bfloat16)

    def block(p, where):
        first, count = piece_rows[p]
        return pick(tokens, where, (core, pl.ds(first, count), pl.ds(*piece_cols[p])))

    def spread(p, where, to):
        return copies.start(block(p, where), block(p, where), to)

    pieces = range(3)
    rights = [device(moved(me, order[2], 1), core) for order in ORDERS]
    lefts = [device(moved(me, order[2], 3), core) for order in ORDERS]
    before = [(me[order[2]] + 3) % 4 for order in ORDERS]
    after = [(me[order[2]] + 1) % 4 for order in ORDERS]
    across = [(me[order[2]] + 2) % 4 for order in ORDERS]
    here = [me[order[2]] for order in ORDERS]

    def group_at(p, k, last):
        second = ORDERS[p][1]
        return {second: (me[second] + 4 - k) % 4, ORDERS[p][2]: last}

    one = [
        [spread(p, me, device(moved(me, ORDERS[p][0], k), core)) for k in (1, 3, 2)] for p in pieces
    ]
    two = [{} for p in pieces]
    to_right, to_left = [{} for p in pieces], [{} for p in pieces]
    far, to_core = [[] for p in pieces], []

    def near(p, k):
        where = group_at(p, k, here[p])
        to_right[p][k] = spread(p, where, rights[p])
        to_left[p][k] = spread(p, where, lefts[p])

    for p in pieces:
        for copy in one[p]:
            copy.wait_recv()
        for k in (1, 3, 2):
            two[p][k] = spread(p, group_at(p, 0, here[p]), device(moved(me, ORDERS[p][1], k), core))
        near(p, 0)
    for k in (1, 3):
        for p in pieces:
            two[p][k].wait_recv()
            near(p, k)
    for p in pieces:
        to_right[p][0].wait_recv()
        far[p].append(spread(p, group_at(p, 0, before[p]), rights[p]))
    for p in pieces:
        two[p][2].wait_recv()
        near(p, 2)
        to_core.append(spread(p, {ORDERS[p][2]: here[p]}, sibling))
    for p in pieces:
        to_left[p][3].wait_recv()
        far[p].append(spread(p, group_at(p, 3, after[p]), lefts[p]))
        to_right[p][1].wait_recv()
        far[p].append(spread(p, group_at(p, 1, before[p]), rights[p]))
    for p in pieces:
        to_left[p][2].wait_recv()
        far[p].append(spread(p, group_at(p, 2, after[p]), lefts[p]))
    for p in pieces:
        for k in (3, 2):
            to_right[p][k].wait_recv()
        to_core.append(spread(p, {ORDERS[p][2]: before[p]}, sibling))
        for k in (0, 1):
            to_left[p][k].wait_recv()
        to_core.append(spread(p, {ORDERS[p][2]: after[p]}, sibling))
    for p in pieces:
        for copy in far[p]:
            copy.wait_recv()
        to_core.append(spread(p, {ORDERS[p][2]: across[p]}, sibling))

    for load in loads[8:]:
        load.wait()
    for copy in from_marks:
        copy.wait_recv()

    def products(side):
        square_sum = jnp.zeros((8 * half, 128), f32)
        gate, up, score = 0.0, 0.0, 0.0
        for x in range(4):
            rows = [tokens[x, pl.ds(zh * 2, 2), :, side].reshape(8 * half, width) for zh in range(2)]
            rows = jnp.concatenate(rows, axis=1).astype(f32)
            for k in range(2 * width // 128):
                part = rows[:, k * 128 : (k + 1) * 128]
                square_sum = square_sum + part * part
            gained = (rows * gain[x]).astype(bf16)
            gate = gate + dot(gained, wg[x])
            up = up + dot(gained, wu[x])
            score = score + lax.dot_general(
                gained, wr[:, x * 2 * width : (x + 1) * 2 * width], contract_last, preferred_element_type=f32
            )

        scale = lax.rsqrt(jnp.sum(square_sum, axis=1, keepdims=True) * (1.0 / (8 * width)) + epsilon)
        affinity = 1.0 / (1.0 + jnp.exp(-score * scale))
        chosen = affinity * marks[:, side].reshape(affinity.shape).astype(f32)
        expert = iota(affinity.shape, 1)
        mine = jnp.sum(jnp.where(expert == lax.axis_index("ep"), chosen, 0.0), axis=1, keepdims=True)
        weight = route_scale * mine / jnp.sum(chosen, axis=1, keepdims=True)
        gate = gate * scale
        hidden = gate / (1.0 + jnp.exp(-gate)) * (up * scale) * weight
        act[:, side] = hidden.astype(bf16).reshape(8, half, hidden.shape[1])

    products(core)
    for copy in to_core:
        copy.wait_recv()

    rank_copies = []
    for slab in range(8):
        for side in range(2):
            rank_copies.append(
                pltpu.make_async_copy(
                    tokens.at[slab // 2, slab % 2 * 2 + me["z"] % 2, me["y"], side],
                    attended.at[pl.ds(side * half, half), pl.ds(slab * width, width)],
                    load_sem.at[32 + 2 * slab + side],
                )
            )
            rank_copies[-1].start()
    products(other)

    def down(p, column_half):
        first, count = out_cols[p]
        quarters = []
        for quarter in range(2):
            start = pl.multiple_of(column_half * (2 * unit_cols) + quarter * unit_cols + first, 128)
            quarters.append(
                dot(act[...].reshape(8 * slots, act.shape[3]), wd[:, pl.ds(start, count)])
                .reshape(2, 4, 4, 2, 8, count)
            )
        both = jnp.concatenate(quarters, axis=4).astype(jnp.bfloat16)
        for zl in range(2):
            for y in range(4):
                for zh in range(2):
                    partial[column_half, :, zh * 2 + zl, y, :, pl.ds(first, count)] = both[zl, y, :, zh]

    rest = [tuple(a for a in AXES if a != order[2]) for order in ORDERS]
    from_core = [{} for p in pieces]

    def own(p, where):
        return pick(partial.at[core], where, (slice(None), pl.ds(*out_cols[p])))

    def landing(ref, p, where):
        return pick(ref, where, (slice(None), pl.ds(0, out_cols[p][1])), rest[p])

    def share_sum(p, name, last):
        where, tail = {ORDERS[p][2]: last}, (slice(None), pl.ds(*out_cols[p]))
        from_core[p][name] = copies.start(
            pick(partial.at[other], where, tail), pick(core_partial, where, tail), sibling
        )

    def take_sum(p, name, last):
        from_core[p][name].wait_recv()
        where, tail = {ORDERS[p][2]: last}, (slice(None), pl.ds(*out_cols[p]))
        mine = own(p, where)
        mine[...] = (mine[...].astype(f32) + pick(core_partial, where, tail)[...].astype(f32)).astype(bf16)

    for p in pieces:
        down(p, other)
        share_sum(p, "across", across[p])
    for p in pieces:
        share_sum(p, "after", after[p])
        share_sum(p, "before", before[p])
    for p in pieces:
        share_sum(p, "here", here[p])
    far, near_sums = [], []
    for p, (first, second, last) in enumerate(ORDERS):
        down(p, core)
        take_sum(p, "across", across[p])
        one, two = {second: pl.ds(0, 2)}, {second: pl.ds(2, 2)}
        far.append(
            (
                copies.start(own(p, {last: across[p], **one}), landing(far_parts.at[p], p, one), rights[p]),
                copies.start(own(p, {last: across[p], **two}), landing(far_parts.at[p], p, two), lefts[p]),
            )
        )
    for p, (first, second, last) in enumerate(ORDERS):
        one, two = {second: pl.ds(0, 2)}, {second: pl.ds(2, 2)}
        take_sum(p, "after", after[p])
        right_b = copies.start(own(p, {last: after[p], **two}), landing(near_parts.at[p, 0], p, two), rights[p])
        take_sum(p, "before", before[p])
        left_a = copies.start(own(p, {last: before[p], **one}), landing(near_parts.at[p, 1], p, one), lefts[p])
        near_sums.append([right_b, left_a])
    for p, (first, second, last) in enumerate(ORDERS):
        for side, (at, span, to) in enumerate(
            ((after[p], pl.ds(0, 2), rights[p]), (before[p], pl.ds(2, 2), lefts[p]))
        ):
            far[p][side].wait_recv()
            mine = own(p, {last: at, second: span})
            came = landing(far_parts.at[p], p, {second: span})
            mine[...] = (mine[...].astype(f32) + came[...].astype(f32)).astype(bf16)
            near_sums[p].append(copies.start(mine, landing(near_parts.at[p, side], p, {second: span}), to))
    for p in pieces:
        take_sum(p, "here", here[p])

    phase_two = {}
    for p, (first, second, last) in enumerate(ORDERS):
        cols = pl.ds(*out_cols[p])
        width_p = out_cols[p][1]
        tail = (slice(None), pl.ds(0, width_p))
        for copy in near_sums[p]:
            copy.wait_recv()
        total = own(p, {last: here[p]})[...].astype(f32)
        for side in range(2):
            total = total + near_parts[p, side, :, :, :, pl.ds(0, width_p)].astype(jnp.float32)
        sums_two[p, :, :, :, pl.ds(0, width_p)] = total.astype(jnp.bfloat16)
        phase_two[p] = []
        for k in (1, 3, 2):
            to = moved(me, second, k)
            phase_two[p].append(
                copies.start(
                    pick(sums_two.at[p], {second: to[second]}, tail, rest[p]),
                    parts_two.at[p, k - 1, :, :, pl.ds(0, width_p)],
                    device(to, core),
                )
            )
    phase_three = {}
    for p, (first, second, last) in enumerate(ORDERS):
        width_p = out_cols[p][1]
        tail = (slice(None), pl.ds(0, width_p))
        for copy in phase_two[p]:
            copy.wait_recv()
        total = pick(sums_two.at[p], {second: me[second]}, tail, rest[p])[...].astype(jnp.float32)
        for k in range(3):
            total = total + parts_two[p, k, :, :, pl.ds(0, width_p)].astype(jnp.float32)
        sums_three[p, :, :, pl.ds(0, width_p)] = total.astype(jnp.bfloat16)
        phase_three[p] = []
        for k in (1, 3, 2):
            to = moved(me, first, k)
            phase_three[p].append(
                copies.start(
                    sums_three.at[p, to[first], :, pl.ds(0, width_p)],
                    parts_three.at[p, k - 1, :, pl.ds(0, width_p)],
                    device(to, core),
                )
            )
    for p, (first, second, last) in enumerate(ORDERS):
        width_p = out_cols[p][1]
        for copy in phase_three[p]:
            copy.wait_recv()
        total = sums_three[p, me[first], :, pl.ds(0, width_p)].astype(jnp.float32)
        for k in range(3):
            total = total + parts_three[p, k, :, pl.ds(0, width_p)].astype(jnp.float32)
        final_half[0, :, pl.ds(*out_cols[p])] = total.astype(jnp.bfloat16)
    last_copy = copies.start(final_half.at[0], final_half.at[1], sibling)
    last_copy.wait_recv()
    for side, column_half in enumerate((core, other)):
        both = final_half[side].astype(f32)
        for quarter in range(2):
            eight = both[quarter * 8 : quarter * 8 + 8]
            own = jnp.where(core == 0, eight[0:4], eight[4:8])
            start = pl.multiple_of(column_half * (2 * unit_cols) + quarter * unit_cols, 128)
            mixed[:, pl.ds(start, unit_cols)] = own.astype(bf16)
    for copy in rank_copies:
        copy.wait()
    copies.finish()


def run_decode(
    queries, plan, lengths, routes, gain, cache_latent, cache_rope, w_absorb, w_out, router, w_gate, w_up, w_down
):
    slots = queries.shape[0]
    cap, latent_width = cache_latent.shape[1:]
    rope_width = cache_rope.shape[2]
    heads = w_absorb.shape[0]
    heads_width = w_out.shape[0]
    model = w_out.shape[1]
    width = model // 8
    half = slots // 2
    hidden = w_gate.shape[1]
    experts = router.shape[1]
    rows = 8 * slots
    unit_cols = model // 4
    share = (unit_cols // 128 * 5 + 6) // 14 * 128
    bf16, f32 = jnp.bfloat16, jnp.float32
    vmem = pl.BlockSpec(memory_space=pltpu.VMEM)
    hbm = pl.BlockSpec(memory_space=pl.ANY)
    return pl.pallas_call(
        decode_kernel,
        out_shape=(
            jax.ShapeDtypeStruct((slots, model), bf16),
            jax.ShapeDtypeStruct((4, model), bf16),
        ),
        in_specs=[vmem] * 3 + [hbm] * 10,
        out_specs=(hbm, vmem),
        scratch_shapes=[
            pltpu.VMEM(queries.shape, bf16),
            pltpu.VMEM((4, 1, 2 * width), f32),
            pltpu.VMEM((slots * cap, latent_width), bf16),
            pltpu.VMEM((slots, rope_width, cap), bf16),
            pltpu.VMEM((slots // 16, rope_width, 16 * cap), bf16),
            pltpu.VMEM(w_absorb.shape, bf16),
            pltpu.VMEM((heads, slots, latent_width), bf16),
            pltpu.VMEM((heads, slots, rope_width), bf16),
            pltpu.VMEM((8, 16, latent_width + 128), bf16),
            pltpu.VMEM((8, 16, latent_width + 128), bf16),
            pltpu.VMEM((2, half, experts), bf16),
            pltpu.VMEM((8, 2, half, experts), bf16),
            pltpu.VMEM((heads, slots, latent_width), bf16),
            pltpu.VMEM((slots, heads_width), bf16),
            pltpu.VMEM((16, heads_width), bf16),
            pltpu.VMEM((8, 16, heads_width), bf16),
            pltpu.VMEM((heads_width, model), bf16),
            pltpu.VMEM((experts, model), bf16),
            pltpu.VMEM((4, 2 * width, hidden), bf16),
            pltpu.VMEM((4, 2 * width, hidden), bf16),
            pltpu.VMEM((hidden, model), bf16),
            pltpu.VMEM((8, 2, half, width), bf16),
            pltpu.VMEM((8, half, width), bf16),
            pltpu.VMEM((7, half, width), bf16),
            pltpu.VMEM((4, 4, 4, 2, half, width), bf16),
            pltpu.VMEM((8, 2, half, hidden), bf16),
            pltpu.VMEM((2, 4, 4, 4, 16, unit_cols), bf16),
            pltpu.VMEM((4, 4, 4, 16, unit_cols), bf16),
            pltpu.VMEM((3, 4, 4, 16, share), bf16),
            pltpu.VMEM((3, 2, 4, 4, 16, share), bf16),
            pltpu.VMEM((3, 4, 4, 16, share), bf16),
            pltpu.VMEM((3, 3, 4, 16, share), bf16),
            pltpu.VMEM((3, 4, 16, share), bf16),
            pltpu.VMEM((3, 3, 16, share), bf16),
            pltpu.VMEM((2, 16, unit_cols), bf16),
            pltpu.SemaphoreType.DMA((56,)),
            pltpu.SemaphoreType.DMA((160,)),
            pltpu.SemaphoreType.DMA((160,)),
        ],
        compiler_params=pltpu.CompilerParams(
            collective_id=0, has_side_effects=True, vmem_limit_bytes=60 * 1024 * 1024
        ),
        name="decode",
    )(
        plan,
        lengths,
        routes.T,
        queries,
        gain.reshape(4, 1, 2 * width),
        cache_latent.reshape(slots * cap, latent_width),
        cache_rope.transpose(0, 2, 1),
        w_absorb,
        w_out,
        router.T,
        w_gate.reshape(4, 2 * width, hidden),
        w_up.reshape(4, 2 * width, hidden),
        w_down,
    )


def copy_kernel(source, small_source, target, small_target, held, small_held, sems):
    parts = held.shape[0]
    width = source.shape[1] // parts
    small_in = pltpu.make_async_copy(small_source, small_held, sems.at[2 * parts])
    small_in.start()
    copies_in, copies_out = [], []
    for k in range(parts):
        columns = pl.ds(k * width, width)
        copies_in.append(pltpu.make_async_copy(source.at[:, columns], held.at[k], sems.at[k]))
        copies_out.append(pltpu.make_async_copy(held.at[k], target.at[:, columns], sems.at[parts + k]))
        copies_in[-1].start()
    small_in.wait()
    small_out = pltpu.make_async_copy(small_held, small_target, sems.at[2 * parts + 1])
    small_out.start()
    for copy_in, copy_out in zip(copies_in, copies_out):
        copy_in.wait()
        copy_out.start()
    for copy in copies_out:
        copy.wait()
    small_out.wait()


def write_out(attended, mixed):
    hbm = pl.BlockSpec(memory_space=pl.ANY)
    parts = 4
    return pl.pallas_call(
        copy_kernel,
        out_shape=(
            jax.ShapeDtypeStruct(attended.shape, attended.dtype),
            jax.ShapeDtypeStruct(mixed.shape, mixed.dtype),
        ),
        in_specs=[hbm, hbm],
        out_specs=(hbm, hbm),
        scratch_shapes=[
            pltpu.VMEM((parts, attended.shape[0], attended.shape[1] // parts), attended.dtype),
            pltpu.VMEM(mixed.shape, mixed.dtype),
            pltpu.SemaphoreType.DMA((2 * parts + 2,)),
        ],
        compiler_params=pltpu.CompilerParams(vmem_limit_bytes=60 * 1024 * 1024),
        name="write_out",
    )(attended, mixed)


def per_device(
    queries,
    cache_latent,
    cache_rope,
    cache_len,
    move_plan,
    w_absorb,
    w_out,
    norm_gain,
    router,
    routes,
    w_gate,
    w_up,
    w_down,
):
    slots = cache_len.shape[0]
    attended, mixed = run_decode(
        queries,
        move_plan.reshape(1, -1),
        cache_len.reshape(1, slots),
        routes,
        norm_gain,
        cache_latent,
        cache_rope,
        w_absorb,
        w_out,
        router,
        w_gate[0],
        w_up[0],
        w_down[0],
    )
    return write_out(attended, mixed)


def solution(mesh):
    in_specs = (
        P("dp", "ep"),
        P("dp", None, None),
        P("dp", None, None),
        P("dp"),
        P(),
        P("ep", None, None),
        P("ep", None),
        P(),
        P(),
        P("dp", None),
        P("ep", None, "dp"),
        P("ep", None, "dp"),
        P("ep", "dp", None),
    )
    out_specs = (P("dp", None), P(("dp", "ep"), None))
    return jax.shard_map(
        per_device, mesh=mesh, in_specs=in_specs, out_specs=out_specs, check_vma=False
    )
```

```python
import jax
import jax.numpy as jnp
from jax import lax
from jax.experimental import pallas as pl
from jax.experimental.pallas import tpu as pltpu
from jax.sharding import PartitionSpec as P

VDIM = 128

epsilon = 1e-06
route_scale = 2.5


MESH = pl.DeviceIdType.MESH
AXES = ("x", "z", "y")
ORDERS = (("y", "z", "x"), ("z", "x", "y"), ("x", "y", "z"))


def coordinates():
    dp, ep = lax.axis_index("dp"), lax.axis_index("ep")
    me = {"x": ep // 4, "z": (ep // 2) % 2 * 2 + dp // 4, "y": dp % 4}
    return me, ep % 2


def device(at, core):
    return ((at["z"] % 2) * 4 + at["y"], at["x"] * 4 + at["z"] // 2 * 2 + core)


def moved(me, axis, offset):
    return {**me, axis: (me[axis] + offset) % 4}


def pick(ref, where, tail=(), axes=AXES):
    return ref.at[tuple(where.get(a, slice(None)) for a in axes) + tuple(tail)]


class Copies:
    def __init__(self, send, recv):
        self.send, self.recv, self.used, self.sent = send, recv, 0, []

    def start(self, src, dst, to):
        copy = pltpu.make_async_remote_copy(
            src_ref=src,
            dst_ref=dst,
            send_sem=self.send.at[self.used],
            recv_sem=self.recv.at[self.used],
            device_id=to,
            device_id_type=MESH,
        )
        copy.start()
        self.used += 1
        self.sent.append(copy)
        return copy

    def finish(self):
        for copy in self.sent:
            copy.wait_send()


def decode_kernel(
    plan,
    lengths,
    routes,
    queries_in,
    gain_in,
    cache_latent,
    cache_rope,
    w_absorb,
    w_out,
    router,
    w_gate,
    w_up,
    w_down,
    attended,
    mixed,
    queries,
    gain,
    keys,
    rope_keys,
    rotary,
    wa,
    query_latent,
    query_rope,
    query_out,
    query_in,
    marks_out,
    marks,
    latent_out,
    values,
    places,
    logits,
    act_source,
    rank_rows,
    wo,
    wr,
    wg,
    wu,
    wd,
    terms,
    core_terms,
    slab_terms,
    tokens,
    act,
    partial,
    core_partial,
    far_parts,
    near_parts,
    sums_two,
    parts_two,
    sums_three,
    parts_three,
    final_half,
    load_sem,
    send_sem,
    recv_sem,
):
    me, core = coordinates()
    other = 1 - core
    sibling = device(me, other)
    copies = Copies(send_sem, recv_sem)
    width = wg.shape[1] // 2
    slots, heads = queries.shape[0], wa.shape[0]
    latent_width, rope_width = keys.shape[1], rope_keys.shape[1]
    cap = keys.shape[0] // slots
    half = slots // 2
    tiles = width // 128
    wide = (tiles * 5 + 6) // 7 * 128
    piece_rows = ((0, half // 2), (half // 2, half // 2), (0, half))
    piece_cols = ((0, wide), (0, wide), (wide, width - wide))
    unit_cols = partial.shape[-1]
    share = (unit_cols // 128 * 5 + 6) // 14 * 128
    out_cols = ((0, share), (share, share), (2 * share, unit_cols - 2 * share))

    slab_offsets = [(dx, dz) for dx in range(4) for dz in range(2) if (dx, dz) != (0, 0)]

    def slab_chip(dx, dz):
        return {**me, "x": (me["x"] + dx) % 4, "z": (me["z"] + 2 * dz) % 4}

    def slab_index(chip):
        return chip["x"] * 2 + chip["z"] // 2

    order = slab_offsets + [(0, 0)]
    slabs = [slab_index(slab_chip(dx, dz)) for dx, dz in order]

    def columns(slab):
        return pl.ds(pl.multiple_of(slab * width, 128), width)

    peers = [sibling]
    for axis in AXES:
        peers += [device(moved(me, axis, k), core) for k in (1, 2, 3)]
    peers += [device(slab_chip(dx, 1), core) for dx in (1, 2, 3)]
    rank_offsets = [(dz, dy) for dz in range(2) for dy in range(4) if (dz, dy) != (0, 0)]

    def rank_chip(dz, dy):
        z = me["z"] // 2 * 2 + (me["z"] + dz) % 2
        return {**me, "z": z, "y": (me["y"] + dy) % 4}

    peers += [device(rank_chip(1, dy), core) for dy in (1, 2, 3)]
    barrier = pltpu.get_barrier_semaphore()
    for peer in peers:
        pl.semaphore_signal(barrier, inc=1, device_id=peer, device_id_type=MESH)

    query_load = pltpu.make_async_copy(queries_in, queries, load_sem.at[50])
    query_load.start()
    gain_load = pltpu.make_async_copy(gain_in, gain, load_sem.at[51])
    loads = []
    group = 16
    group_keys = group * cap
    groups = slots // group
    cache_loads = []
    for g in range(groups):
        rows = pl.ds(g * group_keys, group_keys)
        cache_loads.append(
            (
                pltpu.make_async_copy(cache_latent.at[rows], keys.at[rows], load_sem.at[20 + 2 * g]),
                pltpu.make_async_copy(
                    cache_rope.at[pl.ds(g * group, group)], rope_keys.at[pl.ds(g * group, group)], load_sem.at[21 + 2 * g]
                ),
            )
        )
        for load in cache_loads[-1]:
            load.start()
    absorb_load = pltpu.make_async_copy(w_absorb, wa, load_sem.at[28])
    absorb_load.start()
    for k, slab in enumerate(slabs):
        loads.append(
            pltpu.make_async_copy(w_out.at[:, columns(slab)], wo.at[:, columns(slab)], load_sem.at[k])
        )
    for k, (source, target) in enumerate(((w_gate, wg), (w_up, wu), (router, wr), (w_down, wd))):
        loads.append(pltpu.make_async_copy(source, target, load_sem.at[8 + k]))
    loads.append(gain_load)
    for load in loads:
        load.start()

    f32, bf16 = jnp.float32, jnp.bfloat16
    my_rank = lax.axis_index("dp")

    def iota(shape, axis):
        return lax.broadcasted_iota(jnp.int32, shape, axis)

    def mark(condition):
        return jnp.where(condition, 1.0, 0.0)

    def dot(a, b):
        return jnp.dot(a, b, preferred_element_type=f32)

    shift = slots.bit_length() - 1
    sources = jnp.concatenate([plan[:, r * slots : (r + 1) * slots] for r in range(8)], axis=0)
    rank_of, slot_of = sources >> shift, sources & (slots - 1)
    rank_row = iota((8, slots), 0)
    earlier = mark(iota((slots, slots), 0) < iota((slots, slots), 1)).astype(bf16)
    own_rank = jnp.sum(jnp.where(rank_row == my_rank, rank_of, 0).astype(f32), axis=0, keepdims=True)
    leaving = mark((own_rank == rank_row.astype(f32)) & (rank_row != my_rank))
    letter = jnp.sum(leaving * dot(leaving.astype(bf16), earlier), axis=0, keepdims=True)
    away = jnp.sum(leaving, axis=0, keepdims=True)
    key_row = jnp.where(away > 0.5, own_rank * 2.0 + letter, -1.0)
    diagonal = iota((slots, slots), 0) == iota((slots, slots), 1)
    key = jnp.sum(jnp.where(diagonal, key_row, 0.0), axis=1, keepdims=True).astype(jnp.int32)
    stays = key < 0
    length = jnp.sum(jnp.where(diagonal, lengths[...].astype(f32), 0.0), axis=1, keepdims=True).astype(jnp.int32)

    arriving = mark((rank_of == my_rank) & (rank_row != my_rank))
    nth = dot(arriving.astype(bf16), earlier)
    guest_slot = []
    for k in range(2):
        is_kth = (arriving > 0.5) & (jnp.abs(nth - k) < 0.5)
        guest_slot.append(jnp.sum(jnp.where(is_kth, slot_of + 1, 0).astype(f32), axis=1, keepdims=True) - 1.0)

    def letter_places(axis, shape):
        place = iota(shape, axis)
        inner = place & 15
        return place >> 4, inner >> 1, inner & 1, inner < 2 * heads

    query_load.wait()
    for h in range(heads):
        start = h * (latent_width + rope_width)
        query_latent[h] = queries[:, start : start + latent_width]
        query_rope[h] = queries[:, start + latent_width : start + latent_width + rope_width]

    to_rank, to_head, to_letter, used = letter_places(0, (128, slots))
    wanted = jnp.where(used, to_rank * 2 + to_letter, -2).astype(f32)
    chosen = mark(key_row == wanted)
    out_latent = jnp.zeros((128, latent_width), f32)
    out_rope = jnp.zeros((128, rope_width), f32)
    for h in range(heads):
        rows = jnp.where(to_head == h, chosen, 0.0).astype(bf16)
        out_latent = out_latent + dot(rows, query_latent[h])
        out_rope = out_rope + dot(rows, query_rope[h])
    query_out[:, :, 0:latent_width] = out_latent.astype(bf16).reshape(8, 16, latent_width)
    query_out[:, :, latent_width:] = (
        jnp.concatenate([out_rope, jnp.zeros((128, 128 - rope_width), f32)], axis=1)
        .astype(bf16)
        .reshape(8, 16, 128)
    )
    experts = iota((slots, marks.shape[3]), 1)
    named = jnp.zeros(experts.shape, f32)
    for k in range(routes.shape[0]):
        route = jnp.sum(jnp.where(diagonal, routes[k : k + 1, :], 0).astype(f32), axis=1, keepdims=True)
        named = named + mark(route.astype(jnp.int32) == experts)
    marks_out[...] = named.astype(bf16).reshape(marks_out.shape)
    marks[my_rank] = marks_out[...]
    query_in[my_rank] = jnp.zeros(query_in.shape[1:], bf16)

    pl.semaphore_wait(barrier, len(peers))
    from_ranks = []
    for dz, dy in rank_offsets:
        chip = rank_chip(dz, dy)
        to = device(chip, core)
        from_ranks.append(copies.start(query_out.at[to[0]], query_in.at[my_rank], to))
    from_marks = []
    for dz, dy in rank_offsets:
        from_marks.append(copies.start(marks_out, marks.at[my_rank], device(rank_chip(dz, dy), core)))

    from_rank, from_head, from_letter, used = letter_places(1, (8, 128))
    guests = jnp.where(from_letter == 0, guest_slot[0], guest_slot[1])
    guests = jnp.where((from_rank == iota((8, 128), 0)) & used, guests + 1.0, 0.0)
    guests = jnp.sum(guests, axis=0, keepdims=True) - 1.0
    _, from_head, _, _ = letter_places(1, (slots, 128))
    is_guest = mark(guests == iota((slots, 128), 0).astype(f32))
    for g in range(groups):
        for load in cache_loads[g]:
            load.wait()
    for g in range(groups):
        rotary[g] = jnp.concatenate([rope_keys[g * group + k] for k in range(group)], axis=1)
    for copy in from_ranks:
        copy.wait_recv()
    came = query_in[...].reshape(128, query_in.shape[2])
    for h in range(heads):
        rows = jnp.where(from_head == h, is_guest, 0.0).astype(bf16)
        guest = dot(rows, came)
        query_latent[h] = jnp.where(stays, query_latent[h].astype(f32), guest[:, :latent_width]).astype(bf16)
        query_rope[h] = jnp.where(
            stays, query_rope[h].astype(f32), guest[:, latent_width : latent_width + rope_width]
        ).astype(bf16)

    score_scale = (VDIM + rope_width) ** -0.5
    rows_shape = (heads * group, group_keys)
    position = iota(rows_shape, 1) - iota(rows_shape, 0) % group * cap
    contract_last = (((1,), (1,)), ((), ()))
    for g in range(groups):
        mine = pl.ds(g * group, group)
        q_latent = query_latent[:, mine, :].reshape(heads * group, latent_width)
        q_rope = query_rope[:, mine, :].reshape(heads * group, rope_width)
        here = pl.ds(g * group_keys, group_keys)
        scores = lax.dot_general(q_latent, keys[here, :], contract_last, preferred_element_type=f32)
        scores = scores + dot(q_rope, rotary[g])
        limit = jnp.concatenate([length[g * group : (g + 1) * group]] * heads, axis=0)
        seen = (position >= 0) & (position < limit)
        scores = jnp.where(seen, scores * score_scale, -jnp.inf)
        raised = jnp.exp(scores - jnp.max(scores, axis=1, keepdims=True))
        probs = (raised / jnp.sum(raised, axis=1, keepdims=True)).astype(bf16)
        latent_out[:, mine, :] = dot(probs, keys[here, :]).astype(bf16).reshape(heads, group, latent_width)
    absorb_load.wait()
    for h in range(heads):
        values[:, h * VDIM : (h + 1) * VDIM] = dot(latent_out[h], wa[h]).astype(bf16)

    from_sibling = []
    for load in loads[:8]:
        load.wait()
    for k, slab in enumerate(slabs):
        head_terms = jnp.dot(values[...], wo[:, columns(slab)], preferred_element_type=jnp.float32)
        terms[k] = head_terms.astype(jnp.bfloat16).reshape(2, half, width)
        from_sibling.append(copies.start(terms.at[k, other], core_terms.at[k], sibling))
    from_slabs = []
    for k, (dx, dz) in enumerate(order):
        from_sibling[k].wait_recv()
        total = terms[k, core].astype(jnp.float32) + core_terms[k].astype(jnp.float32)
        if k < len(slab_offsets):
            terms[k, core] = total.astype(jnp.bfloat16)
            from_slabs.append(
                copies.start(terms.at[k, core], slab_terms.at[k], device(slab_chip(dx, dz), core))
            )
    for r in range(8):
        source = jnp.sum(jnp.where(diagonal, sources[r : r + 1, :], 0).astype(f32), axis=1, keepdims=True)
        lanes = iota((slots, 8 * slots), 1)
        places[r] = mark(source.astype(jnp.int32) == lanes).astype(bf16)
    for k, copy in enumerate(from_slabs):
        copy.wait_recv()
        total = total + slab_terms[k].astype(jnp.float32)
    tokens[me["x"], me["z"], me["y"], core] = total.astype(jnp.bfloat16)

    def block(p, where):
        first, count = piece_rows[p]
        return pick(tokens, where, (core, pl.ds(first, count), pl.ds(*piece_cols[p])))

    def spread(p, where, to):
        return copies.start(block(p, where), block(p, where), to)

    pieces = range(3)
    rights = [device(moved(me, order[2], 1), core) for order in ORDERS]
    lefts = [device(moved(me, order[2], 3), core) for order in ORDERS]
    before = [(me[order[2]] + 3) % 4 for order in ORDERS]
    after = [(me[order[2]] + 1) % 4 for order in ORDERS]
    across = [(me[order[2]] + 2) % 4 for order in ORDERS]
    here = [me[order[2]] for order in ORDERS]

    def group_at(p, k, last):
        second = ORDERS[p][1]
        return {second: (me[second] + 4 - k) % 4, ORDERS[p][2]: last}

    one = [
        [spread(p, me, device(moved(me, ORDERS[p][0], k), core)) for k in (1, 3, 2)] for p in pieces
    ]
    two = [{} for p in pieces]
    to_right, to_left = [{} for p in pieces], [{} for p in pieces]
    far, to_core = [[] for p in pieces], []

    def near(p, k):
        where = group_at(p, k, here[p])
        to_right[p][k] = spread(p, where, rights[p])
        to_left[p][k] = spread(p, where, lefts[p])

    for p in pieces:
        for copy in one[p]:
            copy.wait_recv()
        for k in (1, 3, 2):
            two[p][k] = spread(p, group_at(p, 0, here[p]), device(moved(me, ORDERS[p][1], k), core))
        near(p, 0)
    for k in (1, 3):
        for p in pieces:
            two[p][k].wait_recv()
            near(p, k)
    for p in pieces:
        to_right[p][0].wait_recv()
        far[p].append(spread(p, group_at(p, 0, before[p]), rights[p]))
    for p in pieces:
        two[p][2].wait_recv()
        near(p, 2)
        to_core.append(spread(p, {ORDERS[p][2]: here[p]}, sibling))
    for p in pieces:
        to_left[p][3].wait_recv()
        far[p].append(spread(p, group_at(p, 3, after[p]), lefts[p]))
        to_right[p][1].wait_recv()
        far[p].append(spread(p, group_at(p, 1, before[p]), rights[p]))
    for p in pieces:
        to_left[p][2].wait_recv()
        far[p].append(spread(p, group_at(p, 2, after[p]), lefts[p]))
    for p in pieces:
        for k in (3, 2):
            to_right[p][k].wait_recv()
        to_core.append(spread(p, {ORDERS[p][2]: before[p]}, sibling))
        for k in (0, 1):
            to_left[p][k].wait_recv()
        to_core.append(spread(p, {ORDERS[p][2]: after[p]}, sibling))
    for p in pieces:
        for copy in far[p]:
            copy.wait_recv()
        to_core.append(spread(p, {ORDERS[p][2]: across[p]}, sibling))

    for load in loads[8:]:
        load.wait()
    for copy in from_marks:
        copy.wait_recv()

    def products(side):
        square_sum = jnp.zeros((8 * half, 128), f32)
        gate, up, score = 0.0, 0.0, 0.0
        for x in range(4):
            rows = [tokens[x, pl.ds(zh * 2, 2), :, side].reshape(8 * half, width) for zh in range(2)]
            rows = jnp.concatenate(rows, axis=1).astype(f32)
            for k in range(2 * width // 128):
                part = rows[:, k * 128 : (k + 1) * 128]
                square_sum = square_sum + part * part
            gained = (rows * gain[x]).astype(bf16)
            gate = gate + dot(gained, wg[x])
            up = up + dot(gained, wu[x])
            score = score + lax.dot_general(
                gained, wr[:, x * 2 * width : (x + 1) * 2 * width], contract_last, preferred_element_type=f32
            )

        scale = lax.rsqrt(jnp.sum(square_sum, axis=1, keepdims=True) * (1.0 / (8 * width)) + epsilon)
        score = score * scale
        high = score.astype(bf16)
        low = (score - high.astype(f32)).astype(bf16)
        logits[:, side] = jnp.concatenate([high, low], axis=1).reshape(8, half, 2 * score.shape[1])
        gate = gate * scale
        hidden = gate / (1.0 + jnp.exp(-gate)) * (up * scale)
        act_source[:, side] = hidden.astype(bf16).reshape(8, half, hidden.shape[1])

    products(core)
    for copy in to_core:
        copy.wait_recv()

    products(other)

    all_places = places[...].reshape(8 * slots, 8 * slots)
    experts = marks.shape[3]
    pair = dot(all_places, logits[...].reshape(8 * slots, 2 * experts))
    affinity = 1.0 / (1.0 + jnp.exp(-(pair[:, :experts] + pair[:, experts:])))
    chosen = affinity * marks[...].reshape(affinity.shape).astype(f32)
    mine = jnp.where(iota(affinity.shape, 1) == lax.axis_index("ep"), chosen, 0.0)
    weight = route_scale * jnp.sum(mine, axis=1, keepdims=True) / jnp.sum(chosen, axis=1, keepdims=True)
    moved_act = dot(all_places, act_source[...].reshape(8 * slots, act.shape[3])) * weight
    act[...] = moved_act.astype(bf16).reshape(act.shape)

    def down(p, column_half):
        first, count = out_cols[p]
        quarters = []
        for quarter in range(2):
            start = pl.multiple_of(column_half * (2 * unit_cols) + quarter * unit_cols + first, 128)
            quarters.append(
                dot(act[...].reshape(8 * slots, act.shape[3]), wd[:, pl.ds(start, count)])
                .reshape(2, 4, 4, 2, 8, count)
            )
        both = jnp.concatenate(quarters, axis=4).astype(jnp.bfloat16)
        for zl in range(2):
            for y in range(4):
                for zh in range(2):
                    partial[column_half, :, zh * 2 + zl, y, :, pl.ds(first, count)] = both[zl, y, :, zh]

    rest = [tuple(a for a in AXES if a != order[2]) for order in ORDERS]
    from_core = [{} for p in pieces]

    def own(p, where):
        return pick(partial.at[core], where, (slice(None), pl.ds(*out_cols[p])))

    def landing(ref, p, where):
        return pick(ref, where, (slice(None), pl.ds(0, out_cols[p][1])), rest[p])

    def share_sum(p, name, last):
        where, tail = {ORDERS[p][2]: last}, (slice(None), pl.ds(*out_cols[p]))
        from_core[p][name] = copies.start(
            pick(partial.at[other], where, tail), pick(core_partial, where, tail), sibling
        )

    def take_sum(p, name, last):
        from_core[p][name].wait_recv()
        where, tail = {ORDERS[p][2]: last}, (slice(None), pl.ds(*out_cols[p]))
        mine = own(p, where)
        mine[...] = (mine[...].astype(f32) + pick(core_partial, where, tail)[...].astype(f32)).astype(bf16)

    for p in pieces:
        down(p, other)
        share_sum(p, "across", across[p])
    for p in pieces:
        share_sum(p, "after", after[p])
        share_sum(p, "before", before[p])
    for p in pieces:
        share_sum(p, "here", here[p])
    far, near_sums = [], []
    for p, (first, second, last) in enumerate(ORDERS):
        down(p, core)
        take_sum(p, "across", across[p])
        one, two = {second: pl.ds(0, 2)}, {second: pl.ds(2, 2)}
        far.append(
            (
                copies.start(own(p, {last: across[p], **one}), landing(far_parts.at[p], p, one), rights[p]),
                copies.start(own(p, {last: across[p], **two}), landing(far_parts.at[p], p, two), lefts[p]),
            )
        )
    for p, (first, second, last) in enumerate(ORDERS):
        one, two = {second: pl.ds(0, 2)}, {second: pl.ds(2, 2)}
        take_sum(p, "after", after[p])
        right_b = copies.start(own(p, {last: after[p], **two}), landing(near_parts.at[p, 0], p, two), rights[p])
        take_sum(p, "before", before[p])
        left_a = copies.start(own(p, {last: before[p], **one}), landing(near_parts.at[p, 1], p, one), lefts[p])
        near_sums.append([right_b, left_a])

    rank_copies = []
    for slab in range(8):
        rows = tokens[slab // 2, pl.ds(slab % 2 * 2, 2)].reshape(8 * slots, width)
        rank_rows[slab] = dot(places[my_rank], rows).astype(bf16)
    for slab in range(8):
        rank_copies.append(
            pltpu.make_async_copy(
                rank_rows.at[slab], attended.at[:, pl.ds(slab * width, width)], load_sem.at[12 + slab]
            )
        )
        rank_copies[-1].start()

    for p, (first, second, last) in enumerate(ORDERS):
        for side, (at, span, to) in enumerate(
            ((after[p], pl.ds(0, 2), rights[p]), (before[p], pl.ds(2, 2), lefts[p]))
        ):
            far[p][side].wait_recv()
            mine = own(p, {last: at, second: span})
            came = landing(far_parts.at[p], p, {second: span})
            mine[...] = (mine[...].astype(f32) + came[...].astype(f32)).astype(bf16)
            near_sums[p].append(copies.start(mine, landing(near_parts.at[p, side], p, {second: span}), to))
    for p in pieces:
        take_sum(p, "here", here[p])

    phase_two = {}
    for p, (first, second, last) in enumerate(ORDERS):
        cols = pl.ds(*out_cols[p])
        width_p = out_cols[p][1]
        tail = (slice(None), pl.ds(0, width_p))
        for copy in near_sums[p]:
            copy.wait_recv()
        total = own(p, {last: here[p]})[...].astype(f32)
        for side in range(2):
            total = total + near_parts[p, side, :, :, :, pl.ds(0, width_p)].astype(jnp.float32)
        sums_two[p, :, :, :, pl.ds(0, width_p)] = total.astype(jnp.bfloat16)
        phase_two[p] = []
        for k in (1, 3, 2):
            to = moved(me, second, k)
            phase_two[p].append(
                copies.start(
                    pick(sums_two.at[p], {second: to[second]}, tail, rest[p]),
                    parts_two.at[p, k - 1, :, :, pl.ds(0, width_p)],
                    device(to, core),
                )
            )
    phase_three = {}
    for p, (first, second, last) in enumerate(ORDERS):
        width_p = out_cols[p][1]
        tail = (slice(None), pl.ds(0, width_p))
        for copy in phase_two[p]:
            copy.wait_recv()
        total = pick(sums_two.at[p], {second: me[second]}, tail, rest[p])[...].astype(jnp.float32)
        for k in range(3):
            total = total + parts_two[p, k, :, :, pl.ds(0, width_p)].astype(jnp.float32)
        sums_three[p, :, :, pl.ds(0, width_p)] = total.astype(jnp.bfloat16)
        phase_three[p] = []
        for k in (1, 3, 2):
            to = moved(me, first, k)
            phase_three[p].append(
                copies.start(
                    sums_three.at[p, to[first], :, pl.ds(0, width_p)],
                    parts_three.at[p, k - 1, :, pl.ds(0, width_p)],
                    device(to, core),
                )
            )
    for p, (first, second, last) in enumerate(ORDERS):
        width_p = out_cols[p][1]
        for copy in phase_three[p]:
            copy.wait_recv()
        total = sums_three[p, me[first], :, pl.ds(0, width_p)].astype(jnp.float32)
        for k in range(3):
            total = total + parts_three[p, k, :, pl.ds(0, width_p)].astype(jnp.float32)
        final_half[0, :, pl.ds(*out_cols[p])] = total.astype(jnp.bfloat16)
    last_copy = copies.start(final_half.at[0], final_half.at[1], sibling)
    last_copy.wait_recv()
    for side, column_half in enumerate((core, other)):
        both = final_half[side].astype(f32)
        for quarter in range(2):
            eight = both[quarter * 8 : quarter * 8 + 8]
            own = jnp.where(core == 0, eight[0:4], eight[4:8])
            start = pl.multiple_of(column_half * (2 * unit_cols) + quarter * unit_cols, 128)
            mixed[:, pl.ds(start, unit_cols)] = own.astype(bf16)
    for copy in rank_copies:
        copy.wait()
    copies.finish()


def run_decode(
    queries, plan, lengths, routes, gain, cache_latent, cache_rope, w_absorb, w_out, router, w_gate, w_up, w_down
):
    slots = queries.shape[0]
    cap, latent_width = cache_latent.shape[1:]
    rope_width = cache_rope.shape[2]
    heads = w_absorb.shape[0]
    heads_width = w_out.shape[0]
    model = w_out.shape[1]
    width = model // 8
    half = slots // 2
    hidden = w_gate.shape[1]
    experts = router.shape[1]
    rows = 8 * slots
    unit_cols = model // 4
    share = (unit_cols // 128 * 5 + 6) // 14 * 128
    bf16, f32 = jnp.bfloat16, jnp.float32
    vmem = pl.BlockSpec(memory_space=pltpu.VMEM)
    hbm = pl.BlockSpec(memory_space=pl.ANY)
    return pl.pallas_call(
        decode_kernel,
        out_shape=(
            jax.ShapeDtypeStruct((slots, model), bf16),
            jax.ShapeDtypeStruct((4, model), bf16),
        ),
        in_specs=[vmem] * 3 + [hbm] * 10,
        out_specs=(hbm, vmem),
        scratch_shapes=[
            pltpu.VMEM(queries.shape, bf16),
            pltpu.VMEM((4, 1, 2 * width), f32),
            pltpu.VMEM((slots * cap, latent_width), bf16),
            pltpu.VMEM((slots, rope_width, cap), bf16),
            pltpu.VMEM((slots // 16, rope_width, 16 * cap), bf16),
            pltpu.VMEM(w_absorb.shape, bf16),
            pltpu.VMEM((heads, slots, latent_width), bf16),
            pltpu.VMEM((heads, slots, rope_width), bf16),
            pltpu.VMEM((8, 16, latent_width + 128), bf16),
            pltpu.VMEM((8, 16, latent_width + 128), bf16),
            pltpu.VMEM((2, half, experts), bf16),
            pltpu.VMEM((8, 2, half, experts), bf16),
            pltpu.VMEM((heads, slots, latent_width), bf16),
            pltpu.VMEM((slots, heads_width), bf16),
            pltpu.VMEM((8, slots, rows), bf16),
            pltpu.VMEM((8, 2, half, 2 * experts), bf16),
            pltpu.VMEM((8, 2, half, hidden), bf16),
            pltpu.VMEM((8, slots, width), bf16),
            pltpu.VMEM((heads_width, model), bf16),
            pltpu.VMEM((experts, model), bf16),
            pltpu.VMEM((4, 2 * width, hidden), bf16),
            pltpu.VMEM((4, 2 * width, hidden), bf16),
            pltpu.VMEM((hidden, model), bf16),
            pltpu.VMEM((8, 2, half, width), bf16),
            pltpu.VMEM((8, half, width), bf16),
            pltpu.VMEM((7, half, width), bf16),
            pltpu.VMEM((4, 4, 4, 2, half, width), bf16),
            pltpu.VMEM((8, 2, half, hidden), bf16),
            pltpu.VMEM((2, 4, 4, 4, 16, unit_cols), bf16),
            pltpu.VMEM((4, 4, 4, 16, unit_cols), bf16),
            pltpu.VMEM((3, 4, 4, 16, share), bf16),
            pltpu.VMEM((3, 2, 4, 4, 16, share), bf16),
            pltpu.VMEM((3, 4, 4, 16, share), bf16),
            pltpu.VMEM((3, 3, 4, 16, share), bf16),
            pltpu.VMEM((3, 4, 16, share), bf16),
            pltpu.VMEM((3, 3, 16, share), bf16),
            pltpu.VMEM((2, 16, unit_cols), bf16),
            pltpu.SemaphoreType.DMA((56,)),
            pltpu.SemaphoreType.DMA((160,)),
            pltpu.SemaphoreType.DMA((160,)),
        ],
        compiler_params=pltpu.CompilerParams(
            collective_id=0, has_side_effects=True, vmem_limit_bytes=60 * 1024 * 1024
        ),
        name="decode",
    )(
        plan,
        lengths,
        routes.T,
        queries,
        gain.reshape(4, 1, 2 * width),
        cache_latent.reshape(slots * cap, latent_width),
        cache_rope.transpose(0, 2, 1),
        w_absorb,
        w_out,
        router.T,
        w_gate.reshape(4, 2 * width, hidden),
        w_up.reshape(4, 2 * width, hidden),
        w_down,
    )


def copy_kernel(source, small_source, target, small_target, held, small_held, sems):
    parts = held.shape[0]
    width = source.shape[1] // parts
    small_in = pltpu.make_async_copy(small_source, small_held, sems.at[2 * parts])
    small_in.start()
    copies_in, copies_out = [], []
    for k in range(parts):
        columns = pl.ds(k * width, width)
        copies_in.append(pltpu.make_async_copy(source.at[:, columns], held.at[k], sems.at[k]))
        copies_out.append(pltpu.make_async_copy(held.at[k], target.at[:, columns], sems.at[parts + k]))
        copies_in[-1].start()
    small_in.wait()
    small_out = pltpu.make_async_copy(small_held, small_target, sems.at[2 * parts + 1])
    small_out.start()
    for copy_in, copy_out in zip(copies_in, copies_out):
        copy_in.wait()
        copy_out.start()
    for copy in copies_out:
        copy.wait()
    small_out.wait()


def write_out(attended, mixed):
    hbm = pl.BlockSpec(memory_space=pl.ANY)
    parts = 4
    return pl.pallas_call(
        copy_kernel,
        out_shape=(
            jax.ShapeDtypeStruct(attended.shape, attended.dtype),
            jax.ShapeDtypeStruct(mixed.shape, mixed.dtype),
        ),
        in_specs=[hbm, hbm],
        out_specs=(hbm, hbm),
        scratch_shapes=[
            pltpu.VMEM((parts, attended.shape[0], attended.shape[1] // parts), attended.dtype),
            pltpu.VMEM(mixed.shape, mixed.dtype),
            pltpu.SemaphoreType.DMA((2 * parts + 2,)),
        ],
        compiler_params=pltpu.CompilerParams(vmem_limit_bytes=60 * 1024 * 1024),
        name="write_out",
    )(attended, mixed)


def per_device(
    queries,
    cache_latent,
    cache_rope,
    cache_len,
    move_plan,
    w_absorb,
    w_out,
    norm_gain,
    router,
    routes,
    w_gate,
    w_up,
    w_down,
):
    slots = cache_len.shape[0]
    attended, mixed = run_decode(
        queries,
        move_plan.reshape(1, -1),
        cache_len.reshape(1, slots),
        routes,
        norm_gain,
        cache_latent,
        cache_rope,
        w_absorb,
        w_out,
        router,
        w_gate[0],
        w_up[0],
        w_down[0],
    )
    return write_out(attended, mixed)


def solution(mesh):
    in_specs = (
        P("dp", "ep"),
        P("dp", None, None),
        P("dp", None, None),
        P("dp"),
        P(),
        P("ep", None, None),
        P("ep", None),
        P(),
        P(),
        P("dp", None),
        P("ep", None, "dp"),
        P("ep", None, "dp"),
        P("ep", "dp", None),
    )
    out_specs = (P("dp", None), P(("dp", "ep"), None))
    return jax.shard_map(
        per_device, mesh=mesh, in_specs=in_specs, out_specs=out_specs, check_vma=False
    )
```

```python
import jax
import jax.numpy as jnp
from jax import lax
from jax.experimental import pallas as pl
from jax.experimental.pallas import tpu as pltpu
from jax.sharding import PartitionSpec as P

VDIM = 128

epsilon = 1e-06
route_scale = 2.5


MESH = pl.DeviceIdType.MESH
AXES = ("x", "z", "y")
ORDERS = (("y", "z", "x"), ("z", "x", "y"), ("x", "y", "z"))


def coordinates():
    dp, ep = lax.axis_index("dp"), lax.axis_index("ep")
    me = {"x": ep // 4, "z": (ep // 2) % 2 * 2 + dp // 4, "y": dp % 4}
    return me, ep % 2


def device(at, core):
    return ((at["z"] % 2) * 4 + at["y"], at["x"] * 4 + at["z"] // 2 * 2 + core)


def moved(me, axis, offset):
    return {**me, axis: (me[axis] + offset) % 4}


def pick(ref, where, tail=(), axes=AXES):
    return ref.at[tuple(where.get(a, slice(None)) for a in axes) + tuple(tail)]


class Copies:
    def __init__(self, send, recv):
        self.send, self.recv, self.used, self.sent = send, recv, 0, []

    def start(self, src, dst, to):
        copy = pltpu.make_async_remote_copy(
            src_ref=src,
            dst_ref=dst,
            send_sem=self.send.at[self.used],
            recv_sem=self.recv.at[self.used],
            device_id=to,
            device_id_type=MESH,
        )
        copy.start()
        self.used += 1
        self.sent.append(copy)
        return copy

    def finish(self):
        for copy in self.sent:
            copy.wait_send()


def decode_kernel(
    plan,
    lengths,
    routes,
    queries_in,
    gain_in,
    cache_latent,
    cache_rope,
    w_absorb,
    w_out,
    router,
    w_gate,
    w_up,
    w_down,
    attended,
    mixed,
    queries,
    gain,
    keys,
    rope_keys,
    rotary,
    wa,
    query_latent,
    query_rope,
    query_out,
    query_in,
    marks_out,
    marks,
    latent_out,
    values,
    places,
    logits,
    act_source,
    rank_rows,
    wo,
    wr,
    wg,
    wu,
    wd,
    terms,
    core_terms,
    slab_terms,
    tokens,
    act,
    partial,
    core_partial,
    far_parts,
    near_parts,
    sums_two,
    parts_two,
    sums_three,
    parts_three,
    final_half,
    load_sem,
    send_sem,
    recv_sem,
):
    me, core = coordinates()
    other = 1 - core
    sibling = device(me, other)
    copies = Copies(send_sem, recv_sem)
    width = wg.shape[1] // 2
    slots, heads = queries.shape[0], wa.shape[0]
    latent_width, rope_width = keys.shape[1], rope_keys.shape[1]
    cap = keys.shape[0] // slots
    half = slots // 2
    tiles = width // 128
    wide = (tiles * 5 + 6) // 7 * 128
    piece_rows = ((0, half // 2), (half // 2, half // 2), (0, half))
    piece_cols = ((0, wide), (0, wide), (wide, width - wide))
    unit_cols = partial.shape[-1]
    share = (unit_cols // 128 * 5 + 6) // 14 * 128
    out_cols = ((0, share), (share, share), (2 * share, unit_cols - 2 * share))

    slab_offsets = [(2, 1), (1, 1), (3, 1), (2, 0), (0, 1), (1, 0), (3, 0)]

    def slab_chip(dx, dz):
        return {**me, "x": (me["x"] + dx) % 4, "z": (me["z"] + 2 * dz) % 4}

    def slab_index(chip):
        return chip["x"] * 2 + chip["z"] // 2

    order = slab_offsets + [(0, 0)]
    slabs = [slab_index(slab_chip(dx, dz)) for dx, dz in order]

    def columns(slab):
        return pl.ds(pl.multiple_of(slab * width, 128), width)

    peers = [sibling]
    for axis in AXES:
        peers += [device(moved(me, axis, k), core) for k in (1, 2, 3)]
    peers += [device(slab_chip(dx, 1), core) for dx in (1, 2, 3)]
    rank_offsets = [(dz, dy) for dz in range(2) for dy in range(4) if (dz, dy) != (0, 0)]

    def rank_chip(dz, dy):
        z = me["z"] // 2 * 2 + (me["z"] + dz) % 2
        return {**me, "z": z, "y": (me["y"] + dy) % 4}

    peers += [device(rank_chip(1, dy), core) for dy in (1, 2, 3)]
    barrier = pltpu.get_barrier_semaphore()
    for peer in peers:
        pl.semaphore_signal(barrier, inc=1, device_id=peer, device_id_type=MESH)

    query_load = pltpu.make_async_copy(queries_in, queries, load_sem.at[50])
    query_load.start()
    gain_load = pltpu.make_async_copy(gain_in, gain, load_sem.at[51])
    loads = []
    group = 16
    group_keys = group * cap
    groups = slots // group
    cache_loads = []
    for g in range(groups):
        rows = pl.ds(g * group_keys, group_keys)
        cache_loads.append(
            (
                pltpu.make_async_copy(cache_latent.at[rows], keys.at[rows], load_sem.at[20 + 2 * g]),
                pltpu.make_async_copy(
                    cache_rope.at[pl.ds(g * group, group)], rope_keys.at[pl.ds(g * group, group)], load_sem.at[21 + 2 * g]
                ),
            )
        )
        for load in cache_loads[-1]:
            load.start()
    absorb_load = pltpu.make_async_copy(w_absorb, wa, load_sem.at[28])
    absorb_load.start()
    for k, slab in enumerate(slabs):
        loads.append(
            pltpu.make_async_copy(w_out.at[:, columns(slab)], wo.at[:, columns(slab)], load_sem.at[k])
        )
    for k, (source, target) in enumerate(((w_gate, wg), (w_up, wu), (router, wr), (w_down, wd))):
        loads.append(pltpu.make_async_copy(source, target, load_sem.at[8 + k]))
    loads.append(gain_load)
    for load in loads:
        load.start()

    f32, bf16 = jnp.float32, jnp.bfloat16
    my_rank = lax.axis_index("dp")

    def iota(shape, axis):
        return lax.broadcasted_iota(jnp.int32, shape, axis)

    def mark(condition):
        return jnp.where(condition, 1.0, 0.0)

    def dot(a, b):
        return jnp.dot(a, b, preferred_element_type=f32)

    shift = slots.bit_length() - 1
    sources = jnp.concatenate([plan[:, r * slots : (r + 1) * slots] for r in range(8)], axis=0)
    rank_of, slot_of = sources >> shift, sources & (slots - 1)
    rank_row = iota((8, slots), 0)
    earlier = mark(iota((slots, slots), 0) < iota((slots, slots), 1)).astype(bf16)
    own_rank = jnp.sum(jnp.where(rank_row == my_rank, rank_of, 0).astype(f32), axis=0, keepdims=True)
    leaving = mark((own_rank == rank_row.astype(f32)) & (rank_row != my_rank))
    letter = jnp.sum(leaving * dot(leaving.astype(bf16), earlier), axis=0, keepdims=True)
    away = jnp.sum(leaving, axis=0, keepdims=True)
    key_row = jnp.where(away > 0.5, own_rank * 2.0 + letter, -1.0)
    diagonal = iota((slots, slots), 0) == iota((slots, slots), 1)
    key = jnp.sum(jnp.where(diagonal, key_row, 0.0), axis=1, keepdims=True).astype(jnp.int32)
    stays = key < 0
    length = jnp.sum(jnp.where(diagonal, lengths[...].astype(f32), 0.0), axis=1, keepdims=True).astype(jnp.int32)

    arriving = mark((rank_of == my_rank) & (rank_row != my_rank))
    nth = dot(arriving.astype(bf16), earlier)
    guest_slot = []
    for k in range(2):
        is_kth = (arriving > 0.5) & (jnp.abs(nth - k) < 0.5)
        guest_slot.append(jnp.sum(jnp.where(is_kth, slot_of + 1, 0).astype(f32), axis=1, keepdims=True) - 1.0)

    def letter_places(axis, shape):
        place = iota(shape, axis)
        inner = place & 15
        return place >> 4, inner >> 1, inner & 1, inner < 2 * heads

    query_load.wait()
    for h in range(heads):
        start = h * (latent_width + rope_width)
        query_latent[h] = queries[:, start : start + latent_width]
        query_rope[h] = queries[:, start + latent_width : start + latent_width + rope_width]

    to_rank, to_head, to_letter, used = letter_places(0, (128, slots))
    wanted = jnp.where(used, to_rank * 2 + to_letter, -2).astype(f32)
    chosen = mark(key_row == wanted)
    out_latent = jnp.zeros((128, latent_width), f32)
    out_rope = jnp.zeros((128, rope_width), f32)
    for h in range(heads):
        rows = jnp.where(to_head == h, chosen, 0.0).astype(bf16)
        out_latent = out_latent + dot(rows, query_latent[h])
        out_rope = out_rope + dot(rows, query_rope[h])
    query_out[:, :, 0:latent_width] = out_latent.astype(bf16).reshape(8, 16, latent_width)
    query_out[:, :, latent_width:] = (
        jnp.concatenate([out_rope, jnp.zeros((128, 128 - rope_width), f32)], axis=1)
        .astype(bf16)
        .reshape(8, 16, 128)
    )
    experts = iota((slots, marks.shape[3]), 1)
    named = jnp.zeros(experts.shape, f32)
    for k in range(routes.shape[0]):
        route = jnp.sum(jnp.where(diagonal, routes[k : k + 1, :], 0).astype(f32), axis=1, keepdims=True)
        named = named + mark(route.astype(jnp.int32) == experts)
    marks_out[...] = named.astype(bf16).reshape(marks_out.shape)
    marks[my_rank] = marks_out[...]
    query_in[my_rank] = jnp.zeros(query_in.shape[1:], bf16)

    pl.semaphore_wait(barrier, len(peers))
    from_ranks = []
    for dz, dy in rank_offsets:
        chip = rank_chip(dz, dy)
        to = device(chip, core)
        from_ranks.append(copies.start(query_out.at[to[0]], query_in.at[my_rank], to))
    from_marks = []
    for dz, dy in rank_offsets:
        from_marks.append(copies.start(marks_out, marks.at[my_rank], device(rank_chip(dz, dy), core)))

    from_rank, from_head, from_letter, used = letter_places(1, (8, 128))
    guests = jnp.where(from_letter == 0, guest_slot[0], guest_slot[1])
    guests = jnp.where((from_rank == iota((8, 128), 0)) & used, guests + 1.0, 0.0)
    guests = jnp.sum(guests, axis=0, keepdims=True) - 1.0
    _, from_head, _, _ = letter_places(1, (slots, 128))
    is_guest = mark(guests == iota((slots, 128), 0).astype(f32))
    for g in range(groups):
        for load in cache_loads[g]:
            load.wait()
    for g in range(groups):
        rotary[g] = jnp.concatenate([rope_keys[g * group + k] for k in range(group)], axis=1)
    for copy in from_ranks:
        copy.wait_recv()
    came = query_in[...].reshape(128, query_in.shape[2])
    for h in range(heads):
        rows = jnp.where(from_head == h, is_guest, 0.0).astype(bf16)
        guest = dot(rows, came)
        query_latent[h] = jnp.where(stays, query_latent[h].astype(f32), guest[:, :latent_width]).astype(bf16)
        query_rope[h] = jnp.where(
            stays, query_rope[h].astype(f32), guest[:, latent_width : latent_width + rope_width]
        ).astype(bf16)

    score_scale = (VDIM + rope_width) ** -0.5
    rows_shape = (heads * group, group_keys)
    position = iota(rows_shape, 1) - iota(rows_shape, 0) % group * cap
    contract_last = (((1,), (1,)), ((), ()))
    for g in range(groups):
        mine = pl.ds(g * group, group)
        q_latent = query_latent[:, mine, :].reshape(heads * group, latent_width)
        q_rope = query_rope[:, mine, :].reshape(heads * group, rope_width)
        here = pl.ds(g * group_keys, group_keys)
        scores = lax.dot_general(q_latent, keys[here, :], contract_last, preferred_element_type=f32)
        scores = scores + dot(q_rope, rotary[g])
        limit = jnp.concatenate([length[g * group : (g + 1) * group]] * heads, axis=0)
        seen = (position >= 0) & (position < limit)
        scores = jnp.where(seen, scores * score_scale, -jnp.inf)
        raised = jnp.exp(scores - jnp.max(scores, axis=1, keepdims=True))
        probs = (raised * (1.0 / jnp.sum(raised, axis=1, keepdims=True))).astype(bf16)
        latent_out[:, mine, :] = dot(probs, keys[here, :]).astype(bf16).reshape(heads, group, latent_width)
    absorb_load.wait()
    for h in range(heads):
        values[:, h * VDIM : (h + 1) * VDIM] = dot(latent_out[h], wa[h]).astype(bf16)

    from_sibling = []
    for load in loads[:8]:
        load.wait()
    for k, slab in enumerate(slabs):
        head_terms = jnp.dot(values[...], wo[:, columns(slab)], preferred_element_type=jnp.float32)
        terms[k] = head_terms.astype(jnp.bfloat16).reshape(2, half, width)
        from_sibling.append(copies.start(terms.at[k, other], core_terms.at[k], sibling))
    from_slabs = []
    for k, (dx, dz) in enumerate(order):
        from_sibling[k].wait_recv()
        total = terms[k, core].astype(jnp.float32) + core_terms[k].astype(jnp.float32)
        if k < len(slab_offsets):
            terms[k, core] = total.astype(jnp.bfloat16)
            from_slabs.append(
                copies.start(terms.at[k, core], slab_terms.at[k], device(slab_chip(dx, dz), core))
            )
    for r in range(8):
        source = jnp.sum(jnp.where(diagonal, sources[r : r + 1, :], 0).astype(f32), axis=1, keepdims=True)
        lanes = iota((slots, 8 * slots), 1)
        places[r] = mark(source.astype(jnp.int32) == lanes).astype(bf16)
    for k, copy in enumerate(from_slabs):
        copy.wait_recv()
        total = total + slab_terms[k].astype(jnp.float32)
    tokens[me["x"], me["z"], me["y"], core] = total.astype(jnp.bfloat16)

    def block(p, where):
        first, count = piece_rows[p]
        return pick(tokens, where, (core, pl.ds(first, count), pl.ds(*piece_cols[p])))

    def spread(p, where, to):
        return copies.start(block(p, where), block(p, where), to)

    pieces = range(3)
    rights = [device(moved(me, order[2], 1), core) for order in ORDERS]
    lefts = [device(moved(me, order[2], 3), core) for order in ORDERS]
    before = [(me[order[2]] + 3) % 4 for order in ORDERS]
    after = [(me[order[2]] + 1) % 4 for order in ORDERS]
    across = [(me[order[2]] + 2) % 4 for order in ORDERS]
    here = [me[order[2]] for order in ORDERS]

    def group_at(p, k, last):
        second = ORDERS[p][1]
        return {second: (me[second] + 4 - k) % 4, ORDERS[p][2]: last}

    one = [
        [spread(p, me, device(moved(me, ORDERS[p][0], k), core)) for k in (1, 3, 2)] for p in pieces
    ]
    two = [{} for p in pieces]
    to_right, to_left = [{} for p in pieces], [{} for p in pieces]
    far, to_core = [[] for p in pieces], []

    def near(p, k):
        where = group_at(p, k, here[p])
        to_right[p][k] = spread(p, where, rights[p])
        to_left[p][k] = spread(p, where, lefts[p])

    for p in pieces:
        for copy in one[p]:
            copy.wait_recv()
        for k in (1, 3, 2):
            two[p][k] = spread(p, group_at(p, 0, here[p]), device(moved(me, ORDERS[p][1], k), core))
        near(p, 0)
    for k in (1, 3):
        for p in pieces:
            two[p][k].wait_recv()
            near(p, k)
    for p in pieces:
        to_right[p][0].wait_recv()
        far[p].append(spread(p, group_at(p, 0, before[p]), rights[p]))
    for p in pieces:
        two[p][2].wait_recv()
        near(p, 2)
        to_core.append(spread(p, {ORDERS[p][2]: here[p]}, sibling))
    for p in pieces:
        to_left[p][3].wait_recv()
        far[p].append(spread(p, group_at(p, 3, after[p]), lefts[p]))
        to_right[p][1].wait_recv()
        far[p].append(spread(p, group_at(p, 1, before[p]), rights[p]))
    for p in pieces:
        to_left[p][2].wait_recv()
        far[p].append(spread(p, group_at(p, 2, after[p]), lefts[p]))
    for p in pieces:
        for k in (3, 2):
            to_right[p][k].wait_recv()
        to_core.append(spread(p, {ORDERS[p][2]: before[p]}, sibling))
        for k in (0, 1):
            to_left[p][k].wait_recv()
        to_core.append(spread(p, {ORDERS[p][2]: after[p]}, sibling))
    for p in pieces:
        for copy in far[p]:
            copy.wait_recv()
        to_core.append(spread(p, {ORDERS[p][2]: across[p]}, sibling))

    for load in loads[8:]:
        load.wait()
    for copy in from_marks:
        copy.wait_recv()

    def products(side):
        square_sum = jnp.zeros((8 * half, 128), f32)
        gate, up, score = 0.0, 0.0, 0.0
        for x in range(4):
            rows = [tokens[x, pl.ds(zh * 2, 2), :, side].reshape(8 * half, width) for zh in range(2)]
            rows = jnp.concatenate(rows, axis=1).astype(f32)
            for k in range(2 * width // 128):
                part = rows[:, k * 128 : (k + 1) * 128]
                square_sum = square_sum + part * part
            gained = (rows * gain[x]).astype(bf16)
            gate = gate + dot(gained, wg[x])
            up = up + dot(gained, wu[x])
            score = score + lax.dot_general(
                gained, wr[:, x * 2 * width : (x + 1) * 2 * width], contract_last, preferred_element_type=f32
            )

        scale = lax.rsqrt(jnp.sum(square_sum, axis=1, keepdims=True) * (1.0 / (8 * width)) + epsilon)
        score = score * scale
        high = score.astype(bf16)
        low = (score - high.astype(f32)).astype(bf16)
        logits[:, side] = jnp.concatenate([high, low], axis=1).reshape(8, half, 2 * score.shape[1])
        gate = gate * scale
        hidden = gate / (1.0 + jnp.exp(-gate)) * (up * scale)
        act_source[:, side] = hidden.astype(bf16).reshape(8, half, hidden.shape[1])

    products(core)
    for copy in to_core:
        copy.wait_recv()

    products(other)

    all_places = places[...].reshape(8 * slots, 8 * slots)
    experts = marks.shape[3]
    pair = dot(all_places, logits[...].reshape(8 * slots, 2 * experts))
    affinity = 1.0 / (1.0 + jnp.exp(-(pair[:, :experts] + pair[:, experts:])))
    chosen = affinity * marks[...].reshape(affinity.shape).astype(f32)
    mine = jnp.where(iota(affinity.shape, 1) == lax.axis_index("ep"), chosen, 0.0)
    weight = route_scale * jnp.sum(mine, axis=1, keepdims=True) / jnp.sum(chosen, axis=1, keepdims=True)
    moved_act = dot(all_places, act_source[...].reshape(8 * slots, act.shape[3])) * weight
    act[...] = moved_act.astype(bf16).reshape(act.shape)

    def down(p, column_half):
        first, count = out_cols[p]
        quarters = []
        for quarter in range(2):
            start = pl.multiple_of(column_half * (2 * unit_cols) + quarter * unit_cols + first, 128)
            quarters.append(
                dot(act[...].reshape(8 * slots, act.shape[3]), wd[:, pl.ds(start, count)])
                .reshape(2, 4, 4, 2, 8, count)
            )
        both = jnp.concatenate(quarters, axis=4).astype(jnp.bfloat16)
        for zl in range(2):
            for y in range(4):
                for zh in range(2):
                    partial[column_half, :, zh * 2 + zl, y, :, pl.ds(first, count)] = both[zl, y, :, zh]

    rest = [tuple(a for a in AXES if a != order[2]) for order in ORDERS]
    from_core = [{} for p in pieces]

    def own(p, where):
        return pick(partial.at[core], where, (slice(None), pl.ds(*out_cols[p])))

    def landing(ref, p, where):
        return pick(ref, where, (slice(None), pl.ds(0, out_cols[p][1])), rest[p])

    def share_sum(p, name, last):
        where, tail = {ORDERS[p][2]: last}, (slice(None), pl.ds(*out_cols[p]))
        from_core[p][name] = copies.start(
            pick(partial.at[other], where, tail), pick(core_partial, where, tail), sibling
        )

    def take_sum(p, name, last):
        from_core[p][name].wait_recv()
        where, tail = {ORDERS[p][2]: last}, (slice(None), pl.ds(*out_cols[p]))
        mine = own(p, where)
        mine[...] = (mine[...].astype(f32) + pick(core_partial, where, tail)[...].astype(f32)).astype(bf16)

    for p in pieces:
        down(p, other)
        share_sum(p, "across", across[p])
    for p in pieces:
        share_sum(p, "after", after[p])
        share_sum(p, "before", before[p])
    for p in pieces:
        share_sum(p, "here", here[p])
    by_right, by_left = (2, 3), (1, 0)
    far, sum_right, sum_left = [{} for p in pieces], [{} for p in pieces], [{} for p in pieces]

    def step(p, k):
        second = ORDERS[p][1]
        return {second: (me[second] + k) % 4}

    def part(p, last, k):
        return own(p, {ORDERS[p][2]: last, **step(p, k)})

    for p in pieces:
        down(p, core)
        take_sum(p, "across", across[p])
        for kr, kl in zip(by_right, by_left):
            for k, to in ((kr, rights[p]), (kl, lefts[p])):
                far[p][k] = copies.start(part(p, across[p], k), landing(far_parts.at[p], p, step(p, k)), to)
    for p in pieces:
        take_sum(p, "after", after[p])
        for k in by_left:
            there = landing(near_parts.at[p, 0], p, step(p, k))
            sum_right[p][k] = copies.start(part(p, after[p], k), there, rights[p])
        take_sum(p, "before", before[p])
        for k in by_right:
            there = landing(near_parts.at[p, 1], p, step(p, k))
            sum_left[p][k] = copies.start(part(p, before[p], k), there, lefts[p])
    for kr, kl in zip(by_right, by_left):
        for p in pieces:
            for k, at, side, sums, to in (
                (kr, after[p], 0, sum_right, rights[p]),
                (kl, before[p], 1, sum_left, lefts[p]),
            ):
                far[p][k].wait_recv()
                mine, came = part(p, at, k), landing(far_parts.at[p], p, step(p, k))
                mine[...] = (mine[...].astype(f32) + came[...].astype(f32)).astype(bf16)
                sums[p][k] = copies.start(mine, landing(near_parts.at[p, side], p, step(p, k)), to)
    for p in pieces:
        take_sum(p, "here", here[p])

    rank_copies = []
    for slab in range(8):
        rows = tokens[slab // 2, pl.ds(slab % 2 * 2, 2)].reshape(8 * slots, width)
        rank_rows[slab] = dot(places[my_rank], rows).astype(bf16)
    for slab in range(8):
        rank_copies.append(
            pltpu.make_async_copy(
                rank_rows.at[slab], attended.at[:, pl.ds(slab * width, width)], load_sem.at[12 + slab]
            )
        )
        rank_copies[-1].start()

    phase_two = [{} for p in pieces]
    for k in (2, 1, 3, 0):
        for p in pieces:
            sum_right[p][k].wait_recv()
            sum_left[p][k].wait_recv()
            total = part(p, here[p], k)[...].astype(f32)
            for side in range(2):
                total = total + landing(near_parts.at[p, side], p, step(p, k))[...].astype(f32)
            result = landing(sums_two.at[p], p, step(p, k))
            result[...] = total.astype(bf16)
            if k != 0:
                phase_two[p][k] = copies.start(
                    result,
                    parts_two.at[p, k - 1, :, :, pl.ds(0, out_cols[p][1])],
                    device(moved(me, ORDERS[p][1], k), core),
                )
    phase_three = {}
    for p, (first, second, last) in enumerate(ORDERS):
        width_p = out_cols[p][1]
        tail = (slice(None), pl.ds(0, width_p))
        for copy in phase_two[p].values():
            copy.wait_recv()
        total = pick(sums_two.at[p], {second: me[second]}, tail, rest[p])[...].astype(jnp.float32)
        for k in range(3):
            total = total + parts_two[p, k, :, :, pl.ds(0, width_p)].astype(jnp.float32)
        sums_three[p, :, :, pl.ds(0, width_p)] = total.astype(jnp.bfloat16)
        phase_three[p] = []
        for k in (1, 3, 2):
            to = moved(me, first, k)
            phase_three[p].append(
                copies.start(
                    sums_three.at[p, to[first], :, pl.ds(0, width_p)],
                    parts_three.at[p, k - 1, :, pl.ds(0, width_p)],
                    device(to, core),
                )
            )
    for p, (first, second, last) in enumerate(ORDERS):
        width_p = out_cols[p][1]
        for copy in phase_three[p]:
            copy.wait_recv()
        total = sums_three[p, me[first], :, pl.ds(0, width_p)].astype(jnp.float32)
        for k in range(3):
            total = total + parts_three[p, k, :, pl.ds(0, width_p)].astype(jnp.float32)
        final_half[0, :, pl.ds(*out_cols[p])] = total.astype(jnp.bfloat16)
    last_copy = copies.start(final_half.at[0], final_half.at[1], sibling)
    last_copy.wait_recv()
    for side, column_half in enumerate((core, other)):
        both = final_half[side].astype(f32)
        for quarter in range(2):
            eight = both[quarter * 8 : quarter * 8 + 8]
            own = jnp.where(core == 0, eight[0:4], eight[4:8])
            start = pl.multiple_of(column_half * (2 * unit_cols) + quarter * unit_cols, 128)
            mixed[:, pl.ds(start, unit_cols)] = own.astype(bf16)
    for copy in rank_copies:
        copy.wait()
    copies.finish()


def run_decode(
    queries, plan, lengths, routes, gain, cache_latent, cache_rope, w_absorb, w_out, router, w_gate, w_up, w_down
):
    slots = queries.shape[0]
    cap, latent_width = cache_latent.shape[1:]
    rope_width = cache_rope.shape[2]
    heads = w_absorb.shape[0]
    heads_width = w_out.shape[0]
    model = w_out.shape[1]
    width = model // 8
    half = slots // 2
    hidden = w_gate.shape[1]
    experts = router.shape[1]
    rows = 8 * slots
    unit_cols = model // 4
    share = (unit_cols // 128 * 5 + 6) // 14 * 128
    bf16, f32 = jnp.bfloat16, jnp.float32
    vmem = pl.BlockSpec(memory_space=pltpu.VMEM)
    hbm = pl.BlockSpec(memory_space=pl.ANY)
    return pl.pallas_call(
        decode_kernel,
        out_shape=(
            jax.ShapeDtypeStruct((slots, model), bf16),
            jax.ShapeDtypeStruct((4, model), bf16),
        ),
        in_specs=[vmem] * 3 + [hbm] * 10,
        out_specs=(hbm, vmem),
        scratch_shapes=[
            pltpu.VMEM(queries.shape, bf16),
            pltpu.VMEM((4, 1, 2 * width), f32),
            pltpu.VMEM((slots * cap, latent_width), bf16),
            pltpu.VMEM((slots, rope_width, cap), bf16),
            pltpu.VMEM((slots // 16, rope_width, 16 * cap), bf16),
            pltpu.VMEM(w_absorb.shape, bf16),
            pltpu.VMEM((heads, slots, latent_width), bf16),
            pltpu.VMEM((heads, slots, rope_width), bf16),
            pltpu.VMEM((8, 16, latent_width + 128), bf16),
            pltpu.VMEM((8, 16, latent_width + 128), bf16),
            pltpu.VMEM((2, half, experts), bf16),
            pltpu.VMEM((8, 2, half, experts), bf16),
            pltpu.VMEM((heads, slots, latent_width), bf16),
            pltpu.VMEM((slots, heads_width), bf16),
            pltpu.VMEM((8, slots, rows), bf16),
            pltpu.VMEM((8, 2, half, 2 * experts), bf16),
            pltpu.VMEM((8, 2, half, hidden), bf16),
            pltpu.VMEM((8, slots, width), bf16),
            pltpu.VMEM((heads_width, model), bf16),
            pltpu.VMEM((experts, model), bf16),
            pltpu.VMEM((4, 2 * width, hidden), bf16),
            pltpu.VMEM((4, 2 * width, hidden), bf16),
            pltpu.VMEM((hidden, model), bf16),
            pltpu.VMEM((8, 2, half, width), bf16),
            pltpu.VMEM((8, half, width), bf16),
            pltpu.VMEM((7, half, width), bf16),
            pltpu.VMEM((4, 4, 4, 2, half, width), bf16),
            pltpu.VMEM((8, 2, half, hidden), bf16),
            pltpu.VMEM((2, 4, 4, 4, 16, unit_cols), bf16),
            pltpu.VMEM((4, 4, 4, 16, unit_cols), bf16),
            pltpu.VMEM((3, 4, 4, 16, share), bf16),
            pltpu.VMEM((3, 2, 4, 4, 16, share), bf16),
            pltpu.VMEM((3, 4, 4, 16, share), bf16),
            pltpu.VMEM((3, 3, 4, 16, share), bf16),
            pltpu.VMEM((3, 4, 16, share), bf16),
            pltpu.VMEM((3, 3, 16, share), bf16),
            pltpu.VMEM((2, 16, unit_cols), bf16),
            pltpu.SemaphoreType.DMA((56,)),
            pltpu.SemaphoreType.DMA((192,)),
            pltpu.SemaphoreType.DMA((192,)),
        ],
        compiler_params=pltpu.CompilerParams(
            collective_id=0, has_side_effects=True, vmem_limit_bytes=60 * 1024 * 1024
        ),
        name="decode",
    )(
        plan,
        lengths,
        routes.T,
        queries,
        gain.reshape(4, 1, 2 * width),
        cache_latent.reshape(slots * cap, latent_width),
        cache_rope.transpose(0, 2, 1),
        w_absorb,
        w_out,
        router.T,
        w_gate.reshape(4, 2 * width, hidden),
        w_up.reshape(4, 2 * width, hidden),
        w_down,
    )


def copy_kernel(source, small_source, target, small_target, held, small_held, sems):
    parts = held.shape[0]
    width = source.shape[1] // parts
    small_in = pltpu.make_async_copy(small_source, small_held, sems.at[2 * parts])
    small_in.start()
    copies_in, copies_out = [], []
    for k in range(parts):
        columns = pl.ds(k * width, width)
        copies_in.append(pltpu.make_async_copy(source.at[:, columns], held.at[k], sems.at[k]))
        copies_out.append(pltpu.make_async_copy(held.at[k], target.at[:, columns], sems.at[parts + k]))
        copies_in[-1].start()
    small_in.wait()
    small_out = pltpu.make_async_copy(small_held, small_target, sems.at[2 * parts + 1])
    small_out.start()
    for copy_in, copy_out in zip(copies_in, copies_out):
        copy_in.wait()
        copy_out.start()
    for copy in copies_out:
        copy.wait()
    small_out.wait()


def write_out(attended, mixed):
    hbm = pl.BlockSpec(memory_space=pl.ANY)
    parts = 4
    return pl.pallas_call(
        copy_kernel,
        out_shape=(
            jax.ShapeDtypeStruct(attended.shape, attended.dtype),
            jax.ShapeDtypeStruct(mixed.shape, mixed.dtype),
        ),
        in_specs=[hbm, hbm],
        out_specs=(hbm, hbm),
        scratch_shapes=[
            pltpu.VMEM((parts, attended.shape[0], attended.shape[1] // parts), attended.dtype),
            pltpu.VMEM(mixed.shape, mixed.dtype),
            pltpu.SemaphoreType.DMA((2 * parts + 2,)),
        ],
        compiler_params=pltpu.CompilerParams(vmem_limit_bytes=60 * 1024 * 1024),
        name="write_out",
    )(attended, mixed)


def per_device(
    queries,
    cache_latent,
    cache_rope,
    cache_len,
    move_plan,
    w_absorb,
    w_out,
    norm_gain,
    router,
    routes,
    w_gate,
    w_up,
    w_down,
):
    slots = cache_len.shape[0]
    attended, mixed = run_decode(
        queries,
        move_plan.reshape(1, -1),
        cache_len.reshape(1, slots),
        routes,
        norm_gain,
        cache_latent,
        cache_rope,
        w_absorb,
        w_out,
        router,
        w_gate[0],
        w_up[0],
        w_down[0],
    )
    return write_out(attended, mixed)


def solution(mesh):
    in_specs = (
        P("dp", "ep"),
        P("dp", None, None),
        P("dp", None, None),
        P("dp"),
        P(),
        P("ep", None, None),
        P("ep", None),
        P(),
        P(),
        P("dp", None),
        P("ep", None, "dp"),
        P("ep", None, "dp"),
        P("ep", "dp", None),
    )
    out_specs = (P("dp", None), P(("dp", "ep"), None))
    return jax.shard_map(
        per_device, mesh=mesh, in_specs=in_specs, out_specs=out_specs, check_vma=False
    )
```

```python
import jax
import jax.numpy as jnp
from jax import lax
from jax.experimental import pallas as pl
from jax.experimental.pallas import tpu as pltpu
from jax.sharding import PartitionSpec as P

VDIM = 128

epsilon = 1e-06
route_scale = 2.5


MESH = pl.DeviceIdType.MESH
AXES = ("x", "z", "y")
ORDERS = (("y", "z", "x"), ("z", "x", "y"), ("x", "y", "z"))


def coordinates():
    dp, ep = lax.axis_index("dp"), lax.axis_index("ep")
    me = {"x": ep // 4, "z": (ep // 2) % 2 * 2 + dp // 4, "y": dp % 4}
    return me, ep % 2


def device(at, core):
    return ((at["z"] % 2) * 4 + at["y"], at["x"] * 4 + at["z"] // 2 * 2 + core)


def moved(me, axis, offset):
    return {**me, axis: (me[axis] + offset) % 4}


def pick(ref, where, tail=(), axes=AXES):
    return ref.at[tuple(where.get(a, slice(None)) for a in axes) + tuple(tail)]


class Copies:
    def __init__(self, send, recv):
        self.send, self.recv, self.used, self.sent = send, recv, 0, []

    def start(self, src, dst, to):
        copy = pltpu.make_async_remote_copy(
            src_ref=src,
            dst_ref=dst,
            send_sem=self.send.at[self.used],
            recv_sem=self.recv.at[self.used],
            device_id=to,
            device_id_type=MESH,
        )
        copy.start()
        self.used += 1
        self.sent.append(copy)
        return copy

    def finish(self):
        for copy in self.sent:
            copy.wait_send()


def decode_kernel(
    plan,
    lengths,
    routes,
    queries_in,
    gain_in,
    cache_latent,
    cache_rope,
    w_absorb,
    w_out,
    router,
    w_gate,
    w_up,
    w_down,
    attended,
    mixed,
    queries,
    gain,
    keys,
    rope_keys,
    rotary,
    wa,
    query_latent,
    query_rope,
    query_out,
    query_in,
    marks_out,
    marks,
    latent_out,
    values,
    places,
    logits,
    act_source,
    rank_rows,
    wo,
    wr,
    wg,
    wu,
    wd,
    terms,
    core_terms,
    slab_terms,
    tokens,
    act,
    partial,
    core_partial,
    far_parts,
    near_parts,
    sums_two,
    parts_two,
    sums_three,
    parts_three,
    final_half,
    load_sem,
    send_sem,
    recv_sem,
):
    me, core = coordinates()
    other = 1 - core
    sibling = device(me, other)
    copies = Copies(send_sem, recv_sem)
    width = wg.shape[1] // 2
    slots, heads = queries.shape[0], wa.shape[0]
    latent_width, rope_width = keys.shape[1], rope_keys.shape[1]
    cap = keys.shape[0] // slots
    half = slots // 2
    tiles = width // 128
    wide = (tiles * 5 + 6) // 7 * 128
    piece_rows = ((0, half // 2), (half // 2, half // 2), (0, half))
    piece_cols = ((0, wide), (0, wide), (wide, width - wide))
    unit_cols = partial.shape[-1]
    share = (unit_cols // 128 * 5 + 6) // 14 * 128
    out_cols = ((0, share), (share, share), (2 * share, unit_cols - 2 * share))

    slab_offsets = [(2, 1), (1, 1), (3, 1), (2, 0), (0, 1), (1, 0), (3, 0)]

    def slab_chip(dx, dz):
        return {**me, "x": (me["x"] + dx) % 4, "z": (me["z"] + 2 * dz) % 4}

    def slab_index(chip):
        return chip["x"] * 2 + chip["z"] // 2

    order = slab_offsets + [(0, 0)]
    slabs = [slab_index(slab_chip(dx, dz)) for dx, dz in order]

    def columns(slab):
        return pl.ds(pl.multiple_of(slab * width, 128), width)

    peers = [sibling]
    for axis in AXES:
        peers += [device(moved(me, axis, k), core) for k in (1, 2, 3)]
    peers += [device(slab_chip(dx, 1), core) for dx in (1, 2, 3)]
    rank_offsets = [(dz, dy) for dz in range(2) for dy in range(4) if (dz, dy) != (0, 0)]

    def rank_chip(dz, dy):
        z = me["z"] // 2 * 2 + (me["z"] + dz) % 2
        return {**me, "z": z, "y": (me["y"] + dy) % 4}

    peers += [device(rank_chip(1, dy), core) for dy in (1, 2, 3)]
    barrier = pltpu.get_barrier_semaphore()
    for peer in peers:
        pl.semaphore_signal(barrier, inc=1, device_id=peer, device_id_type=MESH)

    query_load = pltpu.make_async_copy(queries_in, queries, load_sem.at[50])
    query_load.start()
    gain_load = pltpu.make_async_copy(gain_in, gain, load_sem.at[51])
    loads = []
    group = 16
    group_keys = group * cap
    groups = slots // group
    cache_loads = []
    for g in range(groups):
        rows = pl.ds(g * group_keys, group_keys)
        cache_loads.append(
            (
                pltpu.make_async_copy(cache_latent.at[rows], keys.at[rows], load_sem.at[20 + 2 * g]),
                pltpu.make_async_copy(
                    cache_rope.at[pl.ds(g * group, group)], rope_keys.at[pl.ds(g * group, group)], load_sem.at[21 + 2 * g]
                ),
            )
        )
        for load in cache_loads[-1]:
            load.start()
    absorb_load = pltpu.make_async_copy(w_absorb, wa, load_sem.at[28])
    absorb_load.start()
    for k, slab in enumerate(slabs):
        loads.append(
            pltpu.make_async_copy(w_out.at[:, columns(slab)], wo.at[:, columns(slab)], load_sem.at[k])
        )
    for k, (source, target) in enumerate(((w_gate, wg), (w_up, wu), (router, wr), (w_down, wd))):
        loads.append(pltpu.make_async_copy(source, target, load_sem.at[8 + k]))
    loads.append(gain_load)
    for load in loads:
        load.start()

    f32, bf16 = jnp.float32, jnp.bfloat16
    my_rank = lax.axis_index("dp")

    def iota(shape, axis):
        return lax.broadcasted_iota(jnp.int32, shape, axis)

    def mark(condition):
        return jnp.where(condition, 1.0, 0.0)

    def dot(a, b):
        return jnp.dot(a, b, preferred_element_type=f32)

    shift = slots.bit_length() - 1
    sources = jnp.concatenate([plan[:, r * slots : (r + 1) * slots] for r in range(8)], axis=0)
    rank_of, slot_of = sources >> shift, sources & (slots - 1)
    rank_row = iota((8, slots), 0)
    earlier = mark(iota((slots, slots), 0) < iota((slots, slots), 1)).astype(bf16)
    own_rank = jnp.sum(jnp.where(rank_row == my_rank, rank_of, 0).astype(f32), axis=0, keepdims=True)
    leaving = mark((own_rank == rank_row.astype(f32)) & (rank_row != my_rank))
    letter = jnp.sum(leaving * dot(leaving.astype(bf16), earlier), axis=0, keepdims=True)
    away = jnp.sum(leaving, axis=0, keepdims=True)
    key_row = jnp.where(away > 0.5, own_rank * 2.0 + letter, -1.0)
    def letter_places(axis, shape):
        place = iota(shape, axis)
        inner = place & 15
        return place >> 4, inner >> 1, inner & 1, inner < 2 * heads

    query_load.wait()
    for h in range(heads):
        start = h * (latent_width + rope_width)
        query_latent[h] = queries[:, start : start + latent_width]
        query_rope[h] = queries[:, start + latent_width : start + latent_width + rope_width]

    to_rank, to_head, to_letter, used = letter_places(0, (128, slots))
    wanted = jnp.where(used, to_rank * 2 + to_letter, -2).astype(f32)
    chosen = mark(key_row == wanted)
    out_latent = jnp.zeros((128, latent_width), f32)
    out_rope = jnp.zeros((128, rope_width), f32)
    for h in range(heads):
        rows = jnp.where(to_head == h, chosen, 0.0).astype(bf16)
        out_latent = out_latent + dot(rows, query_latent[h])
        out_rope = out_rope + dot(rows, query_rope[h])
    query_out[:, :, 0:latent_width] = out_latent.astype(bf16).reshape(8, 16, latent_width)
    query_out[:, :, latent_width:] = (
        jnp.concatenate([out_rope, jnp.zeros((128, 128 - rope_width), f32)], axis=1)
        .astype(bf16)
        .reshape(8, 16, 128)
    )
    pl.semaphore_wait(barrier, len(peers))
    from_ranks = []
    for dz, dy in rank_offsets:
        chip = rank_chip(dz, dy)
        to = device(chip, core)
        from_ranks.append(copies.start(query_out.at[to[0]], query_in.at[my_rank], to))
    diagonal = iota((slots, slots), 0) == iota((slots, slots), 1)
    key = jnp.sum(jnp.where(diagonal, key_row, 0.0), axis=1, keepdims=True).astype(jnp.int32)
    stays = key < 0
    length = jnp.sum(jnp.where(diagonal, lengths[...].astype(f32), 0.0), axis=1, keepdims=True).astype(jnp.int32)

    arriving = mark((rank_of == my_rank) & (rank_row != my_rank))
    nth = dot(arriving.astype(bf16), earlier)
    guest_slot = []
    for k in range(2):
        is_kth = (arriving > 0.5) & (jnp.abs(nth - k) < 0.5)
        guest_slot.append(jnp.sum(jnp.where(is_kth, slot_of + 1, 0).astype(f32), axis=1, keepdims=True) - 1.0)

    experts = iota((slots, marks.shape[3]), 1)
    named = jnp.zeros(experts.shape, f32)
    for k in range(routes.shape[0]):
        route = jnp.sum(jnp.where(diagonal, routes[k : k + 1, :], 0).astype(f32), axis=1, keepdims=True)
        named = named + mark(route.astype(jnp.int32) == experts)
    marks_out[...] = named.astype(bf16).reshape(marks_out.shape)
    marks[my_rank] = marks_out[...]
    query_in[my_rank] = jnp.zeros(query_in.shape[1:], bf16)
    from_marks = []
    for dz, dy in rank_offsets:
        from_marks.append(copies.start(marks_out, marks.at[my_rank], device(rank_chip(dz, dy), core)))

    from_rank, from_head, from_letter, used = letter_places(1, (8, 128))
    guests = jnp.where(from_letter == 0, guest_slot[0], guest_slot[1])
    guests = jnp.where((from_rank == iota((8, 128), 0)) & used, guests + 1.0, 0.0)
    guests = jnp.sum(guests, axis=0, keepdims=True) - 1.0
    _, from_head, _, _ = letter_places(1, (slots, 128))
    is_guest = mark(guests == iota((slots, 128), 0).astype(f32))
    for g in range(groups):
        for load in cache_loads[g]:
            load.wait()
    for g in range(groups):
        rotary[g] = jnp.concatenate([rope_keys[g * group + k] for k in range(group)], axis=1)
    for copy in from_ranks:
        copy.wait_recv()
    came = query_in[...].reshape(128, query_in.shape[2])
    for h in range(heads):
        rows = jnp.where(from_head == h, is_guest, 0.0).astype(bf16)
        guest = dot(rows, came)
        query_latent[h] = jnp.where(stays, query_latent[h].astype(f32), guest[:, :latent_width]).astype(bf16)
        query_rope[h] = jnp.where(
            stays, query_rope[h].astype(f32), guest[:, latent_width : latent_width + rope_width]
        ).astype(bf16)

    score_scale = (VDIM + rope_width) ** -0.5
    rows_shape = (heads * group, group_keys)
    position = iota(rows_shape, 1) - iota(rows_shape, 0) % group * cap
    contract_last = (((1,), (1,)), ((), ()))
    for g in range(groups):
        mine = pl.ds(g * group, group)
        q_latent = query_latent[:, mine, :].reshape(heads * group, latent_width)
        q_rope = query_rope[:, mine, :].reshape(heads * group, rope_width)
        here = pl.ds(g * group_keys, group_keys)
        scores = lax.dot_general(q_latent, keys[here, :], contract_last, preferred_element_type=f32)
        scores = scores + dot(q_rope, rotary[g])
        limit = jnp.concatenate([length[g * group : (g + 1) * group]] * heads, axis=0)
        seen = (position >= 0) & (position < limit)
        scores = jnp.where(seen, scores * score_scale, -jnp.inf)
        raised = jnp.exp(scores - jnp.max(scores, axis=1, keepdims=True))
        probs = (raised * (1.0 / jnp.sum(raised, axis=1, keepdims=True))).astype(bf16)
        latent_out[:, mine, :] = dot(probs, keys[here, :]).astype(bf16).reshape(heads, group, latent_width)
    absorb_load.wait()
    for h in range(heads):
        values[:, h * VDIM : (h + 1) * VDIM] = dot(latent_out[h], wa[h]).astype(bf16)

    from_sibling = []
    for load in loads[:8]:
        load.wait()
    for k, slab in enumerate(slabs):
        head_terms = jnp.dot(values[...], wo[:, columns(slab)], preferred_element_type=jnp.float32)
        terms[k] = head_terms.astype(jnp.bfloat16).reshape(2, half, width)
        from_sibling.append(copies.start(terms.at[k, other], core_terms.at[k], sibling))
    from_slabs = []
    for k, (dx, dz) in enumerate(order):
        from_sibling[k].wait_recv()
        total = terms[k, core].astype(jnp.float32) + core_terms[k].astype(jnp.float32)
        if k < len(slab_offsets):
            terms[k, core] = total.astype(jnp.bfloat16)
            from_slabs.append(
                copies.start(terms.at[k, core], slab_terms.at[k], device(slab_chip(dx, dz), core))
            )
    for r in range(8):
        source = jnp.sum(jnp.where(diagonal, sources[r : r + 1, :], 0).astype(f32), axis=1, keepdims=True)
        lanes = iota((slots, 8 * slots), 1)
        places[r] = mark(source.astype(jnp.int32) == lanes).astype(bf16)
    for k, copy in enumerate(from_slabs):
        copy.wait_recv()
        total = total + slab_terms[k].astype(jnp.float32)
    tokens[me["x"], me["z"], me["y"], core] = total.astype(jnp.bfloat16)

    def block(p, where):
        first, count = piece_rows[p]
        return pick(tokens, where, (core, pl.ds(first, count), pl.ds(*piece_cols[p])))

    def spread(p, where, to):
        return copies.start(block(p, where), block(p, where), to)

    pieces = range(3)
    rights = [device(moved(me, order[2], 1), core) for order in ORDERS]
    lefts = [device(moved(me, order[2], 3), core) for order in ORDERS]
    before = [(me[order[2]] + 3) % 4 for order in ORDERS]
    after = [(me[order[2]] + 1) % 4 for order in ORDERS]
    across = [(me[order[2]] + 2) % 4 for order in ORDERS]
    here = [me[order[2]] for order in ORDERS]

    def group_at(p, k, last):
        second = ORDERS[p][1]
        return {second: (me[second] + 4 - k) % 4, ORDERS[p][2]: last}

    one = [
        [spread(p, me, device(moved(me, ORDERS[p][0], k), core)) for k in (1, 3, 2)] for p in pieces
    ]
    two = [{} for p in pieces]
    to_right, to_left = [{} for p in pieces], [{} for p in pieces]
    far, to_core = [[] for p in pieces], []

    def near(p, k):
        where = group_at(p, k, here[p])
        to_right[p][k] = spread(p, where, rights[p])
        to_left[p][k] = spread(p, where, lefts[p])

    for p in pieces:
        for copy in one[p]:
            copy.wait_recv()
        for k in (1, 3, 2):
            two[p][k] = spread(p, group_at(p, 0, here[p]), device(moved(me, ORDERS[p][1], k), core))
        near(p, 0)
    for k in (1, 3):
        for p in pieces:
            two[p][k].wait_recv()
            near(p, k)
    for p in pieces:
        to_right[p][0].wait_recv()
        far[p].append(spread(p, group_at(p, 0, before[p]), rights[p]))
    for p in pieces:
        two[p][2].wait_recv()
        near(p, 2)
        to_core.append(spread(p, {ORDERS[p][2]: here[p]}, sibling))
    for p in pieces:
        to_left[p][3].wait_recv()
        far[p].append(spread(p, group_at(p, 3, after[p]), lefts[p]))
        to_right[p][1].wait_recv()
        far[p].append(spread(p, group_at(p, 1, before[p]), rights[p]))
    for p in pieces:
        to_left[p][2].wait_recv()
        far[p].append(spread(p, group_at(p, 2, after[p]), lefts[p]))
    for p in pieces:
        for k in (3, 2):
            to_right[p][k].wait_recv()
        to_core.append(spread(p, {ORDERS[p][2]: before[p]}, sibling))
        for k in (0, 1):
            to_left[p][k].wait_recv()
        to_core.append(spread(p, {ORDERS[p][2]: after[p]}, sibling))
    for p in pieces:
        for copy in far[p]:
            copy.wait_recv()
        to_core.append(spread(p, {ORDERS[p][2]: across[p]}, sibling))

    for load in loads[8:]:
        load.wait()
    for copy in from_marks:
        copy.wait_recv()

    def products(side, scored):
        square_sum = jnp.zeros((8 * half, 128), f32)
        gate, up, score = 0.0, 0.0, 0.0
        for x in range(4):
            rows = [tokens[x, pl.ds(zh * 2, 2), :, side].reshape(8 * half, width) for zh in range(2)]
            rows = jnp.concatenate(rows, axis=1).astype(f32)
            for k in range(2 * width // 128):
                part = rows[:, k * 128 : (k + 1) * 128]
                square_sum = square_sum + part * part
            gained = (rows * gain[x]).astype(bf16)
            gate = gate + dot(gained, wg[x])
            up = up + dot(gained, wu[x])
            if scored:
                score = score + lax.dot_general(
                    gained, wr[:, x * 2 * width : (x + 1) * 2 * width], contract_last, preferred_element_type=f32
                )

        scale = lax.rsqrt(jnp.sum(square_sum, axis=1, keepdims=True) * (1.0 / (8 * width)) + epsilon)
        if scored:
            score = score * scale
            high = score.astype(bf16)
            low = (score - high.astype(f32)).astype(bf16)
            logits[:, side] = jnp.concatenate([high, low], axis=1).reshape(8, half, 2 * score.shape[1])
        gate = gate * scale
        hidden = gate / (1.0 + jnp.exp(-gate)) * (up * scale)
        act_source[:, side] = hidden.astype(bf16).reshape(8, half, hidden.shape[1])

    products(core, True)
    scores_copy = copies.start(logits.at[:, core], logits.at[:, core], sibling)
    for copy in to_core:
        copy.wait_recv()

    products(other, False)
    scores_copy.wait_recv()

    all_places = places[...].reshape(8 * slots, 8 * slots)
    experts = marks.shape[3]
    pair = dot(all_places, logits[...].reshape(8 * slots, 2 * experts))
    affinity = 1.0 / (1.0 + jnp.exp(-(pair[:, :experts] + pair[:, experts:])))
    chosen = affinity * marks[...].reshape(affinity.shape).astype(f32)
    mine = jnp.where(iota(affinity.shape, 1) == lax.axis_index("ep"), chosen, 0.0)
    weight = route_scale * jnp.sum(mine, axis=1, keepdims=True) / jnp.sum(chosen, axis=1, keepdims=True)
    moved_act = dot(all_places, act_source[...].reshape(8 * slots, act.shape[3])) * weight
    act[...] = moved_act.astype(bf16).reshape(act.shape)

    def down(p, column_half):
        first, count = out_cols[p]
        quarters = []
        for quarter in range(2):
            start = pl.multiple_of(column_half * (2 * unit_cols) + quarter * unit_cols + first, 128)
            quarters.append(
                dot(act[...].reshape(8 * slots, act.shape[3]), wd[:, pl.ds(start, count)])
                .reshape(2, 4, 4, 2, 8, count)
            )
        both = jnp.concatenate(quarters, axis=4).astype(jnp.bfloat16)
        for zl in range(2):
            for y in range(4):
                for zh in range(2):
                    partial[column_half, :, zh * 2 + zl, y, :, pl.ds(first, count)] = both[zl, y, :, zh]

    rest = [tuple(a for a in AXES if a != order[2]) for order in ORDERS]
    from_core = [{} for p in pieces]

    def own(p, where):
        return pick(partial.at[core], where, (slice(None), pl.ds(*out_cols[p])))

    def landing(ref, p, where):
        return pick(ref, where, (slice(None), pl.ds(0, out_cols[p][1])), rest[p])

    def share_sum(p, name, last):
        where, tail = {ORDERS[p][2]: last}, (slice(None), pl.ds(*out_cols[p]))
        from_core[p][name] = copies.start(
            pick(partial.at[other], where, tail), pick(core_partial, where, tail), sibling
        )

    def take_sum(p, name, last):
        from_core[p][name].wait_recv()
        where, tail = {ORDERS[p][2]: last}, (slice(None), pl.ds(*out_cols[p]))
        mine = own(p, where)
        mine[...] = (mine[...].astype(f32) + pick(core_partial, where, tail)[...].astype(f32)).astype(bf16)

    for p in pieces:
        down(p, other)
        share_sum(p, "across", across[p])
    for p in pieces:
        share_sum(p, "after", after[p])
        share_sum(p, "before", before[p])
    for p in pieces:
        share_sum(p, "here", here[p])
    by_right, by_left = (2, 3), (1, 0)
    far, sum_right, sum_left = [{} for p in pieces], [{} for p in pieces], [{} for p in pieces]

    def step(p, k):
        second = ORDERS[p][1]
        return {second: (me[second] + k) % 4}

    def part(p, last, k):
        return own(p, {ORDERS[p][2]: last, **step(p, k)})

    for p in pieces:
        down(p, core)
        take_sum(p, "across", across[p])
        for kr, kl in zip(by_right, by_left):
            for k, to in ((kr, rights[p]), (kl, lefts[p])):
                far[p][k] = copies.start(part(p, across[p], k), landing(far_parts.at[p], p, step(p, k)), to)
    for p in pieces:
        take_sum(p, "after", after[p])
        for k in by_left:
            there = landing(near_parts.at[p, 0], p, step(p, k))
            sum_right[p][k] = copies.start(part(p, after[p], k), there, rights[p])
        take_sum(p, "before", before[p])
        for k in by_right:
            there = landing(near_parts.at[p, 1], p, step(p, k))
            sum_left[p][k] = copies.start(part(p, before[p], k), there, lefts[p])
    for kr, kl in zip(by_right, by_left):
        for p in pieces:
            for k, at, side, sums, to in (
                (kr, after[p], 0, sum_right, rights[p]),
                (kl, before[p], 1, sum_left, lefts[p]),
            ):
                far[p][k].wait_recv()
                mine, came = part(p, at, k), landing(far_parts.at[p], p, step(p, k))
                mine[...] = (mine[...].astype(f32) + came[...].astype(f32)).astype(bf16)
                sums[p][k] = copies.start(mine, landing(near_parts.at[p, side], p, step(p, k)), to)
    for p in pieces:
        take_sum(p, "here", here[p])

    rank_copies = []
    for slab in range(8):
        rows = tokens[slab // 2, pl.ds(slab % 2 * 2, 2)].reshape(8 * slots, width)
        rank_rows[slab] = dot(places[my_rank], rows).astype(bf16)
    for slab in range(8):
        rank_copies.append(
            pltpu.make_async_copy(
                rank_rows.at[slab], attended.at[:, pl.ds(slab * width, width)], load_sem.at[12 + slab]
            )
        )
        rank_copies[-1].start()

    phase_two = [{} for p in pieces]
    for k in (2, 1, 3, 0):
        for p in pieces:
            sum_right[p][k].wait_recv()
            sum_left[p][k].wait_recv()
            total = part(p, here[p], k)[...].astype(f32)
            for side in range(2):
                total = total + landing(near_parts.at[p, side], p, step(p, k))[...].astype(f32)
            result = landing(sums_two.at[p], p, step(p, k))
            result[...] = total.astype(bf16)
            if k != 0:
                phase_two[p][k] = copies.start(
                    result,
                    parts_two.at[p, k - 1, :, :, pl.ds(0, out_cols[p][1])],
                    device(moved(me, ORDERS[p][1], k), core),
                )
    phase_three = {}
    for p, (first, second, last) in enumerate(ORDERS):
        width_p = out_cols[p][1]
        tail = (slice(None), pl.ds(0, width_p))
        for copy in phase_two[p].values():
            copy.wait_recv()
        total = pick(sums_two.at[p], {second: me[second]}, tail, rest[p])[...].astype(jnp.float32)
        for k in range(3):
            total = total + parts_two[p, k, :, :, pl.ds(0, width_p)].astype(jnp.float32)
        sums_three[p, :, :, pl.ds(0, width_p)] = total.astype(jnp.bfloat16)
        phase_three[p] = []
        for k in (1, 3, 2):
            to = moved(me, first, k)
            phase_three[p].append(
                copies.start(
                    sums_three.at[p, to[first], :, pl.ds(0, width_p)],
                    parts_three.at[p, k - 1, :, pl.ds(0, width_p)],
                    device(to, core),
                )
            )
    for p, (first, second, last) in enumerate(ORDERS):
        width_p = out_cols[p][1]
        for copy in phase_three[p]:
            copy.wait_recv()
        total = sums_three[p, me[first], :, pl.ds(0, width_p)].astype(jnp.float32)
        for k in range(3):
            total = total + parts_three[p, k, :, pl.ds(0, width_p)].astype(jnp.float32)
        final_half[0, :, pl.ds(*out_cols[p])] = total.astype(jnp.bfloat16)
    last_copy = copies.start(final_half.at[0], final_half.at[1], sibling)
    last_copy.wait_recv()
    for side, column_half in enumerate((core, other)):
        both = final_half[side].astype(f32)
        for quarter in range(2):
            eight = both[quarter * 8 : quarter * 8 + 8]
            own = jnp.where(core == 0, eight[0:4], eight[4:8])
            start = pl.multiple_of(column_half * (2 * unit_cols) + quarter * unit_cols, 128)
            mixed[:, pl.ds(start, unit_cols)] = own.astype(bf16)
    for copy in rank_copies:
        copy.wait()
    copies.finish()


def run_decode(
    queries, plan, lengths, routes, gain, cache_latent, cache_rope, w_absorb, w_out, router, w_gate, w_up, w_down
):
    slots = queries.shape[0]
    cap, latent_width = cache_latent.shape[1:]
    rope_width = cache_rope.shape[2]
    heads = w_absorb.shape[0]
    heads_width = w_out.shape[0]
    model = w_out.shape[1]
    width = model // 8
    half = slots // 2
    hidden = w_gate.shape[1]
    experts = router.shape[1]
    rows = 8 * slots
    unit_cols = model // 4
    share = (unit_cols // 128 * 5 + 6) // 14 * 128
    bf16, f32 = jnp.bfloat16, jnp.float32
    vmem = pl.BlockSpec(memory_space=pltpu.VMEM)
    hbm = pl.BlockSpec(memory_space=pl.ANY)
    return pl.pallas_call(
        decode_kernel,
        out_shape=(
            jax.ShapeDtypeStruct((slots, model), bf16),
            jax.ShapeDtypeStruct((4, model), bf16),
        ),
        in_specs=[vmem] * 3 + [hbm] * 10,
        out_specs=(hbm, vmem),
        scratch_shapes=[
            pltpu.VMEM(queries.shape, bf16),
            pltpu.VMEM((4, 1, 2 * width), f32),
            pltpu.VMEM((slots * cap, latent_width), bf16),
            pltpu.VMEM((slots, rope_width, cap), bf16),
            pltpu.VMEM((slots // 16, rope_width, 16 * cap), bf16),
            pltpu.VMEM(w_absorb.shape, bf16),
            pltpu.VMEM((heads, slots, latent_width), bf16),
            pltpu.VMEM((heads, slots, rope_width), bf16),
            pltpu.VMEM((8, 16, latent_width + 128), bf16),
            pltpu.VMEM((8, 16, latent_width + 128), bf16),
            pltpu.VMEM((2, half, experts), bf16),
            pltpu.VMEM((8, 2, half, experts), bf16),
            pltpu.VMEM((heads, slots, latent_width), bf16),
            pltpu.VMEM((slots, heads_width), bf16),
            pltpu.VMEM((8, slots, rows), bf16),
            pltpu.VMEM((8, 2, half, 2 * experts), bf16),
            pltpu.VMEM((8, 2, half, hidden), bf16),
            pltpu.VMEM((8, slots, width), bf16),
            pltpu.VMEM((heads_width, model), bf16),
            pltpu.VMEM((experts, model), bf16),
            pltpu.VMEM((4, 2 * width, hidden), bf16),
            pltpu.VMEM((4, 2 * width, hidden), bf16),
            pltpu.VMEM((hidden, model), bf16),
            pltpu.VMEM((8, 2, half, width), bf16),
            pltpu.VMEM((8, half, width), bf16),
            pltpu.VMEM((7, half, width), bf16),
            pltpu.VMEM((4, 4, 4, 2, half, width), bf16),
            pltpu.VMEM((8, 2, half, hidden), bf16),
            pltpu.VMEM((2, 4, 4, 4, 16, unit_cols), bf16),
            pltpu.VMEM((4, 4, 4, 16, unit_cols), bf16),
            pltpu.VMEM((3, 4, 4, 16, share), bf16),
            pltpu.VMEM((3, 2, 4, 4, 16, share), bf16),
            pltpu.VMEM((3, 4, 4, 16, share), bf16),
            pltpu.VMEM((3, 3, 4, 16, share), bf16),
            pltpu.VMEM((3, 4, 16, share), bf16),
            pltpu.VMEM((3, 3, 16, share), bf16),
            pltpu.VMEM((2, 16, unit_cols), bf16),
            pltpu.SemaphoreType.DMA((56,)),
            pltpu.SemaphoreType.DMA((192,)),
            pltpu.SemaphoreType.DMA((192,)),
        ],
        compiler_params=pltpu.CompilerParams(
            collective_id=0, has_side_effects=True, vmem_limit_bytes=60 * 1024 * 1024
        ),
        name="decode",
    )(
        plan,
        lengths,
        routes.T,
        queries,
        gain.reshape(4, 1, 2 * width),
        cache_latent.reshape(slots * cap, latent_width),
        cache_rope.transpose(0, 2, 1),
        w_absorb,
        w_out,
        router.T,
        w_gate.reshape(4, 2 * width, hidden),
        w_up.reshape(4, 2 * width, hidden),
        w_down,
    )


def copy_kernel(source, small_source, target, small_target, held, small_held, sems):
    parts = held.shape[0]
    width = source.shape[1] // parts
    small_in = pltpu.make_async_copy(small_source, small_held, sems.at[2 * parts])
    small_in.start()
    copies_in, copies_out = [], []
    for k in range(parts):
        columns = pl.ds(k * width, width)
        copies_in.append(pltpu.make_async_copy(source.at[:, columns], held.at[k], sems.at[k]))
        copies_out.append(pltpu.make_async_copy(held.at[k], target.at[:, columns], sems.at[parts + k]))
        copies_in[-1].start()
    small_in.wait()
    small_out = pltpu.make_async_copy(small_held, small_target, sems.at[2 * parts + 1])
    small_out.start()
    for copy_in, copy_out in zip(copies_in, copies_out):
        copy_in.wait()
        copy_out.start()
    for copy in copies_out:
        copy.wait()
    small_out.wait()


def write_out(attended, mixed):
    hbm = pl.BlockSpec(memory_space=pl.ANY)
    parts = 4
    return pl.pallas_call(
        copy_kernel,
        out_shape=(
            jax.ShapeDtypeStruct(attended.shape, attended.dtype),
            jax.ShapeDtypeStruct(mixed.shape, mixed.dtype),
        ),
        in_specs=[hbm, hbm],
        out_specs=(hbm, hbm),
        scratch_shapes=[
            pltpu.VMEM((parts, attended.shape[0], attended.shape[1] // parts), attended.dtype),
            pltpu.VMEM(mixed.shape, mixed.dtype),
            pltpu.SemaphoreType.DMA((2 * parts + 2,)),
        ],
        compiler_params=pltpu.CompilerParams(vmem_limit_bytes=60 * 1024 * 1024),
        name="write_out",
    )(attended, mixed)


def per_device(
    queries,
    cache_latent,
    cache_rope,
    cache_len,
    move_plan,
    w_absorb,
    w_out,
    norm_gain,
    router,
    routes,
    w_gate,
    w_up,
    w_down,
):
    slots = cache_len.shape[0]
    attended, mixed = run_decode(
        queries,
        move_plan.reshape(1, -1),
        cache_len.reshape(1, slots),
        routes,
        norm_gain,
        cache_latent,
        cache_rope,
        w_absorb,
        w_out,
        router,
        w_gate[0],
        w_up[0],
        w_down[0],
    )
    return write_out(attended, mixed)


def solution(mesh):
    in_specs = (
        P("dp", "ep"),
        P("dp", None, None),
        P("dp", None, None),
        P("dp"),
        P(),
        P("ep", None, None),
        P("ep", None),
        P(),
        P(),
        P("dp", None),
        P("ep", None, "dp"),
        P("ep", None, "dp"),
        P("ep", "dp", None),
    )
    out_specs = (P("dp", None), P(("dp", "ep"), None))
    return jax.shard_map(
        per_device, mesh=mesh, in_specs=in_specs, out_specs=out_specs, check_vma=False
    )
```
